32 devices in a mesh: heads: 4 (over z), shard: 8 (over y, x, core).
Axes of the slice: x: 2, y: 2, z: 4, core: 2. Of those that a mesh axis runs over, the one named last changes fastest.
Arguments:
- tokens: bfloat16 [16, 1024, 1024], P('shard', 'heads'), may hold values from -6 to 6
- cotangent: bfloat16 [16, 1024, 1024], P('shard', 'heads'), may hold values from -6 to 6
- lengths: int32 [16], P('shard'), may hold values from 256 to 1024, as said below
- routes: int32 [16, 1024, 8], P('shard', 'heads'), may hold values from 0 to 31, all different within a row
- attention_input_weight: bfloat16 [1024, 2048], P(('heads', 'shard')), may hold values from -0.1875 to 0.1875
- attn_out: bfloat16 [1024, 1024], P(('heads', 'shard')), may hold values from -1.5 to 1.5
- router: bfloat16 [1024, 32], P(('heads', 'shard')), may hold values from -0.09375 to 0.09375
- gain_attn: bfloat16 [1024], P(('heads', 'shard')), may hold values from 0.5 to 1.5
- gain_ffn: bfloat16 [1024], P(('heads', 'shard')), may hold values from 0.5 to 1.5
- expert_in: bfloat16 [32768, 1024], P(('heads', 'shard')), may hold values from -0.1875 to 0.1875
- expert_out: bfloat16 [32768, 512], P(('heads', 'shard')), may hold values from -1 to 1
Outputs:
- mixed: bfloat16 [16, 1024, 1024], P('shard', 'heads')
- grad_tokens: bfloat16 [16, 1024, 1024], P('shard', 'heads')
- grad_attn_in: float32 [1024, 2048], P(('heads', 'shard'))
- grad_attn_out: float32 [1024, 1024], P(('heads', 'shard'))
- grad_router: float32 [1024, 32], P(('heads', 'shard'))
- grad_gain_attn: float32 [1024], P(('heads', 'shard'))
- grad_gain_ffn: float32 [1024], P(('heads', 'shard'))
- grad_expert_in: float32 [32768, 1024], P(('heads', 'shard'))
- grad_expert_out: float32 [32768, 512], P(('heads', 'shard'))
The draws below stay inside these ranges and needn't reach their ends.
Inputs may be any that keep to these rules, and one draw needn't show every extreme that they name: `lengths`: of each 2 consecutive slots, one has length 1024. `routes`: A token's 8 experts differ; every expert is named by some token.
All inputs are finite; a program needn't handle non-finite values.
Results may differ from the reference program's by a relative error of at most 0.017.
Values may be sent and summed in bfloat16 or wider, within the bound.
No kernel may reach another device: no remote copies, remote signals or barrier semaphores. Data moves between devices by JAX's collectives and lax.ppermute only.
A program may use at most 512 MiB of HBM per device.

```python
import math
from functools import partial
import jax
import jax.numpy as jnp
from jax import lax

D = 1024
QUERY_HEADS = 16
KEY_VALUE_HEADS = 8
HEAD_SIZE = 64
E = 32
FFE = 512
TOPK = 8
SPAN = 256
SLOTS_DEV = 2
SLOT_POSITIONS = 1024
SLOTS = 16
QUERIES_PER_KV = 2
QKV = 2048
CAP = 160
N_HEADS = 4
N_SHARD = 8


def draw_lengths(key, part):
    key = jax.random.fold_in(key, 7)
    base_key, pick_key = jax.random.split(key)
    drawn = jax.random.randint(base_key, (SLOTS,), SLOT_POSITIONS // 4, SLOT_POSITIONS + 1)
    chosen = jax.random.randint(pick_key, (SLOTS // SLOTS_DEV,), 0, SLOTS_DEV)
    slot_place = jnp.arange(SLOTS) % SLOTS_DEV
    full_slot = slot_place == jnp.repeat(chosen, SLOTS_DEV)
    return jnp.where(full_slot, SLOT_POSITIONS, drawn).astype(jnp.int32)


def steps_of(stream_key, shape, cuts, smallest, high):
    def one(axis_at, blocks):
        steps = jax.random.uniform(jax.random.fold_in(jax.random.fold_in(stream_key, 6), axis_at), (blocks,), jnp.float32, smallest / len(cuts), high / len(cuts))
        return jnp.repeat(jnp.exp(steps), shape[axis_at] // blocks).reshape((-1,) + (1,) * (len(shape) - axis_at - 1))

    factor_of = one(*cuts[0])
    for cut in cuts[1:]:
        factor_of = factor_of * one(*cut)
    return factor_of


def choose_distinct(stream_key, rows, amount, top, lift):
    sequence = jax.random.permutation(jax.random.fold_in(stream_key, 1), amount)
    pull = sequence
    for power in range(3):
        pull = pull * pull // amount
    pull = pull * lift // amount
    chance = jax.random.randint(jax.random.fold_in(stream_key, 2), (rows, amount), 0, 4096) + pull
    fixed_rows = jax.random.permutation(jax.random.fold_in(stream_key, 3), rows)[jnp.arange(amount) % rows]
    chance = jnp.where(jnp.arange(rows)[:, None] == fixed_rows[None, :], 1 << 14, chance)
    score = chance * amount + jnp.arange(amount)
    return lax.top_k(score.astype(jnp.int32), top)[1].astype(jnp.int32)


def centred(stream_key, extent, scale, most, pieces=(), kind=jnp.bfloat16):
    values = scale * jax.random.normal(stream_key, extent, jnp.float32)
    if pieces:
        values = values * steps_of(stream_key, extent, pieces, -0.22, 0.18)
    return jnp.clip(values, -most, most).astype(kind)


def setup_inputs(seed: int = 0) -> dict:
    seeds = jax.random.split(jax.random.key(seed), 12)
    return {
        "tokens": centred(seeds[0], (SLOTS, SLOT_POSITIONS, D), 1.0, 6.0, ((0, 8), (1, 4))),
        "cotangent": centred(seeds[1], (SLOTS, SLOT_POSITIONS, D), 1.0, 6.0, ((0, 8), (1, 4))),
        "lengths": draw_lengths(jax.random.fold_in(seeds[11], 71), 0),
        "routes": choose_distinct(seeds[3], SLOTS * SLOT_POSITIONS, E, TOPK, 2048).reshape((SLOTS, SLOT_POSITIONS, TOPK)),
        "attention_input_weight": centred(seeds[4], (D, QKV), D ** -0.5, 0.1875, ((0, 32),)),
        "attn_out": centred(seeds[5], (QUERY_HEADS * HEAD_SIZE, D), (QUERY_HEADS * HEAD_SIZE // 64) ** -0.5, 1.5, ((0, 32),)),
        "router": centred(seeds[6], (D, E), (4 * D) ** -0.5, 0.09375, ((0, 32),)),
        "gain_attn": jnp.clip(1.0 + 0.1 * jax.random.normal(seeds[7], (D,), jnp.float32), 0.5, 1.5).astype(jnp.bfloat16),
        "gain_ffn": jnp.clip(1.0 + 0.1 * jax.random.normal(seeds[8], (D,), jnp.float32), 0.5, 1.5).astype(jnp.bfloat16),
        "expert_in": centred(seeds[9], (E * D, 2 * FFE), D ** -0.5, 0.1875, ((0, 32),)),
        "expert_out": centred(seeds[10], (E * D, FFE), (FFE // 16) ** -0.5, 1.0, ((0, 32),)),
    }


EPSILON = 1e-06
THETA_BASE = 10000.0
NEGATIVE = -1e+30
TOP_PRECISION = lax.Precision.HIGHEST

@jax.custom_vjp
def low(v):
    return lax.optimization_barrier(v.astype(jnp.bfloat16)).astype(jnp.float32)

@jax.custom_vjp
def reduced_backward(v):
    return v

def low_keep(v):
    return (low(v), None)

def low_pass(kept, grad):
    return (grad,)

def back_keep(v):
    return (v, None)

def back_low(kept, grad):
    return (low(grad),)
low.defvjp(low_keep, low_pass)
reduced_backward.defvjp(back_keep, back_low)

def norm_rows(value, gain):
    return value * lax.rsqrt(lax.optimization_barrier(jnp.mean(value * value, -1, keepdims=True)) + EPSILON) * gain

def rotary_tables(positions):
    half_size = HEAD_SIZE // 2
    freqs = THETA_BASE ** (-2.0 * jnp.arange(half_size, dtype=jnp.float32) / HEAD_SIZE)
    angles = positions.astype(jnp.float32)[:, None] * freqs[None, :]
    return (jnp.cos(angles), jnp.sin(angles))

def turn(values, cosine, sine, sign):
    half_size = values.shape[-1] // 2
    first_half = values[..., :half_size]
    second_half = values[..., half_size:]
    return jnp.concatenate([first_half * cosine - sign * second_half * sine, second_half * cosine + sign * first_half * sine], -1)

def attend_slot(attention_input_weight, normalized_rows):
    before_projection = reduced_backward(jnp.dot(normalized_rows, attention_input_weight, precision=TOP_PRECISION)).reshape(SLOT_POSITIONS, KEY_VALUE_HEADS, QUERIES_PER_KV + 2, HEAD_SIZE)
    cosine, sine = rotary_tables(jnp.arange(SLOT_POSITIONS))
    turned = turn(before_projection[:, :, :QUERIES_PER_KV + 1], cosine[:, None, None, :], sine[:, None, None, :], 1.0)
    packed_tokens = reduced_backward(low(jnp.concatenate([turned, before_projection[:, :, QUERIES_PER_KV + 1:]], 2)))
    queries = packed_tokens[:, :, :QUERIES_PER_KV]
    keys = packed_tokens[:, :, QUERIES_PER_KV]
    values = packed_tokens[:, :, QUERIES_PER_KV + 1]
    block_rows = math.gcd(512, SLOT_POSITIONS)
    scale = 1.0 / math.sqrt(HEAD_SIZE)

    def one_block(first_row):
        query_block = lax.dynamic_slice_in_dim(queries, first_row, block_rows, 0)
        scores = reduced_backward(jnp.einsum('qhgd,khd->hgqk', query_block, keys, precision=TOP_PRECISION) * scale)
        allowed = jnp.arange(SLOT_POSITIONS)[None, :] <= (first_row + jnp.arange(block_rows))[:, None]
        scores = jnp.where(allowed, scores, NEGATIVE)
        highest_score = lax.optimization_barrier(jnp.max(scores, -1, keepdims=True))
        weights_exp = jnp.exp(scores - highest_score)
        probs = low(weights_exp / lax.optimization_barrier(jnp.sum(weights_exp, -1, keepdims=True)))
        return jnp.einsum('hgqk,khd->qhgd', probs, values, precision=TOP_PRECISION)
    firsts = (jnp.arange(SLOT_POSITIONS // block_rows) * block_rows).astype(jnp.int32)
    outputs = lax.map(jax.checkpoint(one_block), firsts)
    return reduced_backward(low(outputs.reshape(SLOT_POSITIONS, QUERY_HEADS * HEAD_SIZE)))

def expert_block(router, expert_in, expert_out, items):
    normalized_rows, chosen_routes, valid_rows = items
    token_count = normalized_rows.shape[0]
    logits = jnp.dot(normalized_rows, router, precision=TOP_PRECISION)
    chosen = jnp.take_along_axis(logits, chosen_routes, 1)
    highest_logit = lax.optimization_barrier(jnp.max(chosen, -1, keepdims=True))
    weights_exp = jnp.exp(chosen - highest_logit)
    gates = weights_exp / lax.optimization_barrier(jnp.sum(weights_exp, -1, keepdims=True))
    flat_routes = chosen_routes.reshape(token_count * TOPK)
    live_pairs = jnp.repeat(valid_rows, TOPK) > 0
    one_hot = ((flat_routes[:, None] == jnp.arange(E)[None, :]) & live_pairs[:, None]).astype(jnp.int32)
    slot_index = lax.optimization_barrier(jnp.sum((jnp.cumsum(one_hot, 0) - one_hot) * one_hot, 1))
    kept_pairs = live_pairs & (slot_index < CAP)
    target = jnp.where(kept_pairs, slot_index * E + flat_routes, CAP * E).astype(jnp.int32)
    spread = jnp.repeat(normalized_rows, TOPK, 0)
    buffer = jnp.zeros((CAP * E + 1, D), jnp.float32).at[target].add(spread)[:CAP * E].reshape(CAP, E, D)
    pre_ffn = reduced_backward(jnp.einsum('ced,edf->cef', buffer, expert_in.reshape(E, D, 2 * FFE), precision=TOP_PRECISION))
    hidden = low(jax.nn.silu(pre_ffn[..., :FFE]) * pre_ffn[..., FFE:])
    outputs = reduced_backward(jnp.einsum('cef,edf->ced', hidden, expert_out.reshape(E, D, FFE), precision=TOP_PRECISION))
    table = jnp.concatenate([outputs.reshape(CAP * E, D), jnp.zeros((1, D), jnp.float32)], 0)
    picked = table[target].reshape(token_count, TOPK, D)
    return lax.optimization_barrier(jnp.sum(picked * gates[..., None], 1))

def regroup(array):
    rest_shape = array.shape[2:]
    array = array.reshape((N_SHARD, SLOTS_DEV, N_HEADS, SPAN) + rest_shape)
    array = jnp.swapaxes(array, 1, 2)
    return array.reshape((N_SHARD * N_HEADS, SLOTS_DEV * SPAN) + rest_shape)

def ungroup(array):
    rest_shape = array.shape[2:]
    array = array.reshape((N_SHARD, N_HEADS, SLOTS_DEV, SPAN) + rest_shape)
    array = jnp.swapaxes(array, 1, 2)
    return array.reshape((SLOTS, SLOT_POSITIONS) + rest_shape)

def forward(valid, routes, tokens, attention_input_weight, attn_out, router, gain_attn, gain_ffn, expert_in, expert_out):
    normed_attn = low(norm_rows(tokens, gain_attn))
    context = lax.map(jax.checkpoint(partial(attend_slot, attention_input_weight)), normed_attn)
    attention = reduced_backward(jnp.dot(context.reshape(SLOTS * SLOT_POSITIONS, QUERY_HEADS * HEAD_SIZE), attn_out, precision=TOP_PRECISION))
    mid_state = tokens + attention.reshape(tokens.shape)
    normed_ffn = low(norm_rows(mid_state, gain_ffn))
    blocks = lax.map(jax.checkpoint(partial(expert_block, router, expert_in, expert_out)), (regroup(normed_ffn), regroup(routes), regroup(valid)))
    mixture = ungroup(blocks)
    return valid[..., None].astype(jnp.float32) * (mid_state + mixture)

def reference(tokens, cotangent, lengths, routes, attention_input_weight, attn_out, router, gain_attn, gain_ffn, expert_in, expert_out):
    valid = (jnp.arange(SLOT_POSITIONS)[None, :] < lengths[:, None]).astype(jnp.int32)
    mixed, pullback = jax.vjp(partial(forward, valid, routes), tokens.astype(jnp.float32), attention_input_weight.astype(jnp.float32), attn_out.astype(jnp.float32), router.astype(jnp.float32), gain_attn.astype(jnp.float32), gain_ffn.astype(jnp.float32), expert_in.astype(jnp.float32), expert_out.astype(jnp.float32))
    grads = pullback(cotangent.astype(jnp.float32))
    return (mixed.astype(jnp.bfloat16), grads[0].astype(jnp.bfloat16), grads[1].astype(jnp.float32), grads[2].astype(jnp.float32), grads[3].astype(jnp.float32), grads[4].astype(jnp.float32), grads[5].astype(jnp.float32), grads[6].astype(jnp.float32), grads[7].astype(jnp.float32))
```

```python
import math

import jax
import jax.numpy as jnp
from jax import lax
from jax.sharding import PartitionSpec as P

D = 1024
QUERY_HEADS = 16
KEY_VALUE_HEADS = 8
HEAD_SIZE = 64
E = 32
FFE = 512
TOPK = 8
QUERIES_PER_KV = 2
CAP = 160


EPSILON = 1e-06
THETA_BASE = 10000.0
NEGATIVE = -1e30
TOP_PRECISION = lax.Precision.HIGHEST


def norm_rows(value, gain):
    factor = lax.rsqrt(jnp.mean(value * value, -1, keepdims=True) + EPSILON)
    return (value * factor * gain, factor)


def norm_back(grad_in, value, factor, gain):
    normalized_rows = value * factor
    scaled = grad_in * gain
    gain_term = jnp.sum(grad_in * normalized_rows, 0)
    grad_value = factor * (
        scaled - normalized_rows * jnp.mean(scaled * normalized_rows, -1, keepdims=True)
    )
    return (grad_value, gain_term)


def rotary_tables(positions):
    half_size = HEAD_SIZE // 2
    freqs = THETA_BASE ** (-2.0 * jnp.arange(half_size, dtype=jnp.float32) / HEAD_SIZE)
    angles = positions.astype(jnp.float32)[:, None] * freqs[None, :]
    return (jnp.cos(angles), jnp.sin(angles))


def turn(values, cosine, sine, sign):
    half_size = values.shape[-1] // 2
    first_half = values[..., :half_size]
    second_half = values[..., half_size:]
    return jnp.concatenate(
        [
            first_half * cosine - sign * second_half * sine,
            second_half * cosine + sign * first_half * sine,
        ],
        -1,
    )


def split_heads(packed_tokens):
    items, length, local_groups = packed_tokens.shape[:3]
    pieces = packed_tokens.reshape(items, length, local_groups, QUERIES_PER_KV + 2, HEAD_SIZE)
    return (
        pieces[:, :, :, :QUERIES_PER_KV],
        pieces[:, :, :, QUERIES_PER_KV],
        pieces[:, :, :, QUERIES_PER_KV + 1],
    )


def block_scores(query_block, keys, first_row, block_rows, length):
    scale = 1.0 / math.sqrt(HEAD_SIZE)
    scores = (
        jnp.einsum("nqhgd,nkhd->nhgqk", query_block, keys, preferred_element_type=jnp.float32)
        * scale
    )
    allowed = jnp.arange(length)[None, :] <= (first_row + jnp.arange(block_rows))[:, None]
    return jnp.where(allowed, scores, NEGATIVE)


def attend_forward(packed_tokens):
    queries, keys, values = split_heads(packed_tokens)
    items, length, local_groups = packed_tokens.shape[:3]
    block_rows = math.gcd(512, length)

    def one_block(first_row):
        query_block = lax.dynamic_slice_in_dim(queries, first_row, block_rows, 1)
        scores = block_scores(query_block, keys, first_row, block_rows, length)
        highest_score = jnp.max(scores, -1, keepdims=True)
        weights_exp = jnp.exp(scores - highest_score)
        total_exp = jnp.sum(weights_exp, -1, keepdims=True)
        probs = (weights_exp / total_exp).astype(jnp.bfloat16)
        result = jnp.einsum("nhgqk,nkhd->nqhgd", probs, values, preferred_element_type=jnp.float32)
        return (result.astype(jnp.bfloat16), (highest_score + jnp.log(total_exp))[..., 0])

    firsts = jnp.arange(length // block_rows) * block_rows
    results, log_totals = lax.map(one_block, firsts)
    context = jnp.moveaxis(results, 0, 1).reshape(
        items, length, local_groups, QUERIES_PER_KV * HEAD_SIZE
    )
    log_total = jnp.moveaxis(log_totals, 0, 3).reshape(items, local_groups, QUERIES_PER_KV, length)
    return (context, log_total, packed_tokens)


def attend_backward(packed_tokens, log_total, context_gradient):
    queries, keys, values = split_heads(packed_tokens)
    items, length, local_groups = packed_tokens.shape[:3]
    block_rows = math.gcd(512, length)
    scale = 1.0 / math.sqrt(HEAD_SIZE)
    grad_heads = context_gradient.reshape(items, length, local_groups, QUERIES_PER_KV, HEAD_SIZE)

    def one_block(totals, first_row):
        grad_keys, grad_values = totals
        query_block = lax.dynamic_slice_in_dim(queries, first_row, block_rows, 1)
        grad_block = lax.dynamic_slice_in_dim(grad_heads, first_row, block_rows, 1)
        total_block = lax.dynamic_slice_in_dim(log_total, first_row, block_rows, 3)
        scores = block_scores(query_block, keys, first_row, block_rows, length)
        probs = jnp.exp(scores - total_block[..., None])
        probs_low = probs.astype(jnp.bfloat16)
        grad_values = grad_values + jnp.einsum(
            "nhgqk,nqhgd->nkhd", probs_low, grad_block, preferred_element_type=jnp.float32
        )
        grad_probs = jnp.einsum(
            "nqhgd,nkhd->nhgqk", grad_block, values, preferred_element_type=jnp.float32
        )
        grad_scores = (
            probs * (grad_probs - jnp.sum(probs * grad_probs, -1, keepdims=True))
        ).astype(jnp.bfloat16)
        grad_query = (
            jnp.einsum("nhgqk,nkhd->nqhgd", grad_scores, keys, preferred_element_type=jnp.float32)
            * scale
        )
        grad_keys = (
            grad_keys
            + jnp.einsum(
                "nhgqk,nqhgd->nkhd", grad_scores, query_block, preferred_element_type=jnp.float32
            )
            * scale
        )
        return ((grad_keys, grad_values), grad_query.astype(jnp.bfloat16))

    firsts = jnp.arange(length // block_rows) * block_rows
    zeros_kv = jnp.zeros((items, length, local_groups, HEAD_SIZE), jnp.float32)
    (grad_keys, grad_values), grad_queries = lax.scan(one_block, (zeros_kv, zeros_kv), firsts)
    grad_queries = jnp.moveaxis(grad_queries, 0, 1).reshape(
        items, length, local_groups, QUERIES_PER_KV, HEAD_SIZE
    )
    joined = jnp.concatenate(
        [
            grad_queries,
            grad_keys.astype(jnp.bfloat16)[:, :, :, None],
            grad_values.astype(jnp.bfloat16)[:, :, :, None],
        ],
        3,
    )
    return joined.reshape(items, length, local_groups, (QUERIES_PER_KV + 2) * HEAD_SIZE)


def swiglu(pre_ffn):
    gate_pre = pre_ffn[..., :FFE]
    up_pre = pre_ffn[..., FFE:]
    sigmoid_gate = jax.nn.sigmoid(gate_pre)
    silu_gate = gate_pre * sigmoid_gate
    return ((silu_gate * up_pre).astype(jnp.bfloat16), (gate_pre, up_pre, sigmoid_gate, silu_gate))


def swiglu_back(grad_hidden, pieces_kept):
    gate_pre, up_pre, sigmoid_gate, silu_gate = pieces_kept
    grad_gate = grad_hidden * up_pre * sigmoid_gate * (1.0 + gate_pre * (1.0 - sigmoid_gate))
    grad_up = grad_hidden * silu_gate
    return jnp.concatenate([grad_gate, grad_up], -1).astype(jnp.bfloat16)


def norm_factor(value):
    return lax.rsqrt(jnp.mean(value * value, -1, keepdims=True) + EPSILON)


def make_local(n_heads, chip, core):
    everyone = ("heads", "chip", "core")
    group = ("heads", "core")
    group_size = n_heads * core
    n_local = E // group_size
    groups_local = KEY_VALUE_HEADS // n_heads
    group_width = (QUERIES_PER_KV + 2) * HEAD_SIZE

    def own_experts(dense):
        split = dense.reshape(dense.shape[:-1] + (n_heads, n_local, core))
        axis = dense.ndim - 1
        mine = lax.dynamic_index_in_dim(split, lax.axis_index("heads"), axis, False)
        return lax.dynamic_index_in_dim(mine, lax.axis_index("core"), axis + 1, False)

    def local(
        tokens,
        cotangent,
        lengths,
        routes,
        attention_input_weight,
        attn_out,
        router,
        gain_attn,
        gain_ffn,
        expert_in,
        expert_out,
    ):
        slots, span, width = tokens.shape
        token_rows = slots * span
        length = span * n_heads
        rank = lax.axis_index("heads")
        qkv_width = attention_input_weight.shape[1]
        small = jnp.concatenate(
            [
                attention_input_weight,
                attn_out,
                router,
                gain_attn[:, None],
                gain_ffn[:, None],
                jnp.zeros((router.shape[0], 128 - E - 2), jnp.bfloat16),
            ],
            1,
        )
        small = lax.all_gather(small, everyone, axis=0, tiled=True)
        w_qkv = small[:, :qkv_width]
        w_proj = small[:, qkv_width : qkv_width + D]
        w_router = small[:, qkv_width + D : qkv_width + D + E]
        gain_one = small[:, qkv_width + D + E].astype(jnp.float32)
        gain_two = small[:, qkv_width + D + E + 1].astype(jnp.float32)
        whole_tokens = lax.all_gather(tokens, "heads", axis=1, tiled=True)

        positions = rank * span + jnp.arange(span, dtype=jnp.int32)
        valid = (positions[None, :] < lengths[:, None]).reshape(token_rows)
        valid_float = valid.astype(jnp.float32)[:, None]
        route_rows = routes.reshape(token_rows, TOPK)
        routed = jnp.any(
            route_rows[:, :, None] == jnp.arange(E, dtype=jnp.int32)[None, None, :], 1
        )
        live = (routed & valid[:, None]).astype(jnp.bfloat16)
        earlier = (
            jnp.arange(token_rows)[:, None] > jnp.arange(token_rows)[None, :]
        ).astype(jnp.bfloat16)
        count = jnp.dot(earlier, live, preferred_element_type=jnp.float32)
        kept = (live > 0) & (count < CAP)
        code = jnp.where(kept, count, jnp.where(routed, 200.0, -1.0)).astype(jnp.bfloat16)
        early = jnp.concatenate(
            [
                cotangent.reshape(token_rows, width),
                code,
                jnp.zeros((token_rows, 128 - E), jnp.bfloat16),
            ],
            1,
        )
        early = lax.all_gather(early, group, axis=0)
        grad_group = early[:, :, :width]
        code_group = early[:, :, width : width + E].astype(jnp.float32)
        own_in = lax.all_gather(expert_in, "chip", axis=0, tiled=True).reshape(
            n_local, D, 2 * FFE
        )
        own_out = lax.all_gather(expert_out, "chip", axis=0, tiled=True).reshape(n_local, D, FFE)

        whole_state = whole_tokens.astype(jnp.float32)
        normed_whole = (whole_state * norm_factor(whole_state) * gain_one).astype(jnp.bfloat16)
        w_mine = lax.dynamic_slice_in_dim(
            w_qkv, rank * (groups_local * group_width), groups_local * group_width, 1
        )
        before = jnp.dot(
            normed_whole.reshape(slots * length, width), w_mine, preferred_element_type=jnp.float32
        ).reshape(slots, length, groups_local, QUERIES_PER_KV + 2, HEAD_SIZE)
        cosine, sine = rotary_tables(jnp.arange(length, dtype=jnp.int32))
        cosine = cosine[None, :, None, None, :]
        sine = sine[None, :, None, None, :]
        turned = turn(before[:, :, :, : QUERIES_PER_KV + 1], cosine, sine, 1.0)
        packed = jnp.concatenate([turned, before[:, :, :, QUERIES_PER_KV + 1 :]], 3).astype(
            jnp.bfloat16
        )
        packed = packed.reshape(slots, length, groups_local, group_width)
        context_heads, log_total, received = attend_forward(packed)
        context = lax.all_to_all(
            context_heads, "heads", split_axis=1, concat_axis=2, tiled=True
        ).reshape(token_rows, QUERY_HEADS * HEAD_SIZE)

        state = tokens.astype(jnp.float32).reshape(token_rows, width)
        mid_state = state + jnp.dot(context, w_proj, preferred_element_type=jnp.float32)
        normed_two, factor_two = norm_rows(mid_state, gain_two)
        normed_ffn = normed_two.astype(jnp.bfloat16)
        normed_group = lax.all_gather(normed_ffn, group, axis=0)

        def gates_of(rows, codes):
            logits = jnp.dot(rows, w_router, preferred_element_type=jnp.float32)
            inside = codes >= 0
            highest = jnp.max(jnp.where(inside, logits, NEGATIVE), -1, keepdims=True)
            weights = jnp.where(inside, jnp.exp(jnp.where(inside, logits - highest, 0.0)), 0.0)
            return weights / jnp.sum(weights, -1, keepdims=True)

        gates = gates_of(normed_ffn, code.astype(jnp.float32))
        gates_own = own_experts(gates_of(normed_group, code_group))
        code_own = own_experts(code_group)

        place = jnp.arange(CAP, dtype=jnp.float32)[None, :, None]
        picks, out_rows, back_rows, gate_grads, grads_in, grads_out = [], [], [], [], [], []
        flat = group_size * CAP
        for i in range(n_local):
            hit = code_own[:, None, :, i] == place
            pick = hit.astype(jnp.bfloat16)
            gate_row = jnp.sum(
                jnp.where(hit, gates_own[:, None, :, i], 0.0), -1
            ).reshape(flat, 1)
            buffer = jnp.einsum(
                "sct,std->scd", pick, normed_group, preferred_element_type=jnp.bfloat16
            ).reshape(flat, width)
            grad_row = jnp.einsum(
                "sct,std->scd", pick, grad_group, preferred_element_type=jnp.bfloat16
            ).reshape(flat, width)
            pre = jnp.dot(buffer, own_in[i], preferred_element_type=jnp.float32)
            hidden, pieces_kept = swiglu(pre)
            outputs = jnp.dot(hidden, own_out[i].T, preferred_element_type=jnp.float32)
            grad_plain = jnp.dot(grad_row, own_out[i], preferred_element_type=jnp.float32)
            gate_grad = jnp.sum(grad_plain * hidden.astype(jnp.float32), -1)
            grad_pre = swiglu_back(gate_row * grad_plain, pieces_kept)
            back = jnp.dot(grad_pre, own_in[i].T, preferred_element_type=jnp.float32)
            grad_outputs = (gate_row * grad_row.astype(jnp.float32)).astype(jnp.bfloat16)
            grads_in.append(
                lax.dot_general(
                    buffer,
                    grad_pre,
                    (((0,), (0,)), ((), ())),
                    preferred_element_type=jnp.float32,
                )
            )
            grads_out.append(
                lax.dot_general(
                    grad_outputs,
                    hidden,
                    (((0,), (0,)), ((), ())),
                    preferred_element_type=jnp.float32,
                )
            )
            picks.append(pick)
            out_rows.append(
                (gate_row * outputs).astype(jnp.bfloat16).reshape(group_size, CAP, width)
            )
            back_rows.append(back.astype(jnp.bfloat16).reshape(group_size, CAP, width))
            gate_grads.append(
                jnp.sum(
                    jnp.where(hit, gate_grad.reshape(group_size, CAP, 1), 0.0), 1
                )
            )
        pick_all = jnp.concatenate(picks, 1)
        back_sum = jnp.einsum(
            "sct,scd->std",
            pick_all,
            jnp.concatenate(back_rows, 1),
            preferred_element_type=jnp.float32,
        ).astype(jnp.bfloat16)
        back_sum = lax.psum_scatter(
            back_sum.reshape(group_size * token_rows, width),
            group,
            scatter_dimension=0,
            tiled=True,
        )
        gate_back = lax.all_to_all(
            jnp.stack(gate_grads, 1), group, split_axis=0, concat_axis=0, tiled=True
        )
        mix_sum = jnp.einsum(
            "sct,scd->std",
            pick_all,
            jnp.concatenate(out_rows, 1),
            preferred_element_type=jnp.float32,
        ).astype(jnp.bfloat16)
        mixture = lax.psum_scatter(
            mix_sum.reshape(group_size * token_rows, width),
            group,
            scatter_dimension=0,
            tiled=True,
        )
        grad_expert_in = lax.psum_scatter(
            jnp.concatenate(grads_in, 0), "chip", scatter_dimension=0, tiled=True
        )
        grad_expert_out = lax.psum_scatter(
            jnp.concatenate(grads_out, 0), "chip", scatter_dimension=0, tiled=True
        )
        mixed = (valid_float * (mid_state + mixture.astype(jnp.float32))).astype(jnp.bfloat16)

        grad_gates = jnp.transpose(
            gate_back.reshape(n_heads, core, n_local, token_rows), (3, 0, 2, 1)
        ).reshape(token_rows, E)
        grad_logits = gates * (grad_gates - jnp.sum(gates * grad_gates, -1, keepdims=True))
        grad_logits = grad_logits * valid_float
        grad_out = cotangent.astype(jnp.float32).reshape(token_rows, width) * valid_float
        grad_normed_ffn = back_sum.astype(jnp.float32) + jnp.dot(
            grad_logits, w_router.astype(jnp.float32).T, precision=TOP_PRECISION
        )
        router_term = jnp.dot(
            normed_ffn.astype(jnp.float32).T, grad_logits, precision=TOP_PRECISION
        )
        grad_mid_norm, gain_two_term = norm_back(grad_normed_ffn, mid_state, factor_two, gain_two)
        grad_mid = grad_out + grad_mid_norm
        grad_mid_low = grad_mid.astype(jnp.bfloat16)
        proj_term = lax.dot_general(
            context, grad_mid_low, (((0,), (0,)), ((), ())), preferred_element_type=jnp.float32
        )
        second = lax.psum_scatter(
            jnp.concatenate(
                [
                    proj_term,
                    router_term,
                    gain_two_term[:, None],
                    jnp.zeros((D, 128 - E - 1), jnp.float32),
                ],
                1,
            ),
            everyone,
            scatter_dimension=0,
            tiled=True,
        )
        grad_attn_out = second[:, :D]
        grad_router = second[:, D : D + E]
        grad_gain_ffn = second[:, D + E]
        context_gradient = jnp.dot(
            grad_mid_low, w_proj.T, preferred_element_type=jnp.float32
        ).astype(jnp.bfloat16)
        context_gradient = context_gradient.reshape(
            slots, span, KEY_VALUE_HEADS, QUERIES_PER_KV * HEAD_SIZE
        )
        grad_context_heads = lax.all_to_all(
            context_gradient, "heads", split_axis=2, concat_axis=1, tiled=True
        )
        grad_packed = attend_backward(received, log_total, grad_context_heads)
        grad_pieces = grad_packed.astype(jnp.float32).reshape(
            slots, length, groups_local, QUERIES_PER_KV + 2, HEAD_SIZE
        )
        grad_turned = turn(grad_pieces[:, :, :, : QUERIES_PER_KV + 1], cosine, sine, -1.0)
        grad_before = jnp.concatenate(
            [grad_turned, grad_pieces[:, :, :, QUERIES_PER_KV + 1 :]], 3
        ).astype(jnp.bfloat16)
        grad_before = grad_before.reshape(slots, length, groups_local * group_width)
        qkv_term = lax.dot_general(
            normed_whole.reshape(slots * length, width),
            grad_before.reshape(slots * length, groups_local * group_width),
            (((0,), (0,)), ((), ())),
            preferred_element_type=jnp.float32,
        )
        rows_each = D // (n_heads * chip * core)
        qkv_term = jnp.swapaxes(
            qkv_term.reshape(n_heads, chip * core, rows_each, groups_local * group_width), 0, 1
        ).reshape(D, groups_local * group_width)
        qkv_part = lax.psum_scatter(qkv_term, ("chip", "core"), scatter_dimension=0, tiled=True)
        grad_attn_in = lax.all_to_all(
            qkv_part, "heads", split_axis=0, concat_axis=1, tiled=True
        )
        grad_gain_attn = jnp.sum(
            grad_attn_in * attention_input_weight.astype(jnp.float32), -1
        ) / gain_attn.astype(jnp.float32)
        grad_mine = lax.all_to_all(
            grad_before, "heads", split_axis=1, concat_axis=2, tiled=True
        ).reshape(token_rows, qkv_width)
        grad_normed_attn = jnp.dot(grad_mine, w_qkv.T, preferred_element_type=jnp.float32)
        grad_state_norm, _ = norm_back(grad_normed_attn, state, norm_factor(state), gain_one)
        grad_tokens = (grad_mid + grad_state_norm).astype(jnp.bfloat16).reshape(tokens.shape)
        return (
            mixed.reshape(tokens.shape),
            grad_tokens,
            grad_attn_in,
            grad_attn_out,
            grad_router,
            grad_gain_attn,
            grad_gain_ffn,
            grad_expert_in,
            grad_expert_out,
        )

    return local


def solution(mesh):
    n_heads, n_shard = mesh.shape["heads"], mesh.shape["shard"]
    core = 2 if n_heads * n_shard == E else 1
    chip = n_shard // core
    split = jax.sharding.Mesh(
        mesh.devices.reshape(n_heads, chip, core), ("heads", "chip", "core")
    )
    shard = ("chip", "core")
    everyone = ("heads", "chip", "core")
    token_spec = P(shard, "heads", None)
    rows = P(everyone, None)
    in_specs = (
        token_spec,
        token_spec,
        P(shard),
        token_spec,
        rows,
        rows,
        rows,
        P(everyone),
        P(everyone),
        rows,
        rows,
    )
    out_specs = (token_spec, token_spec, rows, rows, rows, P(everyone), P(everyone), rows, rows)
    return jax.shard_map(
        make_local(n_heads, chip, core),
        mesh=split,
        in_specs=in_specs,
        out_specs=out_specs,
        check_vma=False,
    )
```

```python
import functools
import math

import jax
import jax.numpy as jnp
import numpy as np
from jax import lax
from jax.experimental import pallas as pl
from jax.experimental.pallas import tpu as pltpu
from jax.sharding import PartitionSpec as P

D = 1024
QUERY_HEADS = 16
KEY_VALUE_HEADS = 8
HEAD_SIZE = 64
E = 32
FFE = 512
TOPK = 8
QUERIES_PER_KV = 2
CAP = 160
GROUP = (QUERIES_PER_KV + 2) * HEAD_SIZE
PAIR = QUERIES_PER_KV * HEAD_SIZE
TAIL = 128
BLOCK = 256
VMEM_BYTES = 56 * 2**20


EPSILON = 1e-06
THETA_BASE = 10000.0
NEGATIVE = -1e30
TOP_PRECISION = lax.Precision.HIGHEST
SCALE = 1.0 / math.sqrt(HEAD_SIZE)
SHORT = pl.CostEstimate(flops=1024, bytes_accessed=1024, transcendentals=0)


def dot_nn(left, right):
    return jnp.dot(left, right, preferred_element_type=jnp.float32)


def dot_nt(left, right):
    return lax.dot_general(
        left, right, (((1,), (1,)), ((), ())), preferred_element_type=jnp.float32
    )


def dot_tn(left, right):
    return lax.dot_general(
        left, right, (((0,), (0,)), ((), ())), preferred_element_type=jnp.float32
    )


def norm_factor(value):
    return lax.rsqrt(jnp.mean(value * value, -1, keepdims=True) + EPSILON)


def norm_back(grad_in, value, factor, gain):
    normalized_rows = value * factor
    scaled = grad_in * gain
    gain_term = jnp.sum(grad_in * normalized_rows, 0)
    grad_value = factor * (
        scaled - normalized_rows * jnp.mean(scaled * normalized_rows, -1, keepdims=True)
    )
    return (grad_value, gain_term)


def rotary_tables(length):
    half_size = HEAD_SIZE // 2
    freqs = THETA_BASE ** (-2.0 * np.arange(half_size) / HEAD_SIZE)
    angles = np.arange(length)[:, None] * freqs[None, :]
    cosine, sine = np.cos(angles), np.sin(angles)
    one = np.ones((length, HEAD_SIZE))
    own = np.concatenate([cosine, cosine] * (QUERIES_PER_KV + 1) + [one], 1)
    other = np.concatenate([-sine, sine] * (QUERIES_PER_KV + 1) + [0.0 * one], 1)
    return (jnp.asarray(own, jnp.float32), jnp.asarray(other, jnp.float32))


def partner(values):
    width = values.shape[1]
    lane = lax.broadcasted_iota(jnp.int32, values.shape, 1)
    half_size = HEAD_SIZE // 2
    return jnp.where(
        lax.rem(lane, HEAD_SIZE) < half_size,
        pltpu.roll(values, width - half_size, 1),
        pltpu.roll(values, half_size, 1),
    )


def stack_queries(block):
    values = block.astype(jnp.float32) * SCALE
    low = lax.broadcasted_iota(jnp.int32, values.shape, 1) < HEAD_SIZE
    first = jnp.where(low, values, 0.0)
    second = jnp.where(low, pltpu.roll(values, HEAD_SIZE, 1), 0.0)
    return jnp.concatenate([first, second], 0).astype(jnp.bfloat16)


def stack_grads(block):
    values = block.astype(jnp.float32)
    low = lax.broadcasted_iota(jnp.int32, values.shape, 1) < HEAD_SIZE
    first = jnp.where(low, 0.0, pltpu.roll(values, HEAD_SIZE, 1))
    second = jnp.where(low, 0.0, values)
    return jnp.concatenate([first, second], 0).astype(jnp.bfloat16)


def attention_forward_kernel(pieces, place_ref, *refs):
    xs, refs = refs[:pieces], refs[pieces:]
    gain_ref, w_ref, own_ref, other_ref = refs[:4]
    packed_ref, context_ref, lse_ref, normed_ref = refs[4:]
    span = xs[0].shape[1]
    length = pieces * span

    @pl.when(pl.program_id(1) == 0)
    def _():
        for step in range(pieces):
            at = place_ref[step]
            for start in range(0, span, BLOCK):
                value = xs[step][0, start : start + BLOCK, :].astype(jnp.float32)
                normed_ref[at, 0, start : start + BLOCK, :] = (
                    value * norm_factor(value) * gain_ref[...]
                ).astype(jnp.bfloat16)

    for start in range(0, length, BLOCK):
        rows = slice(start, start + BLOCK)
        before = dot_nn(
            normed_ref[start // span, 0, start % span : start % span + BLOCK, :], w_ref[...]
        )
        packed_ref[0, rows, :] = (
            before * own_ref[rows, :] + partner(before) * other_ref[rows, :]
        ).astype(jnp.bfloat16)

    low = lax.broadcasted_iota(jnp.int32, (BLOCK, PAIR), 1) < HEAD_SIZE
    lane_zero = lax.broadcasted_iota(jnp.int32, (BLOCK, PAIR), 1) == 0
    query_row = lax.rem(lax.broadcasted_iota(jnp.int32, (2 * BLOCK, BLOCK), 0), BLOCK)
    allowed = lax.broadcasted_iota(jnp.int32, (2 * BLOCK, BLOCK), 1) <= query_row
    for start in range(0, length, BLOCK):
        rows = slice(start, start + BLOCK)
        queries = stack_queries(packed_ref[0, rows, :PAIR])
        inside = packed_ref[0, rows, PAIR:]
        scores_inside = jnp.where(allowed, dot_nt(queries, inside), NEGATIVE)
        highest = jnp.max(scores_inside, 1, keepdims=True)
        if start:
            before_keys = packed_ref[0, :start, PAIR:]
            scores_before = dot_nt(queries, before_keys)
            highest = jnp.maximum(highest, jnp.max(scores_before, 1, keepdims=True))
        weights = jnp.exp(scores_inside - highest)
        total = jnp.sum(weights, 1, keepdims=True)
        result = dot_nn(weights.astype(jnp.bfloat16), inside)
        if start:
            weights = jnp.exp(scores_before - highest)
            total = total + jnp.sum(weights, 1, keepdims=True)
            result = result + dot_nn(weights.astype(jnp.bfloat16), before_keys)
        result = result / total
        context_ref[start // span, 0, start % span : start % span + BLOCK, :] = jnp.where(
            low, pltpu.roll(result[:BLOCK], HEAD_SIZE, 1), result[BLOCK:]
        ).astype(jnp.bfloat16)
        log_total = highest + jnp.log(total)
        columns = jnp.where(lane_zero, log_total[:BLOCK], log_total[BLOCK:])
        lse_ref[0, 0, :, rows] = columns.T[:8, :]


def attention_forward(xs, places, gain, weights, tables, groups_local):
    pieces = len(xs)
    slots, span, width = xs[0].shape
    length = pieces * span
    bf16, f32 = jnp.bfloat16, jnp.float32
    return pl.pallas_call(
        functools.partial(attention_forward_kernel, pieces),
        grid_spec=pltpu.PrefetchScalarGridSpec(
            num_scalar_prefetch=1,
            grid=(slots, groups_local),
            in_specs=[pl.BlockSpec((1, span, width), lambda s, g, place: (s, 0, 0))] * pieces
            + [
                pl.BlockSpec((1, width), lambda s, g, place: (0, 0)),
                pl.BlockSpec((width, GROUP), lambda s, g, place: (0, g)),
                pl.BlockSpec((length, GROUP), lambda s, g, place: (0, 0)),
                pl.BlockSpec((length, GROUP), lambda s, g, place: (0, 0)),
            ],
            out_specs=[
                pl.BlockSpec((1, length, GROUP), lambda s, g, place: (s, 0, g)),
                pl.BlockSpec((pieces, 1, span, PAIR), lambda s, g, place: (0, s, 0, g)),
                pl.BlockSpec((1, 1, 8, length), lambda s, g, place: (s, g, 0, 0)),
                pl.BlockSpec((pieces, 1, span, width), lambda s, g, place: (0, s, 0, 0)),
            ],
        ),
        out_shape=[
            jax.ShapeDtypeStruct((slots, length, groups_local * GROUP), bf16),
            jax.ShapeDtypeStruct((pieces, slots, span, groups_local * PAIR), bf16),
            jax.ShapeDtypeStruct((slots, groups_local, 8, length), f32),
            jax.ShapeDtypeStruct((pieces, slots, span, width), bf16),
        ],
        compiler_params=pltpu.CompilerParams(vmem_limit_bytes=VMEM_BYTES),
        cost_estimate=SHORT,
        name="attention_forward",
    )(places, *xs, gain, weights, *tables)


def attention_backward_kernel(
    packed_ref, lse_ref, grad_ref, own_ref, other_ref, out_ref, total_ref
):
    length, span = packed_ref.shape[1], grad_ref.shape[2]
    low = lax.broadcasted_iota(jnp.int32, (BLOCK, PAIR), 1) < HEAD_SIZE
    query_lane = lax.rem(lax.broadcasted_iota(jnp.int32, (BLOCK, 2 * BLOCK), 1), BLOCK)
    allowed = lax.broadcasted_iota(jnp.int32, (BLOCK, 2 * BLOCK), 0) <= query_lane
    total_ref[...] = jnp.zeros_like(total_ref)

    def unturn(values, lanes, rows):
        values = values.astype(jnp.bfloat16).astype(jnp.float32)
        return (
            values * own_ref[rows, lanes] - partner(values) * other_ref[rows, lanes]
        ).astype(jnp.bfloat16)

    for start in range(0, length, BLOCK):
        rows = slice(start, start + BLOCK)
        queries = stack_queries(packed_ref[0, rows, :PAIR])
        inner = slice(start % span, start % span + BLOCK)
        grads = stack_grads(grad_ref[start // span, 0, inner, :])
        log_total = jnp.concatenate([lse_ref[0, 0, 0:1, rows], lse_ref[0, 0, 1:2, rows]], 1)

        def piece(keys):
            scores = dot_nt(keys, queries)
            probs = jnp.exp(scores - log_total)
            return (probs, dot_nt(keys, grads))

        inside = packed_ref[0, rows, PAIR:]
        probs_inside, grad_inside = piece(inside)
        probs_inside = jnp.where(allowed, probs_inside, 0.0)
        delta = jnp.sum(probs_inside * grad_inside, 0, keepdims=True)
        if start:
            before = packed_ref[0, :start, PAIR:]
            probs_before, grad_before = piece(before)
            delta = delta + jnp.sum(probs_before * grad_before, 0, keepdims=True)
        score_grads = (probs_inside * (grad_inside - delta)).astype(jnp.bfloat16)
        total_ref[rows, :] += dot_nn(probs_inside.astype(jnp.bfloat16), grads) + dot_nn(
            score_grads, queries
        )
        grad_query = dot_tn(score_grads, inside)
        if start:
            score_grads = (probs_before * (grad_before - delta)).astype(jnp.bfloat16)
            total_ref[:start, :] += dot_nn(probs_before.astype(jnp.bfloat16), grads) + dot_nn(
                score_grads, queries
            )
            grad_query = grad_query + dot_tn(score_grads, before)
        grad_query = (
            jnp.where(low, grad_query[:BLOCK], pltpu.roll(grad_query[BLOCK:], HEAD_SIZE, 1)) * SCALE
        )
        out_ref[start // span, 0, inner, :PAIR] = unturn(grad_query, slice(0, PAIR), rows)
    for start in range(0, length, BLOCK):
        rows = slice(start, start + BLOCK)
        inner = slice(start % span, start % span + BLOCK)
        out_ref[start // span, 0, inner, PAIR:] = unturn(
            total_ref[rows, :], slice(PAIR, GROUP), rows
        )


def attention_backward(packed, lse, grads, tables, groups_local):
    slots, length = packed.shape[:2]
    pieces, span = grads.shape[0], grads.shape[2]
    return pl.pallas_call(
        attention_backward_kernel,
        grid=(slots, groups_local),
        in_specs=[
            pl.BlockSpec((1, length, GROUP), lambda s, g: (s, 0, g)),
            pl.BlockSpec((1, 1, 8, length), lambda s, g: (s, g, 0, 0)),
            pl.BlockSpec((pieces, 1, span, PAIR), lambda s, g: (0, s, 0, g)),
            pl.BlockSpec((length, GROUP), lambda s, g: (0, 0)),
            pl.BlockSpec((length, GROUP), lambda s, g: (0, 0)),
        ],
        out_specs=pl.BlockSpec((pieces, 1, span, GROUP), lambda s, g: (0, s, 0, g)),
        out_shape=jax.ShapeDtypeStruct((pieces, slots, span, packed.shape[2]), jnp.bfloat16),
        scratch_shapes=[pltpu.VMEM((length, PAIR), jnp.float32)],
        compiler_params=pltpu.CompilerParams(vmem_limit_bytes=VMEM_BYTES),
        cost_estimate=SHORT,
        name="attention_backward",
    )(packed, lse, grads, *tables)


def expert_kernel(sources, n_local, kept, ids_ref, *refs):
    xs, refs = refs[:sources], refs[sources:]
    gs, refs = refs[:sources], refs[sources:]
    w_in_ref, w_out_ref = refs[:2]
    refs = refs[2 + kept :]
    buffer_ref, grad_out_ref, hidden_ref, grad_pre_ref = refs[:4]
    backs, mixes = refs[4 : 4 + sources], refs[4 + sources : 4 + 2 * sources]
    table, picks, mix_rows, back_rows, gate_back = refs[4 + 2 * sources :]
    step = pl.program_id(0)
    expert = ids_ref[step]
    tokens = xs[0].shape[0]
    here = pl.ds(pl.multiple_of(step * CAP, 16), CAP)

    @pl.when(step == 0)
    def _():
        for s in range(sources):
            table[s] = xs[s][:, D:].astype(jnp.float32).T
            gate_back[s] = jnp.zeros((TAIL, tokens), jnp.float32)

    place = lax.broadcasted_iota(jnp.int32, (CAP, tokens), 0).astype(jnp.float32)
    hits, gate_rows, grad_rows = [], [], []
    for s in range(sources):
        code = table[s, pl.ds(expert, 1), :]
        gate = table[s, pl.ds(expert + E, 1), :] + table[s, pl.ds(expert + 2 * E, 1), :]
        hit = code == place
        pick = jnp.where(hit, 1.0, 0.0).astype(jnp.bfloat16)
        picks[s, here, :] = pick
        hits.append(hit)
        gate_rows.append(jnp.sum(jnp.where(hit, gate, 0.0), 1, keepdims=True))
        buffer_ref[0, 0, s * CAP : (s + 1) * CAP, :] = dot_nn(pick, xs[s][:, :D]).astype(
            jnp.bfloat16
        )
        grad_rows.append(dot_nn(pick, gs[s][...]))
    gate_row = jnp.concatenate(gate_rows, 0)
    grad_row = jnp.concatenate(grad_rows, 0)
    grad_out_ref[0, 0] = (gate_row * grad_row).astype(jnp.bfloat16)
    pre = dot_nn(buffer_ref[0, 0], w_in_ref[0])
    grad_plain = dot_nn(grad_row.astype(jnp.bfloat16), w_out_ref[0])
    gate_pre, up_pre = pre[:, :FFE], pre[:, FFE:]
    sigmoid_gate = 1.0 / (1.0 + jnp.exp(-gate_pre))
    silu_gate = gate_pre * sigmoid_gate
    hidden = (silu_gate * up_pre).astype(jnp.bfloat16)
    hidden_ref[0, 0] = hidden
    gate_grad = jnp.sum(grad_plain * hidden.astype(jnp.float32), 1, keepdims=True)
    grad_hidden = gate_row * grad_plain
    grad_pre_ref[0, 0, :, :FFE] = (
        grad_hidden * up_pre * sigmoid_gate * (1.0 + gate_pre * (1.0 - sigmoid_gate))
    ).astype(jnp.bfloat16)
    grad_pre_ref[0, 0, :, FFE:] = (grad_hidden * silu_gate).astype(jnp.bfloat16)
    outputs = (gate_row * dot_nt(hidden, w_out_ref[0])).astype(jnp.bfloat16)
    back = dot_nt(grad_pre_ref[0, 0], w_in_ref[0]).astype(jnp.bfloat16)
    for s in range(sources):
        part = slice(s * CAP, (s + 1) * CAP)
        mix_rows[s, here, :] = outputs[part]
        back_rows[s, here, :] = back[part]
        row = jnp.sum(jnp.where(hits[s], gate_grad[part], 0.0), 0, keepdims=True)
        high = row.astype(jnp.bfloat16).astype(jnp.float32)
        gate_back[s, pl.ds(expert, 1), :] = high
        gate_back[s, pl.ds(expert + E, 1), :] = row - high

    @pl.when(step == n_local - 1)
    def _():
        for s in range(sources):
            backs[s][:, :D] = dot_tn(picks[s], back_rows[s]).astype(jnp.bfloat16)
            backs[s][:, D:] = gate_back[s].T.astype(jnp.bfloat16)
            mixes[s][...] = dot_tn(picks[s], mix_rows[s]).astype(jnp.bfloat16)


def experts(chunk, chunks, ids, xs, gs, own_in, own_out, kept):
    sources, n_local, tokens = len(xs), own_in.shape[0], xs[0].shape[0]
    rows = sources * CAP
    bf16, f32 = jnp.bfloat16, jnp.float32
    fixed = lambda i, ids: (0, 0)
    saved = lambda columns: pl.BlockSpec((1, 1, rows, columns), lambda i, ids: (i, chunk, 0, 0))
    widths = (D, D, FFE, 2 * FFE)
    in_specs = (
        [pl.BlockSpec((tokens, D + TAIL), fixed)] * sources
        + [pl.BlockSpec((tokens, D), fixed)] * sources
        + [
            pl.BlockSpec((1, D, 2 * FFE), lambda i, ids: (i, 0, 0)),
            pl.BlockSpec((1, D, FFE), lambda i, ids: (i, 0, 0)),
        ]
        + [pl.BlockSpec(memory_space=pl.ANY)] * len(kept)
    )
    results = pl.pallas_call(
        functools.partial(expert_kernel, sources, n_local, len(kept)),
        grid_spec=pltpu.PrefetchScalarGridSpec(
            num_scalar_prefetch=1,
            grid=(n_local,),
            in_specs=in_specs,
            out_specs=[saved(columns) for columns in widths]
            + [pl.BlockSpec((tokens, D + TAIL), fixed)] * sources
            + [pl.BlockSpec((tokens, D), fixed)] * sources,
            scratch_shapes=[
                pltpu.VMEM((sources, TAIL, tokens), f32),
                pltpu.VMEM((sources, n_local * CAP, tokens), bf16),
                pltpu.VMEM((sources, n_local * CAP, D), bf16),
                pltpu.VMEM((sources, n_local * CAP, D), bf16),
                pltpu.VMEM((sources, TAIL, tokens), f32),
            ],
        ),
        out_shape=[
            jax.ShapeDtypeStruct((n_local, chunks, rows, columns), bf16) for columns in widths
        ]
        + [jax.ShapeDtypeStruct((tokens, D + TAIL), bf16)] * sources
        + [jax.ShapeDtypeStruct((tokens, D), bf16)] * sources,
        input_output_aliases={3 + 2 * sources + i: i for i in range(len(kept))},
        compiler_params=pltpu.CompilerParams(vmem_limit_bytes=VMEM_BYTES),
        cost_estimate=pl.CostEstimate(
            flops=4 * n_local * rows * D * (4 * tokens + 9 * FFE),
            bytes_accessed=n_local * D * FFE * 6 + tokens * sources * D * 8,
            transcendentals=0,
        ),
        name="experts",
    )(ids, *xs, *gs, own_in, own_out, *kept)
    return results[:4], results[4 : 4 + sources], results[4 + sources :]


def cut_rows_kernel(extra, left_ref, right_ref, *refs):
    out_ref = refs[-1]
    parts, rows = out_ref.shape[0], out_ref.shape[2]
    width = right_ref.shape[1]
    product = dot_tn(left_ref[...], right_ref[...])
    out_ref[:, 0, :, :width] = product.reshape(parts, rows, width).astype(out_ref.dtype)
    if extra:
        normed_ref, logits_ref, gain_ref = refs[:3]
        rest = logits_ref[...]
        tail = jnp.zeros((left_ref.shape[1], TAIL), jnp.float32)
        for _ in range(3):
            term = rest.astype(jnp.bfloat16)
            rest = rest - term.astype(jnp.float32)
            tail = tail + dot_tn(normed_ref[...], term)
        lane = lax.broadcasted_iota(jnp.int32, tail.shape, 1)
        tail = jnp.where(lane == E, gain_ref[...], tail)
        out_ref[:, 0, :, width:] = tail.reshape(parts, rows, TAIL).astype(out_ref.dtype)


def cut_rows(left, right, n_heads, parts, extra=()):
    depth, height = left.shape
    each = height // n_heads
    width = right.shape[1]
    columns = width + (TAIL if extra else 0)
    extra_specs = (
        [
            pl.BlockSpec((depth, each), lambda h: (0, h)),
            pl.BlockSpec((depth, TAIL), lambda h: (0, 0)),
            pl.BlockSpec((each, 1), lambda h: (h, 0)),
        ]
        if extra
        else []
    )
    return pl.pallas_call(
        functools.partial(cut_rows_kernel, bool(extra)),
        grid=(n_heads,),
        in_specs=[
            pl.BlockSpec((depth, each), lambda h: (0, h)),
            pl.BlockSpec((depth, width), lambda h: (0, 0)),
        ]
        + extra_specs,
        out_specs=pl.BlockSpec((parts, 1, each // parts, columns), lambda h: (0, h, 0, 0)),
        out_shape=jax.ShapeDtypeStruct(
            (parts, n_heads, each // parts, columns),
            jnp.bfloat16 if each // parts % 16 == 0 else jnp.float32,
        ),
        compiler_params=pltpu.CompilerParams(vmem_limit_bytes=VMEM_BYTES),
        cost_estimate=pl.CostEstimate(
            flops=4 * depth * height * columns,
            bytes_accessed=depth * (height + width) * 2 + height * columns * 4,
            transcendentals=0,
        ),
        name="cut_rows",
    )(left, right, *extra)


def expert_grads_kernel(order_ref, left_ref, right_ref, own_ref, *others):
    product = dot_tn(left_ref[0], right_ref[0])
    step = pl.program_id(0)

    @pl.when(step == 0)
    def _():
        own_ref[...] = product

    for at, other in enumerate(others):

        @pl.when(step == at + 1)
        def _():
            other[...] = product.astype(jnp.bfloat16)


def expert_grads(order, left, right):
    count, depth, height = left.shape
    width = right.shape[2]
    return pl.pallas_call(
        expert_grads_kernel,
        grid_spec=pltpu.PrefetchScalarGridSpec(
            num_scalar_prefetch=1,
            grid=(count,),
            in_specs=[
                pl.BlockSpec((1, depth, height), lambda i, order: (order[i], 0, 0)),
                pl.BlockSpec((1, depth, width), lambda i, order: (order[i], 0, 0)),
            ],
            out_specs=[pl.BlockSpec((height, width), lambda i, order: (0, 0))] * count,
        ),
        out_shape=[jax.ShapeDtypeStruct((height, width), jnp.float32)]
        + [jax.ShapeDtypeStruct((height, width), jnp.bfloat16)] * (count - 1),
        compiler_params=pltpu.CompilerParams(vmem_limit_bytes=VMEM_BYTES),
        cost_estimate=pl.CostEstimate(
            flops=4 * count * depth * height * width,
            bytes_accessed=2 * count * depth * (height + width) + height * width * (2 * count + 2),
            transcendentals=0,
        ),
        name="expert_grads",
    )(order, left, right)


def plain_grads_kernel(left_ref, right_ref, out_ref):
    out_ref[0] = dot_tn(left_ref[0], right_ref[0]).astype(out_ref.dtype)


def plain_grads(left, right):
    count, depth, height = left.shape
    width = right.shape[2]
    return pl.pallas_call(
        plain_grads_kernel,
        grid=(count,),
        in_specs=[
            pl.BlockSpec((1, depth, height), lambda i: (i, 0, 0)),
            pl.BlockSpec((1, depth, width), lambda i: (i, 0, 0)),
        ],
        out_specs=pl.BlockSpec((1, height, width), lambda i: (i, 0, 0)),
        out_shape=jax.ShapeDtypeStruct((count, height, width), jnp.bfloat16),
        compiler_params=pltpu.CompilerParams(vmem_limit_bytes=VMEM_BYTES),
        cost_estimate=pl.CostEstimate(
            flops=4 * count * depth * height * width,
            bytes_accessed=2 * count * (depth * (height + width) + height * width),
            transcendentals=0,
        ),
        name="plain_grads",
    )(left, right)


def make_local(n_heads, chip, core):
    everyone = ("heads", "chip", "core")
    group_size = n_heads * core
    n_local = E // group_size
    groups_local = KEY_VALUE_HEADS // n_heads
    ring = [(i, (i + 1) % n_heads) for i in range(n_heads)]
    crossed = [(i, core - 1 - i) for i in range(core)]

    def onward(value):
        return lax.ppermute(value, "heads", ring)

    def across(value):
        return lax.ppermute(value, "core", crossed)

    def around(value):
        values = [value]
        for _ in range(n_heads - 1):
            values.append(onward(values[-1]))
        return values

    def both(value):
        return [value] if core == 1 else [value, across(value)]

    def joined(parts):
        total = parts[0].astype(jnp.float32)
        if core > 1:
            total = total + across(parts[1]).astype(jnp.float32)
        return total

    def after(value, *others):
        return lax.optimization_barrier((value,) + others)[0]

    def paired(value, other):
        return lax.ppermute(value, "chip", [(i, i ^ other) for i in range(chip)])

    def spread_rows(cut):
        part = lax.psum_scatter(
            cut.reshape(-1, cut.shape[3]), ("chip", "core"), scatter_dimension=0, tiled=True
        )
        return part.reshape(cut.shape[1:])

    def local(
        tokens,
        cotangent,
        lengths,
        routes,
        attention_input_weight,
        attn_out,
        router,
        gain_attn,
        gain_ffn,
        expert_in,
        expert_out,
    ):
        slots, span, width = tokens.shape
        token_rows = slots * span
        length = span * n_heads
        rank = lax.axis_index("heads")
        qkv_width = attention_input_weight.shape[1]
        own_columns = groups_local * GROUP
        rings = around(tokens)
        small = jnp.concatenate(
            [
                attention_input_weight,
                attn_out,
                router,
                gain_attn[:, None],
                gain_ffn[:, None],
                jnp.zeros((router.shape[0], TAIL - E - 2), jnp.bfloat16),
            ],
            1,
        )
        column = lax.all_to_all(
            jnp.broadcast_to(after(small, rings[1])[None], (n_heads,) + small.shape),
            "heads",
            split_axis=0,
            concat_axis=0,
            tiled=True,
        )

        own_out = lax.all_gather(expert_out, "chip", axis=0, tiled=True).reshape(n_local, D, FFE)

        def plane(value):
            value = lax.all_gather(value, ("chip", "core"), axis=1, tiled=True)
            return value.reshape(-1, value.shape[2])

        first = plane(
            after(
                jnp.concatenate(
                    [
                        lax.dynamic_slice_in_dim(column, rank * own_columns, own_columns, 2),
                        column[:, :, qkv_width + D :],
                    ],
                    2,
                ),
                own_out,
                rings[2],
            )
        )
        w_own = first
        gain_one = first[:, own_columns + E].astype(jnp.float32)
        w_proj = plane(column[:, :, qkv_width:])
        w_router = w_proj[:, D : D + E]
        gain_two = w_proj[:, D + E + 1].astype(jnp.float32)
        w_proj = w_proj[:, :D]
        own_grads = cotangent.reshape(token_rows, width)
        own_in = lax.all_gather(after(expert_in, first, rings[-1]), "chip", axis=0, tiled=True).reshape(
            n_local, D, 2 * FFE
        )

        positions = rank * span + jnp.arange(span, dtype=jnp.int32)
        valid = (positions[None, :] < lengths[:, None]).reshape(token_rows)
        valid_float = valid.astype(jnp.float32)[:, None]
        route_rows = routes.reshape(token_rows, TOPK)
        routed = jnp.any(
            route_rows[:, :, None] == jnp.arange(E, dtype=jnp.int32)[None, None, :], 1
        )
        live = (routed & valid[:, None]).astype(jnp.bfloat16)
        earlier = (
            jnp.arange(token_rows)[:, None] > jnp.arange(token_rows)[None, :]
        ).astype(jnp.bfloat16)
        count = jnp.dot(earlier, live, preferred_element_type=jnp.float32)
        kept = (live > 0) & (count < CAP)
        code = jnp.where(kept, count, -1.0).astype(jnp.bfloat16)
        ids = (rank * n_local + jnp.arange(n_local, dtype=jnp.int32)) * core + lax.axis_index("core")

        tables = rotary_tables(length)
        places = (rank + n_heads - jnp.arange(n_heads, dtype=jnp.int32)) % n_heads
        packed, context_heads, lse, normed_whole = attention_forward(
            rings, places, gain_one[None, :], w_own, tables, groups_local
        )
        grad_ring = [own_grads, onward(after(own_grads, rings[-1]))]
        context_heads = after(context_heads, grad_ring[1])
        context = lax.all_to_all(context_heads, "heads", split_axis=0, concat_axis=0, tiled=True)
        grad_ring.append(onward(after(grad_ring[1], context)))
        heads_width = groups_local * PAIR
        context = context.reshape(n_heads, token_rows, heads_width)

        state = tokens.astype(jnp.float32).reshape(token_rows, width)
        mid_state = state
        for h in range(n_heads):
            mid_state = mid_state + dot_nn(
                context[h], w_proj[h * heads_width : (h + 1) * heads_width]
            )
        factor_two = norm_factor(mid_state)
        normed_ffn = (mid_state * factor_two * gain_two).astype(jnp.bfloat16)
        logits = jnp.dot(normed_ffn, w_router, preferred_element_type=jnp.float32)
        highest = jnp.max(jnp.where(routed, logits, NEGATIVE), -1, keepdims=True)
        weights = jnp.where(routed, jnp.exp(jnp.where(routed, logits - highest, 0.0)), 0.0)
        gates = weights / jnp.sum(weights, -1, keepdims=True)
        gates_high = lax.reduce_precision(gates, 8, 7)
        payload = jnp.concatenate(
            [
                normed_ffn,
                code,
                gates_high.astype(jnp.bfloat16),
                (gates - gates_high).astype(jnp.bfloat16),
                jnp.zeros((token_rows, TAIL - 3 * E), jnp.bfloat16),
            ],
            1,
        )
        payloads = around(after(payload, grad_ring[2]))
        for step in range(2, n_heads - 1):
            grad_ring.append(onward(after(grad_ring[-1], payloads[1])))
        saved, backs, mixes, moving = (), [], [], None
        for step, value in enumerate(payloads):
            xs, gs = both(value), both(grad_ring[step])
            ahead = min(step + 1, n_heads - 1)
            if step:
                xs[0] = after(xs[0], payloads[ahead], grad_ring[min(step + 2, n_heads - 1)])
            if moving is not None:
                xs[0] = after(xs[0], moving)
            saved, back, mix = experts(
                step, n_heads, ids, xs, gs, own_in, own_out, tuple(saved)
            )
            backs.append(back)
            mixes.append(mix)
            if step:
                total = joined(back)
                if moving is not None:
                    total = total + onward(moving).astype(jnp.float32)
                moving = total.astype(jnp.bfloat16)
        buffer, grad_outputs, hidden, grad_pre = [
            value.reshape(n_local, group_size * CAP, value.shape[3]) for value in saved
        ]
        hidden = after(hidden, moving)
        last_back = onward(moving)
        grad_pre = after(grad_pre, last_back)
        if expert_in.shape[0] == D:
            order = lax.axis_index("chip") ^ jnp.arange(chip, dtype=jnp.int32)
            parts_in = expert_grads(order, buffer, grad_pre)
        else:
            parts_in = [plain_grads(buffer, grad_pre)]
        parts_out = plain_grads(grad_outputs, hidden)
        grad_expert_out = lax.psum_scatter(
            parts_out.reshape(-1, FFE), "chip", scatter_dimension=0, tiled=True
        ).astype(jnp.float32)
        w_qkv = plane(after(column[:, :, :qkv_width], context))
        mix_moving = joined(mixes[1]).astype(jnp.bfloat16)
        mix_received = onward(after(mix_moving, last_back))
        back_sum = joined(backs[0]) + after(last_back, w_qkv, parts_out, *parts_in).astype(jnp.float32)

        grad_gates = back_sum[:, width : width + E] + back_sum[:, width + E : width + 2 * E]
        grad_logits = gates * (grad_gates - jnp.sum(gates * grad_gates, -1, keepdims=True))
        grad_logits = grad_logits * valid_float
        grad_out = cotangent.astype(jnp.float32).reshape(token_rows, width) * valid_float
        grad_normed_ffn = back_sum[:, :width] + jnp.dot(
            grad_logits, w_router.astype(jnp.float32).T, precision=TOP_PRECISION
        )
        grad_mid_norm, gain_two_term = norm_back(grad_normed_ffn, mid_state, factor_two, gain_two)
        grad_mid = grad_out + grad_mid_norm
        grad_mid_low = grad_mid.astype(jnp.bfloat16)
        context_gradient = jnp.stack(
            [
                dot_nt(grad_mid_low, w_proj[h * heads_width : (h + 1) * heads_width])
                for h in range(n_heads)
            ]
        ).astype(jnp.bfloat16)
        context_gradient = after(context_gradient, mix_received)
        grad_context_heads = lax.all_to_all(
            context_gradient.reshape(n_heads, slots, span, heads_width),
            "heads",
            split_axis=0,
            concat_axis=0,
            tiled=True,
        )
        logits_padded = jnp.concatenate(
            [grad_logits, jnp.zeros((token_rows, TAIL - E), jnp.float32)], 1
        )
        second = cut_rows(
            jnp.concatenate([context[h] for h in range(n_heads)], 1),
            after(grad_mid_low, context_gradient),
            n_heads,
            chip * core,
            (normed_ffn, logits_padded, gain_two_term[:, None]),
        )
        grad_context_heads = after(grad_context_heads, second)
        second = spread_rows(second)

        grad_before = None
        for chunk in range(2, n_heads):
            mix_moving = (joined(mixes[chunk]) + mix_received.astype(jnp.float32)).astype(
                jnp.bfloat16
            )
            if chunk == 2:
                grad_before = attention_backward(
                    packed, lse, after(grad_context_heads, mix_moving), tables, groups_local
                )
            if chunk < n_heads - 1:
                mix_received = onward(after(mix_moving, grad_context_heads))
        received = []
        if len(parts_in) > 1:
            received = [paired(parts_in[1], 1), paired(parts_in[2], 2)]
        grad_before = after(grad_before, mix_moving, grad_expert_out, *received)
        grad_mine = lax.all_to_all(
            grad_before, "heads", split_axis=0, concat_axis=0, tiled=True
        ).reshape(n_heads, token_rows, own_columns)
        qkv_part = spread_rows(
            cut_rows(
                normed_whole.reshape(-1, width),
                grad_before.reshape(-1, own_columns),
                n_heads,
                chip * core,
            )
        )
        if received:
            received.append(paired(after(parts_in[3], *received), 3))
        else:
            grad_expert_in = lax.psum_scatter(
                parts_in[0].reshape(-1, 2 * FFE), "chip", scatter_dimension=0, tiled=True
            ).astype(jnp.float32)
        grad_normed_attn = dot_nt(grad_mine[0], w_qkv[:, :own_columns])
        for h in range(1, n_heads):
            grad_normed_attn = grad_normed_attn + dot_nt(
                grad_mine[h], w_qkv[:, h * own_columns : (h + 1) * own_columns]
            )
        grad_state_norm, _ = norm_back(grad_normed_attn, state, norm_factor(state), gain_one)
        grad_tokens = (grad_mid + grad_state_norm).astype(jnp.bfloat16).reshape(tokens.shape)
        if received:
            received[-1] = after(received[-1], grad_tokens)
            grad_expert_in = parts_in[0]
            for value in received:
                grad_expert_in = grad_expert_in + value.astype(jnp.float32)
        mixture = joined(mixes[0]) + onward(after(mix_moving, grad_mine)).astype(jnp.float32)
        mixed = (valid_float * (mid_state + mixture)).astype(jnp.bfloat16)

        last = lax.all_to_all(
            after(jnp.concatenate([second, qkv_part], 2), grad_mine),
            "heads",
            split_axis=0,
            concat_axis=0,
            tiled=True,
        ).astype(jnp.float32)
        second = jnp.sum(last[:, :, : D + TAIL], 0)
        grad_attn_out = second[:, :D]
        grad_router = second[:, D : D + E]
        grad_gain_ffn = second[:, D + E]
        grad_attn_in = jnp.concatenate([last[h, :, D + TAIL :] for h in range(n_heads)], 1)
        grad_gain_attn = jnp.sum(
            grad_attn_in * attention_input_weight.astype(jnp.float32), -1
        ) / gain_attn.astype(jnp.float32)
        return (
            mixed.reshape(tokens.shape),
            grad_tokens,
            grad_attn_in,
            grad_attn_out,
            grad_router,
            grad_gain_attn,
            grad_gain_ffn,
            grad_expert_in,
            grad_expert_out,
        )

    return local


def solution(mesh):
    n_heads, n_shard = mesh.shape["heads"], mesh.shape["shard"]
    core = 2 if n_heads * n_shard == E else 1
    chip = n_shard // core
    split = jax.sharding.Mesh(
        mesh.devices.reshape(n_heads, chip, core), ("heads", "chip", "core")
    )
    shard = ("chip", "core")
    everyone = ("heads", "chip", "core")
    token_spec = P(shard, "heads", None)
    rows = P(everyone, None)
    in_specs = (
        token_spec,
        token_spec,
        P(shard),
        token_spec,
        rows,
        rows,
        rows,
        P(everyone),
        P(everyone),
        rows,
        rows,
    )
    out_specs = (token_spec, token_spec, rows, rows, rows, P(everyone), P(everyone), rows, rows)
    return jax.shard_map(
        make_local(n_heads, chip, core),
        mesh=split,
        in_specs=in_specs,
        out_specs=out_specs,
        check_vma=False,
    )
```

```python
import functools
import math

import jax
import jax.numpy as jnp
import numpy as np
from jax import lax
from jax.experimental import pallas as pl
from jax.experimental.pallas import tpu as pltpu
from jax.sharding import PartitionSpec as P

D = 1024
QUERY_HEADS = 16
KEY_VALUE_HEADS = 8
HEAD_SIZE = 64
E = 32
FFE = 512
TOPK = 8
QUERIES_PER_KV = 2
CAP = 160
GROUP = (QUERIES_PER_KV + 2) * HEAD_SIZE
PAIR = QUERIES_PER_KV * HEAD_SIZE
TAIL = 128
BLOCK = 256
VMEM_BYTES = 56 * 2**20


EPSILON = 1e-06
THETA_BASE = 10000.0
NEGATIVE = -1e30
TOP_PRECISION = lax.Precision.HIGHEST
SCALE = 1.0 / math.sqrt(HEAD_SIZE)
SHORT = pl.CostEstimate(flops=1024, bytes_accessed=1024, transcendentals=0)


def dot_nn(left, right):
    return jnp.dot(left, right, preferred_element_type=jnp.float32)


def dot_nt(left, right):
    return lax.dot_general(
        left, right, (((1,), (1,)), ((), ())), preferred_element_type=jnp.float32
    )


def dot_tn(left, right):
    return lax.dot_general(
        left, right, (((0,), (0,)), ((), ())), preferred_element_type=jnp.float32
    )


def norm_factor(value):
    return lax.rsqrt(jnp.mean(value * value, -1, keepdims=True) + EPSILON)


def norm_back(grad_in, value, factor, gain):
    normalized_rows = value * factor
    scaled = grad_in * gain
    gain_term = jnp.sum(grad_in * normalized_rows, 0)
    grad_value = factor * (
        scaled - normalized_rows * jnp.mean(scaled * normalized_rows, -1, keepdims=True)
    )
    return (grad_value, gain_term)


def rotary_tables(length):
    half_size = HEAD_SIZE // 2
    freqs = THETA_BASE ** (-2.0 * np.arange(half_size) / HEAD_SIZE)
    angles = np.arange(length)[:, None] * freqs[None, :]
    cosine, sine = np.cos(angles), np.sin(angles)
    one = np.ones((length, HEAD_SIZE))
    own = np.concatenate([cosine, cosine] * (QUERIES_PER_KV + 1) + [one], 1)
    other = np.concatenate([-sine, sine] * (QUERIES_PER_KV + 1) + [0.0 * one], 1)
    return (jnp.asarray(own, jnp.float32), jnp.asarray(other, jnp.float32))


def partner(values):
    width = values.shape[1]
    lane = lax.broadcasted_iota(jnp.int32, values.shape, 1)
    half_size = HEAD_SIZE // 2
    return jnp.where(
        lax.rem(lane, HEAD_SIZE) < half_size,
        pltpu.roll(values, width - half_size, 1),
        pltpu.roll(values, half_size, 1),
    )


def stack_queries(block):
    values = block.astype(jnp.float32) * SCALE
    low = lax.broadcasted_iota(jnp.int32, values.shape, 1) < HEAD_SIZE
    first = jnp.where(low, values, 0.0)
    second = jnp.where(low, pltpu.roll(values, HEAD_SIZE, 1), 0.0)
    return jnp.concatenate([first, second], 0).astype(jnp.bfloat16)


def stack_grads(block):
    values = block.astype(jnp.float32)
    low = lax.broadcasted_iota(jnp.int32, values.shape, 1) < HEAD_SIZE
    first = jnp.where(low, 0.0, pltpu.roll(values, HEAD_SIZE, 1))
    second = jnp.where(low, 0.0, values)
    return jnp.concatenate([first, second], 0).astype(jnp.bfloat16)


def attention_forward_kernel(pieces, place_ref, *refs):
    xs, refs = refs[:pieces], refs[pieces:]
    gain_ref, w_ref, own_ref, other_ref = refs[:4]
    packed_ref, context_ref, lse_ref, normed_ref = refs[4:]
    span = xs[0].shape[1]
    length = pieces * span

    @pl.when(pl.program_id(1) == 0)
    def _():
        for step in range(pieces):
            at = place_ref[step]
            for start in range(0, span, BLOCK):
                value = xs[step][0, start : start + BLOCK, :].astype(jnp.float32)
                normed_ref[at, 0, start : start + BLOCK, :] = (
                    value * norm_factor(value) * gain_ref[...]
                ).astype(jnp.bfloat16)

    for start in range(0, length, BLOCK):
        rows = slice(start, start + BLOCK)
        before = dot_nn(
            normed_ref[start // span, 0, start % span : start % span + BLOCK, :], w_ref[...]
        )
        packed_ref[0, rows, :] = (
            before * own_ref[rows, :] + partner(before) * other_ref[rows, :]
        ).astype(jnp.bfloat16)

    low = lax.broadcasted_iota(jnp.int32, (BLOCK, PAIR), 1) < HEAD_SIZE
    lane_zero = lax.broadcasted_iota(jnp.int32, (BLOCK, PAIR), 1) == 0
    query_row = lax.rem(lax.broadcasted_iota(jnp.int32, (2 * BLOCK, BLOCK), 0), BLOCK)
    allowed = lax.broadcasted_iota(jnp.int32, (2 * BLOCK, BLOCK), 1) <= query_row
    for start in range(0, length, BLOCK):
        rows = slice(start, start + BLOCK)
        queries = stack_queries(packed_ref[0, rows, :PAIR])
        inside = packed_ref[0, rows, PAIR:]
        scores_inside = jnp.where(allowed, dot_nt(queries, inside), NEGATIVE)
        highest = jnp.max(scores_inside, 1, keepdims=True)
        if start:
            before_keys = packed_ref[0, :start, PAIR:]
            scores_before = dot_nt(queries, before_keys)
            highest = jnp.maximum(highest, jnp.max(scores_before, 1, keepdims=True))
        weights = jnp.exp(scores_inside - highest)
        total = jnp.sum(weights, 1, keepdims=True)
        result = dot_nn(weights.astype(jnp.bfloat16), inside)
        if start:
            weights = jnp.exp(scores_before - highest)
            total = total + jnp.sum(weights, 1, keepdims=True)
            result = result + dot_nn(weights.astype(jnp.bfloat16), before_keys)
        result = result / total
        context_ref[start // span, 0, start % span : start % span + BLOCK, :] = jnp.where(
            low, pltpu.roll(result[:BLOCK], HEAD_SIZE, 1), result[BLOCK:]
        ).astype(jnp.bfloat16)
        log_total = highest + jnp.log(total)
        columns = jnp.where(lane_zero, log_total[:BLOCK], log_total[BLOCK:])
        lse_ref[0, 0, :, rows] = columns.T[:8, :]


def attention_forward(xs, places, gain, weights, tables, groups_local):
    pieces = len(xs)
    slots, span, width = xs[0].shape
    length = pieces * span
    bf16, f32 = jnp.bfloat16, jnp.float32
    return pl.pallas_call(
        functools.partial(attention_forward_kernel, pieces),
        grid_spec=pltpu.PrefetchScalarGridSpec(
            num_scalar_prefetch=1,
            grid=(slots, groups_local),
            in_specs=[pl.BlockSpec((1, span, width), lambda s, g, place: (s, 0, 0))] * pieces
            + [
                pl.BlockSpec((1, width), lambda s, g, place: (0, 0)),
                pl.BlockSpec((width, GROUP), lambda s, g, place: (0, g)),
                pl.BlockSpec((length, GROUP), lambda s, g, place: (0, 0)),
                pl.BlockSpec((length, GROUP), lambda s, g, place: (0, 0)),
            ],
            out_specs=[
                pl.BlockSpec((1, length, GROUP), lambda s, g, place: (s, 0, g)),
                pl.BlockSpec((pieces, 1, span, PAIR), lambda s, g, place: (0, s, 0, g)),
                pl.BlockSpec((1, 1, 8, length), lambda s, g, place: (s, g, 0, 0)),
                pl.BlockSpec((pieces, 1, span, width), lambda s, g, place: (0, s, 0, 0)),
            ],
        ),
        out_shape=[
            jax.ShapeDtypeStruct((slots, length, groups_local * GROUP), bf16),
            jax.ShapeDtypeStruct((pieces, slots, span, groups_local * PAIR), bf16),
            jax.ShapeDtypeStruct((slots, groups_local, 8, length), f32),
            jax.ShapeDtypeStruct((pieces, slots, span, width), bf16),
        ],
        compiler_params=pltpu.CompilerParams(vmem_limit_bytes=VMEM_BYTES),
        cost_estimate=SHORT,
        name="attention_forward",
    )(places, *xs, gain, weights, *tables)


def attention_backward_kernel(
    packed_ref,
    lse_ref,
    grad_ref,
    normed_ref,
    own_ref,
    other_ref,
    out_ref,
    cut_ref,
    total_ref,
    product_ref,
):
    length, span = packed_ref.shape[1], grad_ref.shape[2]
    low = lax.broadcasted_iota(jnp.int32, (BLOCK, PAIR), 1) < HEAD_SIZE
    query_lane = lax.rem(lax.broadcasted_iota(jnp.int32, (BLOCK, 2 * BLOCK), 1), BLOCK)
    allowed = lax.broadcasted_iota(jnp.int32, (BLOCK, 2 * BLOCK), 0) <= query_lane
    total_ref[...] = jnp.zeros_like(total_ref)

    def unturn(values, lanes, rows):
        values = values.astype(jnp.bfloat16).astype(jnp.float32)
        return (
            values * own_ref[rows, lanes] - partner(values) * other_ref[rows, lanes]
        ).astype(jnp.bfloat16)

    for start in range(0, length, BLOCK):
        rows = slice(start, start + BLOCK)
        queries = stack_queries(packed_ref[0, rows, :PAIR])
        inner = slice(start % span, start % span + BLOCK)
        grads = stack_grads(grad_ref[start // span, 0, inner, :])
        log_total = jnp.concatenate([lse_ref[0, 0, 0:1, rows], lse_ref[0, 0, 1:2, rows]], 1)

        def piece(keys):
            scores = dot_nt(keys, queries)
            probs = jnp.exp(scores - log_total)
            return (probs, dot_nt(keys, grads))

        inside = packed_ref[0, rows, PAIR:]
        probs_inside, grad_inside = piece(inside)
        probs_inside = jnp.where(allowed, probs_inside, 0.0)
        delta = jnp.sum(probs_inside * grad_inside, 0, keepdims=True)
        if start:
            before = packed_ref[0, :start, PAIR:]
            probs_before, grad_before = piece(before)
            delta = delta + jnp.sum(probs_before * grad_before, 0, keepdims=True)
        score_grads = (probs_inside * (grad_inside - delta)).astype(jnp.bfloat16)
        total_ref[rows, :] += dot_nn(probs_inside.astype(jnp.bfloat16), grads) + dot_nn(
            score_grads, queries
        )
        grad_query = dot_tn(score_grads, inside)
        if start:
            score_grads = (probs_before * (grad_before - delta)).astype(jnp.bfloat16)
            total_ref[:start, :] += dot_nn(probs_before.astype(jnp.bfloat16), grads) + dot_nn(
                score_grads, queries
            )
            grad_query = grad_query + dot_tn(score_grads, before)
        grad_query = (
            jnp.where(low, grad_query[:BLOCK], pltpu.roll(grad_query[BLOCK:], HEAD_SIZE, 1)) * SCALE
        )
        out_ref[start // span, 0, inner, :PAIR] = unturn(grad_query, slice(0, PAIR), rows)
    for start in range(0, length, BLOCK):
        rows = slice(start, start + BLOCK)
        inner = slice(start % span, start % span + BLOCK)
        out_ref[start // span, 0, inner, PAIR:] = unturn(
            total_ref[rows, :], slice(PAIR, GROUP), rows
        )

    @pl.when(pl.program_id(1) == 0)
    def _():
        product_ref[...] = jnp.zeros_like(product_ref)

    for at in range(length // span):
        product_ref[...] += dot_tn(normed_ref[at, 0], out_ref[at, 0])

    @pl.when(pl.program_id(1) == pl.num_programs(1) - 1)
    def _():
        parts, heads, each = cut_ref.shape[:3]
        for h in range(heads):
            block = product_ref[h * parts * each : (h + 1) * parts * each, :]
            cut_ref[:, h] = block.reshape(parts, each, GROUP).astype(cut_ref.dtype)


def attention_backward(packed, lse, grads, normed, tables, groups_local, parts):
    slots, length = packed.shape[:2]
    pieces, span, width = grads.shape[0], grads.shape[2], normed.shape[3]
    each = width // (pieces * parts)
    kind = jnp.bfloat16 if each % 16 == 0 else jnp.float32
    return pl.pallas_call(
        attention_backward_kernel,
        grid=(groups_local, slots),
        in_specs=[
            pl.BlockSpec((1, length, GROUP), lambda g, s: (s, 0, g)),
            pl.BlockSpec((1, 1, 8, length), lambda g, s: (s, g, 0, 0)),
            pl.BlockSpec((pieces, 1, span, PAIR), lambda g, s: (0, s, 0, g)),
            pl.BlockSpec((pieces, 1, span, width), lambda g, s: (0, s, 0, 0)),
            pl.BlockSpec((length, GROUP), lambda g, s: (0, 0)),
            pl.BlockSpec((length, GROUP), lambda g, s: (0, 0)),
        ],
        out_specs=[
            pl.BlockSpec((pieces, 1, span, GROUP), lambda g, s: (0, s, 0, g)),
            pl.BlockSpec((parts, pieces, each, GROUP), lambda g, s: (0, 0, 0, g)),
        ],
        out_shape=[
            jax.ShapeDtypeStruct((pieces, slots, span, packed.shape[2]), jnp.bfloat16),
            jax.ShapeDtypeStruct((parts, pieces, each, packed.shape[2]), kind),
        ],
        scratch_shapes=[
            pltpu.VMEM((length, PAIR), jnp.float32),
            pltpu.VMEM((width, GROUP), jnp.float32),
        ],
        compiler_params=pltpu.CompilerParams(vmem_limit_bytes=VMEM_BYTES),
        cost_estimate=SHORT,
        name="attention_backward",
    )(packed, lse, grads, normed, *tables)


def expert_kernel(sources, n_local, kept, ids_ref, *refs):
    xs, refs = refs[:sources], refs[sources:]
    gs, refs = refs[:sources], refs[sources:]
    w_in_ref, w_out_ref = refs[:2]
    refs = refs[2 + kept :]
    buffer_ref, grad_out_ref, hidden_ref, grad_pre_ref = refs[:4]
    backs, mixes = refs[4 : 4 + sources], refs[4 + sources : 4 + 2 * sources]
    table, picks, mix_rows, back_rows, gate_back = refs[4 + 2 * sources :]
    step = pl.program_id(0)
    expert = ids_ref[step]
    tokens = xs[0].shape[0]
    here = pl.ds(pl.multiple_of(step * CAP, 16), CAP)

    @pl.when(step == 0)
    def _():
        for s in range(sources):
            table[s] = xs[s][:, D:].astype(jnp.float32).T
            gate_back[s] = jnp.zeros((TAIL, tokens), jnp.float32)

    place = lax.broadcasted_iota(jnp.int32, (CAP, tokens), 0).astype(jnp.float32)
    hits, gate_rows, grad_rows = [], [], []
    for s in range(sources):
        code = table[s, pl.ds(expert, 1), :]
        gate = table[s, pl.ds(expert + E, 1), :] + table[s, pl.ds(expert + 2 * E, 1), :]
        hit = code == place
        pick = jnp.where(hit, 1.0, 0.0).astype(jnp.bfloat16)
        picks[s, here, :] = pick
        hits.append(hit)
        gate_rows.append(jnp.sum(jnp.where(hit, gate, 0.0), 1, keepdims=True))
        buffer_ref[0, 0, s * CAP : (s + 1) * CAP, :] = dot_nn(pick, xs[s][:, :D]).astype(
            jnp.bfloat16
        )
        grad_rows.append(dot_nn(pick, gs[s][...]))
    gate_row = jnp.concatenate(gate_rows, 0)
    grad_row = jnp.concatenate(grad_rows, 0)
    grad_out_ref[0, 0] = (gate_row * grad_row).astype(jnp.bfloat16)
    pre = dot_nn(buffer_ref[0, 0], w_in_ref[0])
    grad_plain = dot_nn(grad_row.astype(jnp.bfloat16), w_out_ref[0])
    gate_pre, up_pre = pre[:, :FFE], pre[:, FFE:]
    sigmoid_gate = 1.0 / (1.0 + jnp.exp(-gate_pre))
    silu_gate = gate_pre * sigmoid_gate
    hidden = (silu_gate * up_pre).astype(jnp.bfloat16)
    hidden_ref[0, 0] = hidden
    gate_grad = jnp.sum(grad_plain * hidden.astype(jnp.float32), 1, keepdims=True)
    grad_hidden = gate_row * grad_plain
    grad_pre_ref[0, 0, :, :FFE] = (
        grad_hidden * up_pre * sigmoid_gate * (1.0 + gate_pre * (1.0 - sigmoid_gate))
    ).astype(jnp.bfloat16)
    grad_pre_ref[0, 0, :, FFE:] = (grad_hidden * silu_gate).astype(jnp.bfloat16)
    outputs = (gate_row * dot_nt(hidden, w_out_ref[0])).astype(jnp.bfloat16)
    back = dot_nt(grad_pre_ref[0, 0], w_in_ref[0]).astype(jnp.bfloat16)
    for s in range(sources):
        part = slice(s * CAP, (s + 1) * CAP)
        mix_rows[s, here, :] = outputs[part]
        back_rows[s, here, :] = back[part]
        row = jnp.sum(jnp.where(hits[s], gate_grad[part], 0.0), 0, keepdims=True)
        high = row.astype(jnp.bfloat16).astype(jnp.float32)
        gate_back[s, pl.ds(expert, 1), :] = high
        gate_back[s, pl.ds(expert + E, 1), :] = row - high

    @pl.when(step == n_local - 1)
    def _():
        for s in range(sources):
            backs[s][:, :D] = dot_tn(picks[s], back_rows[s]).astype(jnp.bfloat16)
            backs[s][:, D:] = gate_back[s].T.astype(jnp.bfloat16)
            mixes[s][...] = dot_tn(picks[s], mix_rows[s]).astype(jnp.bfloat16)


def experts(chunk, chunks, ids, xs, gs, own_in, own_out, kept):
    sources, n_local, tokens = len(xs), own_in.shape[0], xs[0].shape[0]
    rows = sources * CAP
    bf16, f32 = jnp.bfloat16, jnp.float32
    fixed = lambda i, ids: (0, 0)
    saved = lambda columns: pl.BlockSpec((1, 1, rows, columns), lambda i, ids: (i, chunk, 0, 0))
    widths = (D, D, FFE, 2 * FFE)
    in_specs = (
        [pl.BlockSpec((tokens, D + TAIL), fixed)] * sources
        + [pl.BlockSpec((tokens, D), fixed)] * sources
        + [
            pl.BlockSpec((1, D, 2 * FFE), lambda i, ids: (i, 0, 0)),
            pl.BlockSpec((1, D, FFE), lambda i, ids: (i, 0, 0)),
        ]
        + [pl.BlockSpec(memory_space=pl.ANY)] * len(kept)
    )
    results = pl.pallas_call(
        functools.partial(expert_kernel, sources, n_local, len(kept)),
        grid_spec=pltpu.PrefetchScalarGridSpec(
            num_scalar_prefetch=1,
            grid=(n_local,),
            in_specs=in_specs,
            out_specs=[saved(columns) for columns in widths]
            + [pl.BlockSpec((tokens, D + TAIL), fixed)] * sources
            + [pl.BlockSpec((tokens, D), fixed)] * sources,
            scratch_shapes=[
                pltpu.VMEM((sources, TAIL, tokens), f32),
                pltpu.VMEM((sources, n_local * CAP, tokens), bf16),
                pltpu.VMEM((sources, n_local * CAP, D), bf16),
                pltpu.VMEM((sources, n_local * CAP, D), bf16),
                pltpu.VMEM((sources, TAIL, tokens), f32),
            ],
        ),
        out_shape=[
            jax.ShapeDtypeStruct((n_local, chunks, rows, columns), bf16) for columns in widths
        ]
        + [jax.ShapeDtypeStruct((tokens, D + TAIL), bf16)] * sources
        + [jax.ShapeDtypeStruct((tokens, D), bf16)] * sources,
        input_output_aliases={3 + 2 * sources + i: i for i in range(len(kept))},
        compiler_params=pltpu.CompilerParams(vmem_limit_bytes=VMEM_BYTES),
        cost_estimate=pl.CostEstimate(
            flops=n_local * rows * D * (4 * tokens + 9 * FFE),
            bytes_accessed=n_local * D * FFE * 6 + tokens * sources * D * 8,
            transcendentals=0,
        ),
        name="experts",
    )(ids, *xs, *gs, own_in, own_out, *kept)
    return results[:4], results[4 : 4 + sources], results[4 + sources :]


def cut_rows_kernel(extra, left_ref, right_ref, *refs):
    out_ref = refs[-1]
    parts, rows = out_ref.shape[0], out_ref.shape[2]
    width = right_ref.shape[1]
    product = dot_tn(left_ref[...], right_ref[...])
    out_ref[:, 0, :, :width] = product.reshape(parts, rows, width).astype(out_ref.dtype)
    if extra:
        normed_ref, logits_ref, gain_ref = refs[:3]
        rest = logits_ref[...]
        tail = jnp.zeros((left_ref.shape[1], TAIL), jnp.float32)
        for _ in range(3):
            term = rest.astype(jnp.bfloat16)
            rest = rest - term.astype(jnp.float32)
            tail = tail + dot_tn(normed_ref[...], term)
        lane = lax.broadcasted_iota(jnp.int32, tail.shape, 1)
        tail = jnp.where(lane == E, gain_ref[...], tail)
        out_ref[:, 0, :, width:] = tail.reshape(parts, rows, TAIL).astype(out_ref.dtype)


def cut_rows(left, right, n_heads, parts, extra=()):
    depth, height = left.shape
    each = height // n_heads
    width = right.shape[1]
    columns = width + (TAIL if extra else 0)
    extra_specs = (
        [
            pl.BlockSpec((depth, each), lambda h: (0, h)),
            pl.BlockSpec((depth, TAIL), lambda h: (0, 0)),
            pl.BlockSpec((each, 1), lambda h: (h, 0)),
        ]
        if extra
        else []
    )
    return pl.pallas_call(
        functools.partial(cut_rows_kernel, bool(extra)),
        grid=(n_heads,),
        in_specs=[
            pl.BlockSpec((depth, each), lambda h: (0, h)),
            pl.BlockSpec((depth, width), lambda h: (0, 0)),
        ]
        + extra_specs,
        out_specs=pl.BlockSpec((parts, 1, each // parts, columns), lambda h: (0, h, 0, 0)),
        out_shape=jax.ShapeDtypeStruct(
            (parts, n_heads, each // parts, columns),
            jnp.bfloat16 if each // parts % 16 == 0 else jnp.float32,
        ),
        compiler_params=pltpu.CompilerParams(vmem_limit_bytes=VMEM_BYTES),
        cost_estimate=pl.CostEstimate(
            flops=4 * depth * height * columns,
            bytes_accessed=depth * (height + width) * 2 + height * columns * 4,
            transcendentals=0,
        ),
        name="cut_rows",
    )(left, right, *extra)


def expert_grads_kernel(
    order_ref, left_ref, right_ref, own_ref, first_send, second_send, first_keep, second_keep
):
    product = dot_tn(left_ref[0], right_ref[0])
    step = pl.program_id(0)
    half = product.shape[0] // 2
    low = jnp.bfloat16

    @pl.when(step == 0)
    def _():
        own_ref[...] = product

    @pl.when(step == 1)
    def _():
        first_send[0] = product[:half].astype(low)
        second_keep[...] = product[half:]

    @pl.when(step == 2)
    def _():
        first_keep[...] = product[:half]
        second_send[0] = product[half:].astype(low)

    @pl.when(step == 3)
    def _():
        first_send[1] = product[:half].astype(low)
        second_send[1] = product[half:].astype(low)


def expert_grads(order, left, right):
    count, depth, height = left.shape
    width = right.shape[2]
    half = height // 2
    bf16, f32 = jnp.bfloat16, jnp.float32
    whole, pair, one = (height, width), (2, half, width), (half, width)
    return pl.pallas_call(
        expert_grads_kernel,
        grid_spec=pltpu.PrefetchScalarGridSpec(
            num_scalar_prefetch=1,
            grid=(count,),
            in_specs=[
                pl.BlockSpec((1, depth, height), lambda i, order: (order[i], 0, 0)),
                pl.BlockSpec((1, depth, width), lambda i, order: (order[i], 0, 0)),
            ],
            out_specs=[
                pl.BlockSpec(whole, lambda i, order: (0, 0)),
                pl.BlockSpec(pair, lambda i, order: (0, 0, 0)),
                pl.BlockSpec(pair, lambda i, order: (0, 0, 0)),
                pl.BlockSpec(one, lambda i, order: (0, 0)),
                pl.BlockSpec(one, lambda i, order: (0, 0)),
            ],
        ),
        out_shape=[
            jax.ShapeDtypeStruct(whole, f32),
            jax.ShapeDtypeStruct(pair, bf16),
            jax.ShapeDtypeStruct(pair, bf16),
            jax.ShapeDtypeStruct(one, f32),
            jax.ShapeDtypeStruct(one, f32),
        ],
        compiler_params=pltpu.CompilerParams(vmem_limit_bytes=VMEM_BYTES),
        cost_estimate=SHORT,
        name="expert_grads",
    )(order, left, right)


def plain_grads_kernel(left_ref, right_ref, out_ref):
    out_ref[0] = dot_tn(left_ref[0], right_ref[0]).astype(out_ref.dtype)


def plain_grads(left, right):
    count, depth, height = left.shape
    width = right.shape[2]
    return pl.pallas_call(
        plain_grads_kernel,
        grid=(count,),
        in_specs=[
            pl.BlockSpec((1, depth, height), lambda i: (i, 0, 0)),
            pl.BlockSpec((1, depth, width), lambda i: (i, 0, 0)),
        ],
        out_specs=pl.BlockSpec((1, height, width), lambda i: (i, 0, 0)),
        out_shape=jax.ShapeDtypeStruct((count, height, width), jnp.bfloat16),
        compiler_params=pltpu.CompilerParams(vmem_limit_bytes=VMEM_BYTES),
        cost_estimate=pl.CostEstimate(
            flops=4 * count * depth * height * width,
            bytes_accessed=2 * count * (depth * (height + width) + height * width),
            transcendentals=0,
        ),
        name="plain_grads",
    )(left, right)


def make_local(n_heads, chip, core):
    everyone = ("heads", "chip", "core")
    group_size = n_heads * core
    n_local = E // group_size
    groups_local = KEY_VALUE_HEADS // n_heads
    ring = [(i, (i + 1) % n_heads) for i in range(n_heads)]
    crossed = [(i, core - 1 - i) for i in range(core)]

    def onward(value):
        return lax.ppermute(value, "heads", ring)

    def across(value):
        return lax.ppermute(value, "core", crossed)

    def around(value):
        values = [value]
        for _ in range(n_heads - 1):
            values.append(onward(values[-1]))
        return values

    def both(value):
        return [value] if core == 1 else [value, across(value)]

    def joined(parts):
        total = parts[0].astype(jnp.float32)
        if core > 1:
            total = total + across(parts[1]).astype(jnp.float32)
        return total

    def first_phase(parts):
        return (paired(parts[1], 1), paired(parts[2], 2))

    def second_phase(parts, got):
        own, _, _, first_keep, second_keep = parts
        first_next = (first_keep + got[0][1].astype(jnp.float32)).astype(jnp.bfloat16)
        second_next = (second_keep + got[1][1].astype(jnp.float32)).astype(jnp.bfloat16)
        return (paired(first_next, 2), paired(second_next, 1))

    def finished(parts, got, last):
        own = parts[0]
        half = own.shape[0] // 2
        first = own[:half] + got[0][0].astype(jnp.float32) + last[0].astype(jnp.float32)
        second = own[half:] + got[1][0].astype(jnp.float32) + last[1].astype(jnp.float32)
        return jnp.concatenate([first, second], 0)

    def after(value, *others):
        return lax.optimization_barrier((value, others))[0]

    def paired(value, other):
        return lax.ppermute(value, "chip", [(i, i ^ other) for i in range(chip)])

    def spread_rows(cut):
        part = lax.psum_scatter(
            cut.reshape(-1, cut.shape[3]), ("chip", "core"), scatter_dimension=0, tiled=True
        )
        return part.reshape(cut.shape[1:])

    def local(
        tokens,
        cotangent,
        lengths,
        routes,
        attention_input_weight,
        attn_out,
        router,
        gain_attn,
        gain_ffn,
        expert_in,
        expert_out,
    ):
        slots, span, width = tokens.shape
        token_rows = slots * span
        length = span * n_heads
        rank = lax.axis_index("heads")
        qkv_width = attention_input_weight.shape[1]
        own_columns = groups_local * GROUP
        rings = around(tokens)
        small = jnp.concatenate(
            [
                attention_input_weight,
                attn_out,
                router,
                gain_attn[:, None],
                gain_ffn[:, None],
                jnp.zeros((router.shape[0], TAIL - E - 2), jnp.bfloat16),
            ],
            1,
        )
        column = lax.all_to_all(
            jnp.broadcast_to(after(small, rings[1])[None], (n_heads,) + small.shape),
            "heads",
            split_axis=0,
            concat_axis=0,
            tiled=True,
        )

        own_out = lax.all_gather(expert_out, "chip", axis=0, tiled=True).reshape(n_local, D, FFE)

        def plane(value):
            value = lax.all_gather(value, ("chip", "core"), axis=1, tiled=True)
            return value.reshape(-1, value.shape[2])

        first = plane(
            after(
                jnp.concatenate(
                    [
                        lax.dynamic_slice_in_dim(column, rank * own_columns, own_columns, 2),
                        column[:, :, qkv_width + D :],
                    ],
                    2,
                ),
                own_out,
                rings[2],
            )
        )
        w_own = first
        gain_one = first[:, own_columns + E].astype(jnp.float32)
        w_proj = plane(column[:, :, qkv_width:])
        w_router = w_proj[:, D : D + E]
        gain_two = w_proj[:, D + E + 1].astype(jnp.float32)
        w_proj = w_proj[:, :D]
        own_grads = cotangent.reshape(token_rows, width)
        own_in = lax.all_gather(after(expert_in, first, rings[-1]), "chip", axis=0, tiled=True).reshape(
            n_local, D, 2 * FFE
        )

        positions = rank * span + jnp.arange(span, dtype=jnp.int32)
        valid = (positions[None, :] < lengths[:, None]).reshape(token_rows)
        valid_float = valid.astype(jnp.float32)[:, None]
        route_rows = routes.reshape(token_rows, TOPK)
        routed = jnp.any(
            route_rows[:, :, None] == jnp.arange(E, dtype=jnp.int32)[None, None, :], 1
        )
        live = (routed & valid[:, None]).astype(jnp.bfloat16)
        earlier = (
            jnp.arange(token_rows)[:, None] > jnp.arange(token_rows)[None, :]
        ).astype(jnp.bfloat16)
        count = jnp.dot(earlier, live, preferred_element_type=jnp.float32)
        kept = (live > 0) & (count < CAP)
        code = jnp.where(kept, count, -1.0).astype(jnp.bfloat16)
        ids = (rank * n_local + jnp.arange(n_local, dtype=jnp.int32)) * core + lax.axis_index("core")

        tables = rotary_tables(length)
        places = (rank + n_heads - jnp.arange(n_heads, dtype=jnp.int32)) % n_heads
        packed, context_heads, lse, normed_whole = attention_forward(
            rings, places, gain_one[None, :], w_own, tables, groups_local
        )
        grad_ring = [own_grads, onward(after(own_grads, rings[-1]))]
        context_heads = after(context_heads, grad_ring[1])
        context = lax.all_to_all(context_heads, "heads", split_axis=0, concat_axis=0, tiled=True)
        grad_ring.append(onward(after(grad_ring[1], context)))
        heads_width = groups_local * PAIR
        context = context.reshape(n_heads, token_rows, heads_width)

        state = tokens.astype(jnp.float32).reshape(token_rows, width)
        mid_state = state
        for h in range(n_heads):
            mid_state = mid_state + dot_nn(
                context[h], w_proj[h * heads_width : (h + 1) * heads_width]
            )
        factor_two = norm_factor(mid_state)
        normed_ffn = (mid_state * factor_two * gain_two).astype(jnp.bfloat16)
        logits = jnp.dot(normed_ffn, w_router, preferred_element_type=jnp.float32)
        highest = jnp.max(jnp.where(routed, logits, NEGATIVE), -1, keepdims=True)
        weights = jnp.where(routed, jnp.exp(jnp.where(routed, logits - highest, 0.0)), 0.0)
        gates = weights / jnp.sum(weights, -1, keepdims=True)
        gates_high = lax.reduce_precision(gates, 8, 7)
        payload = jnp.concatenate(
            [
                normed_ffn,
                code,
                gates_high.astype(jnp.bfloat16),
                (gates - gates_high).astype(jnp.bfloat16),
                jnp.zeros((token_rows, TAIL - 3 * E), jnp.bfloat16),
            ],
            1,
        )
        while len(grad_ring) < n_heads:
            grad_ring.append(onward(grad_ring[-1]))
        payloads = around(after(payload, grad_ring[-1]))
        sequence = list(range(1, n_heads - 1)) + [0, n_heads - 1]
        saved, moving = (), None
        backs, mixes = {}, {}
        for step in sequence:
            xs, gs = both(payloads[step]), both(grad_ring[step])
            if moving is not None and step:
                xs[0] = after(xs[0], moving)
            saved, back, mix = experts(
                step, n_heads, ids, xs, gs, own_in, own_out, tuple(saved)
            )
            backs[step], mixes[step] = back, mix
            if step:
                total = joined(back)
                if moving is not None:
                    total = total + onward(moving).astype(jnp.float32)
                moving = total.astype(jnp.bfloat16)
        buffer, grad_outputs, hidden, grad_pre = [
            value.reshape(n_local, group_size * CAP, value.shape[3]) for value in saved
        ]
        grad_pre = after(grad_pre, moving)
        last_back = onward(moving)
        if expert_in.shape[0] == D:
            order = lax.axis_index("chip") ^ jnp.arange(chip, dtype=jnp.int32)
            parts_in = expert_grads(order, buffer, grad_pre)
        else:
            parts_in = [plain_grads(buffer, grad_pre)]
        w_qkv = plane(after(column[:, :, :qkv_width], context))
        mix_moving = joined(mixes[1]).astype(jnp.bfloat16)
        mix_received = onward(after(mix_moving, last_back))
        back_sum = joined(backs[0]) + after(last_back, w_qkv, *parts_in).astype(jnp.float32)

        grad_gates = back_sum[:, width : width + E] + back_sum[:, width + E : width + 2 * E]
        grad_logits = gates * (grad_gates - jnp.sum(gates * grad_gates, -1, keepdims=True))
        grad_logits = grad_logits * valid_float
        grad_out = cotangent.astype(jnp.float32).reshape(token_rows, width) * valid_float
        grad_normed_ffn = back_sum[:, :width] + jnp.dot(
            grad_logits, w_router.astype(jnp.float32).T, precision=TOP_PRECISION
        )
        grad_mid_norm, gain_two_term = norm_back(grad_normed_ffn, mid_state, factor_two, gain_two)
        grad_mid = grad_out + grad_mid_norm
        grad_mid_low = grad_mid.astype(jnp.bfloat16)
        context_gradient = jnp.stack(
            [
                dot_nt(grad_mid_low, w_proj[h * heads_width : (h + 1) * heads_width])
                for h in range(n_heads)
            ]
        ).astype(jnp.bfloat16)
        context_gradient = after(context_gradient, mix_received)
        hidden = after(hidden, context_gradient)
        if len(parts_in) > 1:
            parts_out = expert_grads(order, grad_outputs, hidden)
        else:
            parts_out = [plain_grads(grad_outputs, hidden)]
        near, near_out = (), ()
        if len(parts_in) > 1:
            near, near_out = first_phase(parts_in), first_phase(parts_out)
        grad_context_heads = lax.all_to_all(
            context_gradient.reshape(n_heads, slots, span, heads_width),
            "heads",
            split_axis=0,
            concat_axis=0,
            tiled=True,
        )
        logits_padded = jnp.concatenate(
            [grad_logits, jnp.zeros((token_rows, TAIL - E), jnp.float32)], 1
        )
        second = cut_rows(
            jnp.concatenate([context[h] for h in range(n_heads)], 1),
            after(grad_mid_low, context_gradient, *near),
            n_heads,
            chip * core,
            (normed_ffn, logits_padded, gain_two_term[:, None]),
        )
        grad_context_heads = after(grad_context_heads, second)
        second = spread_rows(second)

        for chunk in range(2, n_heads):
            mix_moving = (joined(mixes[chunk]) + mix_received.astype(jnp.float32)).astype(
                jnp.bfloat16
            )
            if chunk == 2:
                grad_before, cut = attention_backward(
                    packed,
                    lse,
                    after(grad_context_heads, mix_moving, *parts_out),
                    normed_whole,
                    tables,
                    groups_local,
                    chip * core,
                )
            if chunk < n_heads - 1:
                mix_received = onward(after(mix_moving, grad_context_heads))
        grad_mine = lax.all_to_all(
            after(grad_before, mix_received, *near_out), "heads", split_axis=0, concat_axis=0, tiled=True
        ).reshape(n_heads, token_rows, own_columns)
        qkv_part = spread_rows(after(cut, second))
        if near:
            far_in, far_out = second_phase(parts_in, near), second_phase(parts_out, near_out)
        grad_normed_attn = dot_nt(grad_mine[0], w_qkv[:, :own_columns])
        for h in range(1, n_heads):
            grad_normed_attn = grad_normed_attn + dot_nt(
                grad_mine[h], w_qkv[:, h * own_columns : (h + 1) * own_columns]
            )
        grad_state_norm, _ = norm_back(grad_normed_attn, state, norm_factor(state), gain_one)
        grad_tokens = (grad_mid + grad_state_norm).astype(jnp.bfloat16).reshape(tokens.shape)
        if near:
            grad_expert_in = finished(parts_in, near, after(far_in, grad_tokens))
            grad_expert_out = finished(parts_out, near_out, after(far_out, grad_tokens))
        else:
            grad_expert_in, grad_expert_out = [
                lax.psum_scatter(
                    value[0].reshape(-1, value[0].shape[2]),
                    "chip",
                    scatter_dimension=0,
                    tiled=True,
                ).astype(jnp.float32)
                for value in (parts_in, parts_out)
            ]
        mixture = joined(mixes[0]) + onward(after(mix_moving, grad_mine)).astype(jnp.float32)
        mixed = (valid_float * (mid_state + mixture)).astype(jnp.bfloat16)

        last = lax.all_to_all(
            after(jnp.concatenate([second, qkv_part], 2), grad_mine),
            "heads",
            split_axis=0,
            concat_axis=0,
            tiled=True,
        ).astype(jnp.float32)
        second = jnp.sum(last[:, :, : D + TAIL], 0)
        grad_attn_out = second[:, :D]
        grad_router = second[:, D : D + E]
        grad_gain_ffn = second[:, D + E]
        grad_attn_in = jnp.concatenate([last[h, :, D + TAIL :] for h in range(n_heads)], 1)
        grad_gain_attn = jnp.sum(
            grad_attn_in * attention_input_weight.astype(jnp.float32), -1
        ) / gain_attn.astype(jnp.float32)
        return (
            mixed.reshape(tokens.shape),
            grad_tokens,
            grad_attn_in,
            grad_attn_out,
            grad_router,
            grad_gain_attn,
            grad_gain_ffn,
            grad_expert_in,
            grad_expert_out,
        )

    return local


def solution(mesh):
    n_heads, n_shard = mesh.shape["heads"], mesh.shape["shard"]
    core = 2 if n_heads * n_shard == E else 1
    chip = n_shard // core
    split = jax.sharding.Mesh(
        mesh.devices.reshape(n_heads, chip, core), ("heads", "chip", "core")
    )
    shard = ("chip", "core")
    everyone = ("heads", "chip", "core")
    token_spec = P(shard, "heads", None)
    rows = P(everyone, None)
    in_specs = (
        token_spec,
        token_spec,
        P(shard),
        token_spec,
        rows,
        rows,
        rows,
        P(everyone),
        P(everyone),
        rows,
        rows,
    )
    out_specs = (token_spec, token_spec, rows, rows, rows, P(everyone), P(everyone), rows, rows)
    return jax.shard_map(
        make_local(n_heads, chip, core),
        mesh=split,
        in_specs=in_specs,
        out_specs=out_specs,
        check_vma=False,
    )
```

```python
import functools
import math

import jax
import jax.numpy as jnp
import numpy as np
from jax import lax
from jax.experimental import pallas as pl
from jax.experimental.pallas import tpu as pltpu
from jax.sharding import PartitionSpec as P

D = 1024
QUERY_HEADS = 16
KEY_VALUE_HEADS = 8
HEAD_SIZE = 64
E = 32
FFE = 512
TOPK = 8
QUERIES_PER_KV = 2
CAP = 160
GROUP = (QUERIES_PER_KV + 2) * HEAD_SIZE
PAIR = QUERIES_PER_KV * HEAD_SIZE
TAIL = 128
BLOCK = 256
VMEM_BYTES = 56 * 2**20


EPSILON = 1e-06
THETA_BASE = 10000.0
NEGATIVE = -1e30
TOP_PRECISION = lax.Precision.HIGHEST
SCALE = 1.0 / math.sqrt(HEAD_SIZE)
SHORT = pl.CostEstimate(flops=1024, bytes_accessed=1024, transcendentals=0)


def dot_nn(left, right):
    return jnp.dot(left, right, preferred_element_type=jnp.float32)


def dot_nt(left, right):
    return lax.dot_general(
        left, right, (((1,), (1,)), ((), ())), preferred_element_type=jnp.float32
    )


def dot_tn(left, right):
    return lax.dot_general(
        left, right, (((0,), (0,)), ((), ())), preferred_element_type=jnp.float32
    )


def norm_factor(value):
    return lax.rsqrt(jnp.mean(value * value, -1, keepdims=True) + EPSILON)


def norm_back(grad_in, value, factor, gain):
    normalized_rows = value * factor
    scaled = grad_in * gain
    gain_term = jnp.sum(grad_in * normalized_rows, 0)
    grad_value = factor * (
        scaled - normalized_rows * jnp.mean(scaled * normalized_rows, -1, keepdims=True)
    )
    return (grad_value, gain_term)


def rotary_tables(length):
    half_size = HEAD_SIZE // 2
    freqs = THETA_BASE ** (-2.0 * np.arange(half_size) / HEAD_SIZE)
    angles = np.arange(length)[:, None] * freqs[None, :]
    cosine, sine = np.cos(angles), np.sin(angles)
    one = np.ones((length, HEAD_SIZE))
    own = np.concatenate([cosine, cosine] * (QUERIES_PER_KV + 1) + [one], 1)
    other = np.concatenate([-sine, sine] * (QUERIES_PER_KV + 1) + [0.0 * one], 1)
    return (jnp.asarray(own, jnp.float32), jnp.asarray(other, jnp.float32))


def partner(values):
    width = values.shape[1]
    lane = lax.broadcasted_iota(jnp.int32, values.shape, 1)
    half_size = HEAD_SIZE // 2
    return jnp.where(
        lax.rem(lane, HEAD_SIZE) < half_size,
        pltpu.roll(values, width - half_size, 1),
        pltpu.roll(values, half_size, 1),
    )


def stack_queries(block):
    values = block.astype(jnp.float32) * SCALE
    low = lax.broadcasted_iota(jnp.int32, values.shape, 1) < HEAD_SIZE
    first = jnp.where(low, values, 0.0)
    second = jnp.where(low, pltpu.roll(values, HEAD_SIZE, 1), 0.0)
    return jnp.concatenate([first, second], 0).astype(jnp.bfloat16)


def stack_grads(block):
    values = block.astype(jnp.float32)
    low = lax.broadcasted_iota(jnp.int32, values.shape, 1) < HEAD_SIZE
    first = jnp.where(low, 0.0, pltpu.roll(values, HEAD_SIZE, 1))
    second = jnp.where(low, 0.0, values)
    return jnp.concatenate([first, second], 0).astype(jnp.bfloat16)


def attention_forward_kernel(pieces, place_ref, *refs):
    xs, refs = refs[:pieces], refs[pieces:]
    gain_ref, w_ref, own_ref, other_ref = refs[:4]
    packed_ref, context_ref, lse_ref, normed_ref = refs[4:]
    span = xs[0].shape[1]
    length = pieces * span

    @pl.when(pl.program_id(1) == 0)
    def _():
        for step in range(pieces):
            at = place_ref[step]
            for start in range(0, span, BLOCK):
                value = xs[step][0, start : start + BLOCK, :].astype(jnp.float32)
                normed_ref[at, 0, start : start + BLOCK, :] = (
                    value * norm_factor(value) * gain_ref[...]
                ).astype(jnp.bfloat16)

    for start in range(0, length, BLOCK):
        rows = slice(start, start + BLOCK)
        before = dot_nn(
            normed_ref[start // span, 0, start % span : start % span + BLOCK, :], w_ref[...]
        )
        packed_ref[0, rows, :] = (
            before * own_ref[rows, :] + partner(before) * other_ref[rows, :]
        ).astype(jnp.bfloat16)

    low = lax.broadcasted_iota(jnp.int32, (BLOCK, PAIR), 1) < HEAD_SIZE
    lane_zero = lax.broadcasted_iota(jnp.int32, (BLOCK, PAIR), 1) == 0
    query_row = lax.rem(lax.broadcasted_iota(jnp.int32, (2 * BLOCK, BLOCK), 0), BLOCK)
    allowed = lax.broadcasted_iota(jnp.int32, (2 * BLOCK, BLOCK), 1) <= query_row
    for start in range(0, length, BLOCK):
        rows = slice(start, start + BLOCK)
        queries = stack_queries(packed_ref[0, rows, :PAIR])
        inside = packed_ref[0, rows, PAIR:]
        scores_inside = jnp.where(allowed, dot_nt(queries, inside), NEGATIVE)
        highest = jnp.max(scores_inside, 1, keepdims=True)
        if start:
            before_keys = packed_ref[0, :start, PAIR:]
            scores_before = dot_nt(queries, before_keys)
            highest = jnp.maximum(highest, jnp.max(scores_before, 1, keepdims=True))
        weights = jnp.exp(scores_inside - highest)
        total = jnp.sum(weights, 1, keepdims=True)
        result = dot_nn(weights.astype(jnp.bfloat16), inside)
        if start:
            weights = jnp.exp(scores_before - highest)
            total = total + jnp.sum(weights, 1, keepdims=True)
            result = result + dot_nn(weights.astype(jnp.bfloat16), before_keys)
        result = result / total
        context_ref[start // span, 0, start % span : start % span + BLOCK, :] = jnp.where(
            low, pltpu.roll(result[:BLOCK], HEAD_SIZE, 1), result[BLOCK:]
        ).astype(jnp.bfloat16)
        log_total = highest + jnp.log(total)
        columns = jnp.where(lane_zero, log_total[:BLOCK], log_total[BLOCK:])
        lse_ref[0, 0, :, rows] = columns.T[:8, :]


def attention_forward(xs, places, gain, weights, tables, groups_local):
    pieces = len(xs)
    slots, span, width = xs[0].shape
    length = pieces * span
    bf16, f32 = jnp.bfloat16, jnp.float32
    return pl.pallas_call(
        functools.partial(attention_forward_kernel, pieces),
        grid_spec=pltpu.PrefetchScalarGridSpec(
            num_scalar_prefetch=1,
            grid=(slots, groups_local),
            in_specs=[pl.BlockSpec((1, span, width), lambda s, g, place: (s, 0, 0))] * pieces
            + [
                pl.BlockSpec((1, width), lambda s, g, place: (0, 0)),
                pl.BlockSpec((width, GROUP), lambda s, g, place: (0, g)),
                pl.BlockSpec((length, GROUP), lambda s, g, place: (0, 0)),
                pl.BlockSpec((length, GROUP), lambda s, g, place: (0, 0)),
            ],
            out_specs=[
                pl.BlockSpec((1, length, GROUP), lambda s, g, place: (s, 0, g)),
                pl.BlockSpec((pieces, 1, span, PAIR), lambda s, g, place: (0, s, 0, g)),
                pl.BlockSpec((1, 1, 8, length), lambda s, g, place: (s, g, 0, 0)),
                pl.BlockSpec((pieces, 1, span, width), lambda s, g, place: (0, s, 0, 0)),
            ],
        ),
        out_shape=[
            jax.ShapeDtypeStruct((slots, length, groups_local * GROUP), bf16),
            jax.ShapeDtypeStruct((pieces, slots, span, groups_local * PAIR), bf16),
            jax.ShapeDtypeStruct((slots, groups_local, 8, length), f32),
            jax.ShapeDtypeStruct((pieces, slots, span, width), bf16),
        ],
        compiler_params=pltpu.CompilerParams(vmem_limit_bytes=VMEM_BYTES),
        cost_estimate=SHORT,
        name="attention_forward",
    )(places, *xs, gain, weights, *tables)


def attention_backward_kernel(
    packed_ref,
    lse_ref,
    grad_ref,
    normed_ref,
    own_ref,
    other_ref,
    filled_ref,
    out_ref,
    cut_ref,
    total_ref,
    product_ref,
):
    length, span = packed_ref.shape[1], grad_ref.shape[2]
    low = lax.broadcasted_iota(jnp.int32, (BLOCK, PAIR), 1) < HEAD_SIZE
    query_lane = lax.rem(lax.broadcasted_iota(jnp.int32, (BLOCK, 2 * BLOCK), 1), BLOCK)
    allowed = lax.broadcasted_iota(jnp.int32, (BLOCK, 2 * BLOCK), 0) <= query_lane
    total_ref[...] = jnp.zeros_like(total_ref)

    def unturn(values, lanes, rows):
        values = values.astype(jnp.bfloat16).astype(jnp.float32)
        return (
            values * own_ref[rows, lanes] - partner(values) * other_ref[rows, lanes]
        ).astype(jnp.bfloat16)

    for start in range(0, length, BLOCK):
        rows = slice(start, start + BLOCK)
        queries = stack_queries(packed_ref[0, rows, :PAIR])
        inner = slice(start % span, start % span + BLOCK)
        grads = stack_grads(grad_ref[start // span, 0, inner, :])
        log_total = jnp.concatenate([lse_ref[0, 0, 0:1, rows], lse_ref[0, 0, 1:2, rows]], 1)

        def piece(keys):
            scores = dot_nt(keys, queries)
            probs = jnp.exp(scores - log_total)
            return (probs, dot_nt(keys, grads))

        inside = packed_ref[0, rows, PAIR:]
        probs_inside, grad_inside = piece(inside)
        probs_inside = jnp.where(allowed, probs_inside, 0.0)
        delta = jnp.sum(probs_inside * grad_inside, 0, keepdims=True)
        if start:
            before = packed_ref[0, :start, PAIR:]
            probs_before, grad_before = piece(before)
            delta = delta + jnp.sum(probs_before * grad_before, 0, keepdims=True)
        score_grads = (probs_inside * (grad_inside - delta)).astype(jnp.bfloat16)
        total_ref[rows, :] += dot_nn(probs_inside.astype(jnp.bfloat16), grads) + dot_nn(
            score_grads, queries
        )
        grad_query = dot_tn(score_grads, inside)
        if start:
            score_grads = (probs_before * (grad_before - delta)).astype(jnp.bfloat16)
            total_ref[:start, :] += dot_nn(probs_before.astype(jnp.bfloat16), grads) + dot_nn(
                score_grads, queries
            )
            grad_query = grad_query + dot_tn(score_grads, before)
        grad_query = (
            jnp.where(low, grad_query[:BLOCK], pltpu.roll(grad_query[BLOCK:], HEAD_SIZE, 1)) * SCALE
        )
        out_ref[start // span, 0, inner, :PAIR] = unturn(grad_query, slice(0, PAIR), rows)
    for start in range(0, length, BLOCK):
        rows = slice(start, start + BLOCK)
        inner = slice(start % span, start % span + BLOCK)
        out_ref[start // span, 0, inner, PAIR:] = unturn(
            total_ref[rows, :], slice(PAIR, GROUP), rows
        )

    @pl.when(pl.program_id(1) == 0)
    def _():
        product_ref[...] = jnp.zeros_like(product_ref)

    for at in range(length // span):
        product_ref[...] += dot_tn(normed_ref[at, 0], out_ref[at, 0])

    @pl.when(pl.program_id(1) == pl.num_programs(1) - 1)
    def _():
        parts, heads, each = cut_ref.shape[:3]
        for h in range(heads):
            block = product_ref[h * parts * each : (h + 1) * parts * each, :]
            cut_ref[:, h] = block.reshape(parts, each, GROUP).astype(cut_ref.dtype)


def attention_backward(packed, lse, grads, normed, tables, groups_local, cut):
    slots, length = packed.shape[:2]
    pieces, span, width = grads.shape[0], grads.shape[2], normed.shape[3]
    parts, _, each, _ = cut.shape
    return pl.pallas_call(
        attention_backward_kernel,
        grid=(groups_local, slots),
        in_specs=[
            pl.BlockSpec((1, length, GROUP), lambda g, s: (s, 0, g)),
            pl.BlockSpec((1, 1, 8, length), lambda g, s: (s, g, 0, 0)),
            pl.BlockSpec((pieces, 1, span, PAIR), lambda g, s: (0, s, 0, g)),
            pl.BlockSpec((pieces, 1, span, width), lambda g, s: (0, s, 0, 0)),
            pl.BlockSpec((length, GROUP), lambda g, s: (0, 0)),
            pl.BlockSpec((length, GROUP), lambda g, s: (0, 0)),
            pl.BlockSpec(memory_space=pl.ANY),
        ],
        out_specs=[
            pl.BlockSpec((pieces, 1, span, GROUP), lambda g, s: (0, s, 0, g)),
            pl.BlockSpec((parts, pieces, each, GROUP), lambda g, s: (0, 0, 0, g)),
        ],
        out_shape=[
            jax.ShapeDtypeStruct((pieces, slots, span, packed.shape[2]), jnp.bfloat16),
            jax.ShapeDtypeStruct(cut.shape, cut.dtype),
        ],
        input_output_aliases={6: 1},
        scratch_shapes=[
            pltpu.VMEM((length, PAIR), jnp.float32),
            pltpu.VMEM((width, GROUP), jnp.float32),
        ],
        compiler_params=pltpu.CompilerParams(vmem_limit_bytes=VMEM_BYTES),
        cost_estimate=SHORT,
        name="attention_backward",
    )(packed, lse, grads, normed, *tables, cut)


def expert_kernel(sources, n_local, kept, ids_ref, *refs):
    xs, refs = refs[:sources], refs[sources:]
    gs, refs = refs[:sources], refs[sources:]
    w_in_ref, w_out_ref = refs[:2]
    refs = refs[2 + kept :]
    buffer_ref, grad_out_ref, hidden_ref, grad_pre_ref = refs[:4]
    backs, mixes = refs[4 : 4 + sources], refs[4 + sources : 4 + 2 * sources]
    table, picks, mix_rows, back_rows, gate_back = refs[4 + 2 * sources :]
    step = pl.program_id(0)
    expert = ids_ref[step]
    tokens = xs[0].shape[0]
    here = pl.ds(pl.multiple_of(step * CAP, 16), CAP)

    @pl.when(step == 0)
    def _():
        for s in range(sources):
            table[s] = xs[s][:, D:].astype(jnp.float32).T
            gate_back[s] = jnp.zeros((TAIL, tokens), jnp.float32)

    place = lax.broadcasted_iota(jnp.int32, (CAP, tokens), 0).astype(jnp.float32)
    hits, gate_rows, grad_rows = [], [], []
    for s in range(sources):
        code = table[s, pl.ds(expert, 1), :]
        gate = table[s, pl.ds(expert + E, 1), :] + table[s, pl.ds(expert + 2 * E, 1), :]
        hit = code == place
        pick = jnp.where(hit, 1.0, 0.0).astype(jnp.bfloat16)
        picks[s, here, :] = pick
        hits.append(hit)
        gate_rows.append(jnp.sum(jnp.where(hit, gate, 0.0), 1, keepdims=True))
        buffer_ref[0, 0, s * CAP : (s + 1) * CAP, :] = dot_nn(pick, xs[s][:, :D]).astype(
            jnp.bfloat16
        )
        grad_rows.append(dot_nn(pick, gs[s][...]))
    gate_row = jnp.concatenate(gate_rows, 0)
    grad_row = jnp.concatenate(grad_rows, 0)
    grad_out_ref[0, 0] = (gate_row * grad_row).astype(jnp.bfloat16)
    pre = dot_nn(buffer_ref[0, 0], w_in_ref[0])
    grad_plain = dot_nn(grad_row.astype(jnp.bfloat16), w_out_ref[0])
    gate_pre, up_pre = pre[:, :FFE], pre[:, FFE:]
    sigmoid_gate = 1.0 / (1.0 + jnp.exp(-gate_pre))
    silu_gate = gate_pre * sigmoid_gate
    hidden = (silu_gate * up_pre).astype(jnp.bfloat16)
    hidden_ref[0, 0] = hidden
    gate_grad = jnp.sum(grad_plain * hidden.astype(jnp.float32), 1, keepdims=True)
    grad_hidden = gate_row * grad_plain
    grad_pre_ref[0, 0, :, :FFE] = (
        grad_hidden * up_pre * sigmoid_gate * (1.0 + gate_pre * (1.0 - sigmoid_gate))
    ).astype(jnp.bfloat16)
    grad_pre_ref[0, 0, :, FFE:] = (grad_hidden * silu_gate).astype(jnp.bfloat16)
    outputs = (gate_row * dot_nt(hidden, w_out_ref[0])).astype(jnp.bfloat16)
    back = dot_nt(grad_pre_ref[0, 0], w_in_ref[0]).astype(jnp.bfloat16)
    for s in range(sources):
        part = slice(s * CAP, (s + 1) * CAP)
        mix_rows[s, here, :] = outputs[part]
        back_rows[s, here, :] = back[part]
        row = jnp.sum(jnp.where(hits[s], gate_grad[part], 0.0), 0, keepdims=True)
        high = row.astype(jnp.bfloat16).astype(jnp.float32)
        gate_back[s, pl.ds(expert, 1), :] = high
        gate_back[s, pl.ds(expert + E, 1), :] = row - high

    @pl.when(step == n_local - 1)
    def _():
        for s in range(sources):
            backs[s][:, :D] = dot_tn(picks[s], back_rows[s]).astype(jnp.bfloat16)
            backs[s][:, D:] = gate_back[s].T.astype(jnp.bfloat16)
            mixes[s][...] = dot_tn(picks[s], mix_rows[s]).astype(jnp.bfloat16)


def experts(chunk, chunks, ids, xs, gs, own_in, own_out, kept):
    sources, n_local, tokens = len(xs), own_in.shape[0], xs[0].shape[0]
    rows = sources * CAP
    bf16, f32 = jnp.bfloat16, jnp.float32
    fixed = lambda i, ids: (0, 0)
    saved = lambda columns: pl.BlockSpec((1, 1, rows, columns), lambda i, ids: (i, chunk, 0, 0))
    widths = (D, D, FFE, 2 * FFE)
    in_specs = (
        [pl.BlockSpec((tokens, D + TAIL), fixed)] * sources
        + [pl.BlockSpec((tokens, D), fixed)] * sources
        + [
            pl.BlockSpec((1, D, 2 * FFE), lambda i, ids: (i, 0, 0)),
            pl.BlockSpec((1, D, FFE), lambda i, ids: (i, 0, 0)),
        ]
        + [pl.BlockSpec(memory_space=pl.ANY)] * len(kept)
    )
    results = pl.pallas_call(
        functools.partial(expert_kernel, sources, n_local, len(kept)),
        grid_spec=pltpu.PrefetchScalarGridSpec(
            num_scalar_prefetch=1,
            grid=(n_local,),
            in_specs=in_specs,
            out_specs=[saved(columns) for columns in widths]
            + [pl.BlockSpec((tokens, D + TAIL), fixed)] * sources
            + [pl.BlockSpec((tokens, D), fixed)] * sources,
            scratch_shapes=[
                pltpu.VMEM((sources, TAIL, tokens), f32),
                pltpu.VMEM((sources, n_local * CAP, tokens), bf16),
                pltpu.VMEM((sources, n_local * CAP, D), bf16),
                pltpu.VMEM((sources, n_local * CAP, D), bf16),
                pltpu.VMEM((sources, TAIL, tokens), f32),
            ],
        ),
        out_shape=[
            jax.ShapeDtypeStruct((n_local, chunks, rows, columns), bf16) for columns in widths
        ]
        + [jax.ShapeDtypeStruct((tokens, D + TAIL), bf16)] * sources
        + [jax.ShapeDtypeStruct((tokens, D), bf16)] * sources,
        input_output_aliases={3 + 2 * sources + i: i for i in range(len(kept))},
        compiler_params=pltpu.CompilerParams(vmem_limit_bytes=VMEM_BYTES),
        cost_estimate=pl.CostEstimate(
            flops=n_local * rows * D * (4 * tokens + 9 * FFE),
            bytes_accessed=n_local * D * FFE * 6 + tokens * sources * D * 8,
            transcendentals=0,
        ),
        name="experts",
    )(ids, *xs, *gs, own_in, own_out, *kept)
    return results[:4], results[4 : 4 + sources], results[4 + sources :]


def cut_rows_kernel(offset, left_ref, right_ref, normed_ref, logits_ref, gain_ref, out_ref):
    parts, rows = out_ref.shape[0], out_ref.shape[2]
    width = right_ref.shape[1]
    product = dot_tn(left_ref[...], right_ref[...])
    out_ref[:, 0, :, :offset] = jnp.zeros((parts, rows, offset), out_ref.dtype)
    out_ref[:, 0, :, offset : offset + width] = product.reshape(parts, rows, width).astype(
        out_ref.dtype
    )
    rest = logits_ref[...]
    tail = jnp.zeros((left_ref.shape[1], TAIL), jnp.float32)
    for _ in range(3):
        term = rest.astype(jnp.bfloat16)
        rest = rest - term.astype(jnp.float32)
        tail = tail + dot_tn(normed_ref[...], term)
    lane = lax.broadcasted_iota(jnp.int32, tail.shape, 1)
    tail = jnp.where(lane == E, gain_ref[...], tail)
    out_ref[:, 0, :, offset + width :] = tail.reshape(parts, rows, TAIL).astype(out_ref.dtype)


def cut_rows(left, right, normed, logits, gain_term, parts, offset):
    n_heads, depth, each = left.shape
    width = right.shape[1]
    columns = offset + width + TAIL
    return pl.pallas_call(
        functools.partial(cut_rows_kernel, offset),
        grid=(n_heads,),
        in_specs=[
            pl.BlockSpec((pl.squeezed, depth, each), lambda h: (h, 0, 0)),
            pl.BlockSpec((depth, width), lambda h: (0, 0)),
            pl.BlockSpec((depth, each), lambda h: (0, h)),
            pl.BlockSpec((depth, TAIL), lambda h: (0, 0)),
            pl.BlockSpec((each, 1), lambda h: (h, 0)),
        ],
        out_specs=pl.BlockSpec((parts, 1, each // parts, columns), lambda h: (0, h, 0, 0)),
        out_shape=jax.ShapeDtypeStruct(
            (parts, n_heads, each // parts, columns),
            jnp.bfloat16 if each // parts % 16 == 0 else jnp.float32,
        ),
        compiler_params=pltpu.CompilerParams(vmem_limit_bytes=VMEM_BYTES),
        cost_estimate=pl.CostEstimate(
            flops=4 * depth * each * n_heads * columns,
            bytes_accessed=depth * (each * n_heads + width) * 2 + each * n_heads * columns * 4,
            transcendentals=0,
        ),
        name="cut_rows",
    )(left, right, normed, logits, gain_term)


def expert_grads_kernel(
    order_ref, left_ref, right_ref, own_ref, first_send, second_send, first_keep, second_keep
):
    product = dot_tn(left_ref[0], right_ref[0])
    step = pl.program_id(0)
    half = product.shape[0] // 2
    low = jnp.bfloat16

    @pl.when(step == 0)
    def _():
        own_ref[...] = product

    @pl.when(step == 1)
    def _():
        first_send[0] = product[:half].astype(low)
        second_keep[...] = product[half:]

    @pl.when(step == 2)
    def _():
        first_keep[...] = product[:half]
        second_send[0] = product[half:].astype(low)

    @pl.when(step == 3)
    def _():
        first_send[1] = product[:half].astype(low)
        second_send[1] = product[half:].astype(low)


def expert_grads(order, left, right):
    count, depth, height = left.shape
    width = right.shape[2]
    half = height // 2
    bf16, f32 = jnp.bfloat16, jnp.float32
    whole, pair, one = (height, width), (2, half, width), (half, width)
    return pl.pallas_call(
        expert_grads_kernel,
        grid_spec=pltpu.PrefetchScalarGridSpec(
            num_scalar_prefetch=1,
            grid=(count,),
            in_specs=[
                pl.BlockSpec((1, depth, height), lambda i, order: (order[i], 0, 0)),
                pl.BlockSpec((1, depth, width), lambda i, order: (order[i], 0, 0)),
            ],
            out_specs=[
                pl.BlockSpec(whole, lambda i, order: (0, 0)),
                pl.BlockSpec(pair, lambda i, order: (0, 0, 0)),
                pl.BlockSpec(pair, lambda i, order: (0, 0, 0)),
                pl.BlockSpec(one, lambda i, order: (0, 0)),
                pl.BlockSpec(one, lambda i, order: (0, 0)),
            ],
        ),
        out_shape=[
            jax.ShapeDtypeStruct(whole, f32),
            jax.ShapeDtypeStruct(pair, bf16),
            jax.ShapeDtypeStruct(pair, bf16),
            jax.ShapeDtypeStruct(one, f32),
            jax.ShapeDtypeStruct(one, f32),
        ],
        compiler_params=pltpu.CompilerParams(vmem_limit_bytes=VMEM_BYTES),
        cost_estimate=SHORT,
        name="expert_grads",
    )(order, left, right)


def plain_grads_kernel(left_ref, right_ref, out_ref):
    out_ref[0] = dot_tn(left_ref[0], right_ref[0]).astype(out_ref.dtype)


def plain_grads(left, right):
    count, depth, height = left.shape
    width = right.shape[2]
    return pl.pallas_call(
        plain_grads_kernel,
        grid=(count,),
        in_specs=[
            pl.BlockSpec((1, depth, height), lambda i: (i, 0, 0)),
            pl.BlockSpec((1, depth, width), lambda i: (i, 0, 0)),
        ],
        out_specs=pl.BlockSpec((1, height, width), lambda i: (i, 0, 0)),
        out_shape=jax.ShapeDtypeStruct((count, height, width), jnp.bfloat16),
        compiler_params=pltpu.CompilerParams(vmem_limit_bytes=VMEM_BYTES),
        cost_estimate=pl.CostEstimate(
            flops=4 * count * depth * height * width,
            bytes_accessed=2 * count * (depth * (height + width) + height * width),
            transcendentals=0,
        ),
        name="plain_grads",
    )(left, right)


def make_local(n_heads, chip, core):
    everyone = ("heads", "chip", "core")
    group_size = n_heads * core
    n_local = E // group_size
    groups_local = KEY_VALUE_HEADS // n_heads
    ring = [(i, (i + 1) % n_heads) for i in range(n_heads)]
    crossed = [(i, core - 1 - i) for i in range(core)]

    def onward(value):
        return lax.ppermute(value, "heads", ring)

    def across(value):
        return lax.ppermute(value, "core", crossed)

    def around(value):
        values = [value]
        for _ in range(n_heads - 1):
            values.append(onward(values[-1]))
        return values

    def both(value):
        return [value] if core == 1 else [value, across(value)]

    def joined(parts):
        total = parts[0].astype(jnp.float32)
        if core > 1:
            total = total + across(parts[1]).astype(jnp.float32)
        return total

    def first_phase(parts):
        return (paired(parts[1], 1), paired(parts[2], 2))

    def second_phase(parts, got):
        own, _, _, first_keep, second_keep = parts
        first_next = (first_keep + got[0][1].astype(jnp.float32)).astype(jnp.bfloat16)
        second_next = (second_keep + got[1][1].astype(jnp.float32)).astype(jnp.bfloat16)
        return (paired(first_next, 2), paired(second_next, 1))

    def finished(parts, got, last):
        own = parts[0]
        half = own.shape[0] // 2
        first = own[:half] + got[0][0].astype(jnp.float32) + last[0].astype(jnp.float32)
        second = own[half:] + got[1][0].astype(jnp.float32) + last[1].astype(jnp.float32)
        return jnp.concatenate([first, second], 0)

    def after(value, *others):
        return lax.optimization_barrier((value, others))[0]

    def paired(value, other):
        return lax.ppermute(value, "chip", [(i, i ^ other) for i in range(chip)])

    def spread_rows(cut):
        part = lax.psum_scatter(
            cut.reshape(-1, cut.shape[3]), ("chip", "core"), scatter_dimension=0, tiled=True
        )
        return part.reshape(cut.shape[1:])

    def local(
        tokens,
        cotangent,
        lengths,
        routes,
        attention_input_weight,
        attn_out,
        router,
        gain_attn,
        gain_ffn,
        expert_in,
        expert_out,
    ):
        slots, span, width = tokens.shape
        token_rows = slots * span
        length = span * n_heads
        rank = lax.axis_index("heads")
        qkv_width = attention_input_weight.shape[1]
        own_columns = groups_local * GROUP
        rings = around(tokens)
        small = jnp.concatenate(
            [
                attention_input_weight,
                attn_out,
                router,
                gain_attn[:, None],
                gain_ffn[:, None],
                jnp.zeros((router.shape[0], TAIL - E - 2), jnp.bfloat16),
            ],
            1,
        )
        column = lax.all_to_all(
            jnp.broadcast_to(after(small, rings[1])[None], (n_heads,) + small.shape),
            "heads",
            split_axis=0,
            concat_axis=0,
            tiled=True,
        )

        own_out = lax.all_gather(expert_out, "chip", axis=0, tiled=True).reshape(n_local, D, FFE)

        def plane(value):
            value = lax.all_gather(value, ("chip", "core"), axis=1, tiled=True)
            return value.reshape(-1, value.shape[2])

        first = plane(
            after(
                jnp.concatenate(
                    [
                        lax.dynamic_slice_in_dim(column, rank * own_columns, own_columns, 2),
                        column[:, :, qkv_width + D :],
                    ],
                    2,
                ),
                own_out,
                rings[2],
            )
        )
        w_own = first
        gain_one = first[:, own_columns + E].astype(jnp.float32)
        w_proj = plane(column[:, :, qkv_width:])
        w_router = w_proj[:, D : D + E]
        gain_two = w_proj[:, D + E + 1].astype(jnp.float32)
        w_proj = w_proj[:, :D]
        own_grads = cotangent.reshape(token_rows, width)
        own_in = lax.all_gather(after(expert_in, first, rings[-1]), "chip", axis=0, tiled=True).reshape(
            n_local, D, 2 * FFE
        )

        positions = rank * span + jnp.arange(span, dtype=jnp.int32)
        valid = (positions[None, :] < lengths[:, None]).reshape(token_rows)
        valid_float = valid.astype(jnp.float32)[:, None]
        route_rows = routes.reshape(token_rows, TOPK)
        routed = jnp.any(
            route_rows[:, :, None] == jnp.arange(E, dtype=jnp.int32)[None, None, :], 1
        )
        live = (routed & valid[:, None]).astype(jnp.bfloat16)
        earlier = (
            jnp.arange(token_rows)[:, None] > jnp.arange(token_rows)[None, :]
        ).astype(jnp.bfloat16)
        count = jnp.dot(earlier, live, preferred_element_type=jnp.float32)
        kept = (live > 0) & (count < CAP)
        code = jnp.where(kept, count, -1.0).astype(jnp.bfloat16)
        ids = (rank * n_local + jnp.arange(n_local, dtype=jnp.int32)) * core + lax.axis_index("core")

        tables = rotary_tables(length)
        places = (rank + n_heads - jnp.arange(n_heads, dtype=jnp.int32)) % n_heads
        packed, context_heads, lse, normed_whole = attention_forward(
            rings, places, gain_one[None, :], w_own, tables, groups_local
        )
        grad_ring = [own_grads, onward(after(own_grads, rings[-1]))]
        context_heads = after(context_heads, grad_ring[1])
        context = lax.all_to_all(context_heads, "heads", split_axis=0, concat_axis=0, tiled=True)
        grad_ring.append(onward(after(grad_ring[1], context)))
        heads_width = groups_local * PAIR
        context = context.reshape(n_heads, token_rows, heads_width)

        state = tokens.astype(jnp.float32).reshape(token_rows, width)
        mid_state = state
        for h in range(n_heads):
            mid_state = mid_state + dot_nn(
                context[h], w_proj[h * heads_width : (h + 1) * heads_width]
            )
        factor_two = norm_factor(mid_state)
        normed_ffn = (mid_state * factor_two * gain_two).astype(jnp.bfloat16)
        logits = jnp.dot(normed_ffn, w_router, preferred_element_type=jnp.float32)
        highest = jnp.max(jnp.where(routed, logits, NEGATIVE), -1, keepdims=True)
        weights = jnp.where(routed, jnp.exp(jnp.where(routed, logits - highest, 0.0)), 0.0)
        gates = weights / jnp.sum(weights, -1, keepdims=True)
        gates_high = lax.reduce_precision(gates, 8, 7)
        payload = jnp.concatenate(
            [
                normed_ffn,
                code,
                gates_high.astype(jnp.bfloat16),
                (gates - gates_high).astype(jnp.bfloat16),
                jnp.zeros((token_rows, TAIL - 3 * E), jnp.bfloat16),
            ],
            1,
        )
        while len(grad_ring) < n_heads:
            grad_ring.append(onward(grad_ring[-1]))
        payloads = around(after(payload, grad_ring[-1]))
        sequence = list(range(1, n_heads - 1)) + [0, n_heads - 1]
        saved, moving = (), None
        backs, mixes = {}, {}
        for step in sequence:
            xs, gs = both(payloads[step]), both(grad_ring[step])
            if moving is not None and step:
                xs[0] = after(xs[0], moving)
            saved, back, mix = experts(
                step, n_heads, ids, xs, gs, own_in, own_out, tuple(saved)
            )
            backs[step], mixes[step] = back, mix
            if step:
                total = joined(back)
                if moving is not None:
                    total = total + onward(moving).astype(jnp.float32)
                moving = total.astype(jnp.bfloat16)
        buffer, grad_outputs, hidden, grad_pre = [
            value.reshape(n_local, group_size * CAP, value.shape[3]) for value in saved
        ]
        grad_pre = after(grad_pre, moving)
        last_back = onward(moving)
        hidden, last_back = lax.optimization_barrier((hidden, last_back))
        if expert_in.shape[0] == D:
            order = lax.axis_index("chip") ^ jnp.arange(chip, dtype=jnp.int32)
            parts_in = expert_grads(order, buffer, grad_pre)
        else:
            parts_in = [plain_grads(buffer, grad_pre)]
        w_qkv = plane(after(column[:, :, :qkv_width], context))
        mix_moving = joined(mixes[1]).astype(jnp.bfloat16)
        mix_received = onward(after(mix_moving, last_back))
        back_sum = joined(backs[0]) + after(last_back, w_qkv, *parts_in).astype(jnp.float32)

        grad_gates = back_sum[:, width : width + E] + back_sum[:, width + E : width + 2 * E]
        grad_logits = gates * (grad_gates - jnp.sum(gates * grad_gates, -1, keepdims=True))
        grad_logits = grad_logits * valid_float
        grad_out = cotangent.astype(jnp.float32).reshape(token_rows, width) * valid_float
        grad_normed_ffn = back_sum[:, :width] + jnp.dot(
            grad_logits, w_router.astype(jnp.float32).T, precision=TOP_PRECISION
        )
        grad_mid_norm, gain_two_term = norm_back(grad_normed_ffn, mid_state, factor_two, gain_two)
        grad_mid = grad_out + grad_mid_norm
        grad_mid_low = grad_mid.astype(jnp.bfloat16)
        context_gradient = jnp.stack(
            [
                dot_nt(grad_mid_low, w_proj[h * heads_width : (h + 1) * heads_width])
                for h in range(n_heads)
            ]
        ).astype(jnp.bfloat16)
        context_gradient = after(context_gradient, mix_received)
        near, near_out = (), ()
        if len(parts_in) > 1:
            near = first_phase(parts_in)
            parts_out = expert_grads(order, grad_outputs, hidden)
        else:
            parts_out = [plain_grads(grad_outputs, hidden)]
        context_gradient, parts_out = lax.optimization_barrier((context_gradient, parts_out))
        if near:
            near_out = first_phase(parts_out)
        grad_context_heads = lax.all_to_all(
            context_gradient.reshape(n_heads, slots, span, heads_width),
            "heads",
            split_axis=0,
            concat_axis=0,
            tiled=True,
        )
        logits_padded = jnp.concatenate(
            [grad_logits, jnp.zeros((token_rows, TAIL - E), jnp.float32)], 1
        )
        second = cut_rows(
            context,
            after(grad_mid_low, context_gradient),
            normed_ffn,
            logits_padded,
            gain_two_term[:, None],
            chip * core,
            own_columns,
        )

        mix_received, near, second = lax.optimization_barrier((mix_received, near, second))
        for chunk in range(2, n_heads):
            mix_moving = (joined(mixes[chunk]) + mix_received.astype(jnp.float32)).astype(
                jnp.bfloat16
            )
            if chunk == 2:
                grad_before, cut = attention_backward(
                    packed,
                    lse,
                    after(grad_context_heads, mix_moving),
                    normed_whole,
                    tables,
                    groups_local,
                    second,
                )
            if chunk < n_heads - 1:
                mix_received = onward(after(mix_moving, grad_context_heads))
        grad_mine = lax.all_to_all(
            after(grad_before, mix_received), "heads", split_axis=0, concat_axis=0, tiled=True
        ).reshape(n_heads, token_rows, own_columns)
        part = spread_rows(cut)
        if near:
            far_in, far_out = second_phase(parts_in, near), second_phase(parts_out, near_out)
        mix_moving, grad_mine = lax.optimization_barrier((mix_moving, grad_mine))
        mix_last = onward(mix_moving)
        grad_normed_attn = dot_nt(grad_mine[0], w_qkv[:, :own_columns])
        for h in range(1, n_heads):
            grad_normed_attn = grad_normed_attn + dot_nt(
                grad_mine[h], w_qkv[:, h * own_columns : (h + 1) * own_columns]
            )
        grad_state_norm, _ = norm_back(grad_normed_attn, state, norm_factor(state), gain_one)
        grad_tokens = (grad_mid + grad_state_norm).astype(jnp.bfloat16).reshape(tokens.shape)
        if near:
            grad_expert_in = finished(parts_in, near, after(far_in, mix_last))
            grad_expert_out = finished(parts_out, near_out, after(far_out, mix_last))
        else:
            grad_expert_in, grad_expert_out = [
                lax.psum_scatter(
                    value[0].reshape(-1, value[0].shape[2]),
                    "chip",
                    scatter_dimension=0,
                    tiled=True,
                ).astype(jnp.float32)
                for value in (parts_in, parts_out)
            ]
        mixture = joined(mixes[0]) + mix_last.astype(jnp.float32)
        mixed = (valid_float * (mid_state + mixture)).astype(jnp.bfloat16)

        last = lax.all_to_all(
            part, "heads", split_axis=0, concat_axis=0, tiled=True
        ).astype(jnp.float32)
        second = jnp.sum(last[:, :, own_columns:], 0)
        grad_attn_out = second[:, :D]
        grad_router = second[:, D : D + E]
        grad_gain_ffn = second[:, D + E]
        grad_attn_in = jnp.concatenate([last[h, :, :own_columns] for h in range(n_heads)], 1)
        grad_gain_attn = jnp.sum(
            grad_attn_in * attention_input_weight.astype(jnp.float32), -1
        ) / gain_attn.astype(jnp.float32)
        return (
            mixed.reshape(tokens.shape),
            grad_tokens,
            grad_attn_in,
            grad_attn_out,
            grad_router,
            grad_gain_attn,
            grad_gain_ffn,
            grad_expert_in,
            grad_expert_out,
        )

    return local


def solution(mesh):
    n_heads, n_shard = mesh.shape["heads"], mesh.shape["shard"]
    core = 2 if n_heads * n_shard == E else 1
    chip = n_shard // core
    split = jax.sharding.Mesh(
        mesh.devices.reshape(n_heads, chip, core), ("heads", "chip", "core")
    )
    shard = ("chip", "core")
    everyone = ("heads", "chip", "core")
    token_spec = P(shard, "heads", None)
    rows = P(everyone, None)
    in_specs = (
        token_spec,
        token_spec,
        P(shard),
        token_spec,
        rows,
        rows,
        rows,
        P(everyone),
        P(everyone),
        rows,
        rows,
    )
    out_specs = (token_spec, token_spec, rows, rows, rows, P(everyone), P(everyone), rows, rows)
    return jax.shard_map(
        make_local(n_heads, chip, core),
        mesh=split,
        in_specs=in_specs,
        out_specs=out_specs,
        check_vma=False,
    )
```

```python
import functools
import math

import jax
import jax.numpy as jnp
import numpy as np
from jax import lax
from jax.experimental import pallas as pl
from jax.experimental.pallas import tpu as pltpu
from jax.sharding import PartitionSpec as P

D = 1024
QUERY_HEADS = 16
KEY_VALUE_HEADS = 8
HEAD_SIZE = 64
E = 32
FFE = 512
TOPK = 8
QUERIES_PER_KV = 2
CAP = 160
GROUP = (QUERIES_PER_KV + 2) * HEAD_SIZE
PAIR = QUERIES_PER_KV * HEAD_SIZE
TAIL = 128
BLOCK = 256
VMEM_BYTES = 56 * 2**20


EPSILON = 1e-06
THETA_BASE = 10000.0
NEGATIVE = -1e30
TOP_PRECISION = lax.Precision.HIGHEST
SCALE = 1.0 / math.sqrt(HEAD_SIZE)
SHORT = pl.CostEstimate(flops=1024, bytes_accessed=1024, transcendentals=0)


def dot_nn(left, right):
    return jnp.dot(left, right, preferred_element_type=jnp.float32)


def dot_nt(left, right):
    return lax.dot_general(
        left, right, (((1,), (1,)), ((), ())), preferred_element_type=jnp.float32
    )


def dot_tn(left, right):
    return lax.dot_general(
        left, right, (((0,), (0,)), ((), ())), preferred_element_type=jnp.float32
    )


def norm_factor(value):
    return lax.rsqrt(jnp.mean(value * value, -1, keepdims=True) + EPSILON)


def norm_back(grad_in, value, factor, gain):
    normalized_rows = value * factor
    scaled = grad_in * gain
    gain_term = jnp.sum(grad_in * normalized_rows, 0)
    grad_value = factor * (
        scaled - normalized_rows * jnp.mean(scaled * normalized_rows, -1, keepdims=True)
    )
    return (grad_value, gain_term)


def rotary_tables(length):
    half_size = HEAD_SIZE // 2
    freqs = THETA_BASE ** (-2.0 * np.arange(half_size) / HEAD_SIZE)
    angles = np.arange(length)[:, None] * freqs[None, :]
    cosine, sine = np.cos(angles), np.sin(angles)
    one = np.ones((length, HEAD_SIZE))
    own = np.concatenate([cosine, cosine] * (QUERIES_PER_KV + 1) + [one], 1)
    other = np.concatenate([-sine, sine] * (QUERIES_PER_KV + 1) + [0.0 * one], 1)
    return (jnp.asarray(own, jnp.float32), jnp.asarray(other, jnp.float32))


def partner(values):
    width = values.shape[1]
    lane = lax.broadcasted_iota(jnp.int32, values.shape, 1)
    half_size = HEAD_SIZE // 2
    return jnp.where(
        lax.rem(lane, HEAD_SIZE) < half_size,
        pltpu.roll(values, width - half_size, 1),
        pltpu.roll(values, half_size, 1),
    )


def stack_queries(block):
    values = block.astype(jnp.float32) * SCALE
    low = lax.broadcasted_iota(jnp.int32, values.shape, 1) < HEAD_SIZE
    first = jnp.where(low, values, 0.0)
    second = jnp.where(low, pltpu.roll(values, HEAD_SIZE, 1), 0.0)
    return jnp.concatenate([first, second], 0).astype(jnp.bfloat16)


def stack_grads(block):
    values = block.astype(jnp.float32)
    low = lax.broadcasted_iota(jnp.int32, values.shape, 1) < HEAD_SIZE
    first = jnp.where(low, 0.0, pltpu.roll(values, HEAD_SIZE, 1))
    second = jnp.where(low, 0.0, values)
    return jnp.concatenate([first, second], 0).astype(jnp.bfloat16)


def attention_forward_kernel(pieces, place_ref, *refs):
    xs, refs = refs[:pieces], refs[pieces:]
    gain_ref, w_ref, own_ref, other_ref = refs[:4]
    packed_ref, context_ref, lse_ref, normed_ref = refs[4:]
    span = xs[0].shape[1]
    length = pieces * span

    @pl.when(pl.program_id(1) == 0)
    def _():
        for step in range(pieces):
            at = place_ref[step]
            for start in range(0, span, BLOCK):
                value = xs[step][0, start : start + BLOCK, :].astype(jnp.float32)
                normed_ref[at, 0, start : start + BLOCK, :] = (
                    value * norm_factor(value) * gain_ref[...]
                ).astype(jnp.bfloat16)

    for start in range(0, length, BLOCK):
        rows = slice(start, start + BLOCK)
        before = dot_nn(
            normed_ref[start // span, 0, start % span : start % span + BLOCK, :], w_ref[...]
        )
        packed_ref[0, rows, :] = (
            before * own_ref[rows, :] + partner(before) * other_ref[rows, :]
        ).astype(jnp.bfloat16)

    low = lax.broadcasted_iota(jnp.int32, (BLOCK, PAIR), 1) < HEAD_SIZE
    lane_zero = lax.broadcasted_iota(jnp.int32, (BLOCK, PAIR), 1) == 0
    query_row = lax.rem(lax.broadcasted_iota(jnp.int32, (2 * BLOCK, BLOCK), 0), BLOCK)
    allowed = lax.broadcasted_iota(jnp.int32, (2 * BLOCK, BLOCK), 1) <= query_row
    for start in range(0, length, BLOCK):
        rows = slice(start, start + BLOCK)
        queries = stack_queries(packed_ref[0, rows, :PAIR])
        inside = packed_ref[0, rows, PAIR:]
        scores_inside = jnp.where(allowed, dot_nt(queries, inside), NEGATIVE)
        highest = jnp.max(scores_inside, 1, keepdims=True)
        if start:
            before_keys = packed_ref[0, :start, PAIR:]
            scores_before = dot_nt(queries, before_keys)
            highest = jnp.maximum(highest, jnp.max(scores_before, 1, keepdims=True))
        weights = jnp.exp(scores_inside - highest)
        total = jnp.sum(weights, 1, keepdims=True)
        result = dot_nn(weights.astype(jnp.bfloat16), inside)
        if start:
            weights = jnp.exp(scores_before - highest)
            total = total + jnp.sum(weights, 1, keepdims=True)
            result = result + dot_nn(weights.astype(jnp.bfloat16), before_keys)
        result = result / total
        context_ref[start // span, 0, start % span : start % span + BLOCK, :] = jnp.where(
            low, pltpu.roll(result[:BLOCK], HEAD_SIZE, 1), result[BLOCK:]
        ).astype(jnp.bfloat16)
        log_total = highest + jnp.log(total)
        columns = jnp.where(lane_zero, log_total[:BLOCK], log_total[BLOCK:])
        lse_ref[0, 0, :, rows] = columns.T[:8, :]


def attention_forward(xs, places, gain, weights, tables, groups_local):
    pieces = len(xs)
    slots, span, width = xs[0].shape
    length = pieces * span
    bf16, f32 = jnp.bfloat16, jnp.float32
    return pl.pallas_call(
        functools.partial(attention_forward_kernel, pieces),
        grid_spec=pltpu.PrefetchScalarGridSpec(
            num_scalar_prefetch=1,
            grid=(slots, groups_local),
            in_specs=[pl.BlockSpec((1, span, width), lambda s, g, place: (s, 0, 0))] * pieces
            + [
                pl.BlockSpec((1, width), lambda s, g, place: (0, 0)),
                pl.BlockSpec((width, GROUP), lambda s, g, place: (0, g)),
                pl.BlockSpec((length, GROUP), lambda s, g, place: (0, 0)),
                pl.BlockSpec((length, GROUP), lambda s, g, place: (0, 0)),
            ],
            out_specs=[
                pl.BlockSpec((1, length, GROUP), lambda s, g, place: (s, 0, g)),
                pl.BlockSpec((pieces, 1, span, PAIR), lambda s, g, place: (0, s, 0, g)),
                pl.BlockSpec((1, 1, 8, length), lambda s, g, place: (s, g, 0, 0)),
                pl.BlockSpec((pieces, 1, span, width), lambda s, g, place: (0, s, 0, 0)),
            ],
        ),
        out_shape=[
            jax.ShapeDtypeStruct((slots, length, groups_local * GROUP), bf16),
            jax.ShapeDtypeStruct((pieces, slots, span, groups_local * PAIR), bf16),
            jax.ShapeDtypeStruct((slots, groups_local, 8, length), f32),
            jax.ShapeDtypeStruct((pieces, slots, span, width), bf16),
        ],
        compiler_params=pltpu.CompilerParams(vmem_limit_bytes=VMEM_BYTES),
        cost_estimate=SHORT,
        name="attention_forward",
    )(places, *xs, gain, weights, *tables)


def attention_backward_kernel(
    packed_ref,
    lse_ref,
    grad_ref,
    normed_ref,
    own_ref,
    other_ref,
    filled_ref,
    out_ref,
    cut_ref,
    total_ref,
    product_ref,
):
    length, span = packed_ref.shape[1], grad_ref.shape[2]
    low = lax.broadcasted_iota(jnp.int32, (BLOCK, PAIR), 1) < HEAD_SIZE
    query_lane = lax.rem(lax.broadcasted_iota(jnp.int32, (BLOCK, 2 * BLOCK), 1), BLOCK)
    allowed = lax.broadcasted_iota(jnp.int32, (BLOCK, 2 * BLOCK), 0) <= query_lane
    total_ref[...] = jnp.zeros_like(total_ref)

    def unturn(values, lanes, rows):
        values = values.astype(jnp.bfloat16).astype(jnp.float32)
        return (
            values * own_ref[rows, lanes] - partner(values) * other_ref[rows, lanes]
        ).astype(jnp.bfloat16)

    for start in range(0, length, BLOCK):
        rows = slice(start, start + BLOCK)
        queries = stack_queries(packed_ref[0, rows, :PAIR])
        inner = slice(start % span, start % span + BLOCK)
        grads = stack_grads(grad_ref[start // span, 0, inner, :])
        log_total = jnp.concatenate([lse_ref[0, 0, 0:1, rows], lse_ref[0, 0, 1:2, rows]], 1)

        def piece(keys):
            scores = dot_nt(keys, queries)
            probs = jnp.exp(scores - log_total)
            return (probs, dot_nt(keys, grads))

        inside = packed_ref[0, rows, PAIR:]
        probs_inside, grad_inside = piece(inside)
        probs_inside = jnp.where(allowed, probs_inside, 0.0)
        delta = jnp.sum(probs_inside * grad_inside, 0, keepdims=True)
        if start:
            before = packed_ref[0, :start, PAIR:]
            probs_before, grad_before = piece(before)
            delta = delta + jnp.sum(probs_before * grad_before, 0, keepdims=True)
        score_grads = (probs_inside * (grad_inside - delta)).astype(jnp.bfloat16)
        total_ref[rows, :] += dot_nn(probs_inside.astype(jnp.bfloat16), grads) + dot_nn(
            score_grads, queries
        )
        grad_query = dot_tn(score_grads, inside)
        if start:
            score_grads = (probs_before * (grad_before - delta)).astype(jnp.bfloat16)
            total_ref[:start, :] += dot_nn(probs_before.astype(jnp.bfloat16), grads) + dot_nn(
                score_grads, queries
            )
            grad_query = grad_query + dot_tn(score_grads, before)
        grad_query = (
            jnp.where(low, grad_query[:BLOCK], pltpu.roll(grad_query[BLOCK:], HEAD_SIZE, 1)) * SCALE
        )
        out_ref[start // span, 0, inner, :PAIR] = unturn(grad_query, slice(0, PAIR), rows)
    for start in range(0, length, BLOCK):
        rows = slice(start, start + BLOCK)
        inner = slice(start % span, start % span + BLOCK)
        out_ref[start // span, 0, inner, PAIR:] = unturn(
            total_ref[rows, :], slice(PAIR, GROUP), rows
        )

    @pl.when(pl.program_id(1) == 0)
    def _():
        product_ref[...] = jnp.zeros_like(product_ref)

    for at in range(length // span):
        product_ref[...] += dot_tn(normed_ref[at, 0], out_ref[at, 0])

    @pl.when(pl.program_id(1) == pl.num_programs(1) - 1)
    def _():
        parts, heads, each = cut_ref.shape[:3]
        for h in range(heads):
            block = product_ref[h * parts * each : (h + 1) * parts * each, :]
            cut_ref[:, h] = block.reshape(parts, each, GROUP).astype(cut_ref.dtype)


def attention_backward(packed, lse, grads, normed, tables, groups_local, cut):
    slots, length = packed.shape[:2]
    pieces, span, width = grads.shape[0], grads.shape[2], normed.shape[3]
    parts, _, each, _ = cut.shape
    return pl.pallas_call(
        attention_backward_kernel,
        grid=(groups_local, slots),
        in_specs=[
            pl.BlockSpec((1, length, GROUP), lambda g, s: (s, 0, g)),
            pl.BlockSpec((1, 1, 8, length), lambda g, s: (s, g, 0, 0)),
            pl.BlockSpec((pieces, 1, span, PAIR), lambda g, s: (0, s, 0, g)),
            pl.BlockSpec((pieces, 1, span, width), lambda g, s: (0, s, 0, 0)),
            pl.BlockSpec((length, GROUP), lambda g, s: (0, 0)),
            pl.BlockSpec((length, GROUP), lambda g, s: (0, 0)),
            pl.BlockSpec(memory_space=pl.ANY),
        ],
        out_specs=[
            pl.BlockSpec((pieces, 1, span, GROUP), lambda g, s: (0, s, 0, g)),
            pl.BlockSpec((parts, pieces, each, GROUP), lambda g, s: (0, 0, 0, g)),
        ],
        out_shape=[
            jax.ShapeDtypeStruct((pieces, slots, span, packed.shape[2]), jnp.bfloat16),
            jax.ShapeDtypeStruct(cut.shape, cut.dtype),
        ],
        input_output_aliases={6: 1},
        scratch_shapes=[
            pltpu.VMEM((length, PAIR), jnp.float32),
            pltpu.VMEM((width, GROUP), jnp.float32),
        ],
        compiler_params=pltpu.CompilerParams(vmem_limit_bytes=VMEM_BYTES),
        cost_estimate=SHORT,
        name="attention_backward",
    )(packed, lse, grads, normed, *tables, cut)


def expert_kernel(sources, n_local, kept, ids_ref, *refs):
    xs, refs = refs[:sources], refs[sources:]
    gs, refs = refs[:sources], refs[sources:]
    w_in_ref, w_out_ref = refs[:2]
    refs = refs[2 + kept :]
    buffer_ref, grad_out_ref, hidden_ref, grad_pre_ref = refs[:4]
    backs, mixes = refs[4 : 4 + sources], refs[4 + sources : 4 + 2 * sources]
    table, picks, mix_rows, back_rows, gate_back = refs[4 + 2 * sources :]
    step = pl.program_id(0)
    expert = ids_ref[step]
    tokens = xs[0].shape[0]
    here = pl.ds(pl.multiple_of(step * CAP, 16), CAP)

    @pl.when(step == 0)
    def _():
        for s in range(sources):
            table[s] = xs[s][:, D:].astype(jnp.float32).T
            gate_back[s] = jnp.zeros((TAIL, tokens), jnp.float32)

    place = lax.broadcasted_iota(jnp.int32, (CAP, tokens), 0).astype(jnp.float32)
    hits, gate_rows, grad_rows = [], [], []
    for s in range(sources):
        code = table[s, pl.ds(expert, 1), :]
        gate = table[s, pl.ds(expert + E, 1), :] + table[s, pl.ds(expert + 2 * E, 1), :]
        hit = code == place
        pick = jnp.where(hit, 1.0, 0.0).astype(jnp.bfloat16)
        picks[s, here, :] = pick
        hits.append(hit)
        gate_rows.append(jnp.sum(jnp.where(hit, gate, 0.0), 1, keepdims=True))
        buffer_ref[0, 0, s * CAP : (s + 1) * CAP, :] = dot_nn(pick, xs[s][:, :D]).astype(
            jnp.bfloat16
        )
        grad_rows.append(dot_nn(pick, gs[s][...]))
    gate_row = jnp.concatenate(gate_rows, 0)
    grad_row = jnp.concatenate(grad_rows, 0)
    grad_out_ref[0, 0] = (gate_row * grad_row).astype(jnp.bfloat16)
    pre = dot_nn(buffer_ref[0, 0], w_in_ref[0])
    grad_plain = dot_nn(grad_row.astype(jnp.bfloat16), w_out_ref[0])
    gate_pre, up_pre = pre[:, :FFE], pre[:, FFE:]
    sigmoid_gate = 1.0 / (1.0 + jnp.exp(-gate_pre))
    silu_gate = gate_pre * sigmoid_gate
    hidden = (silu_gate * up_pre).astype(jnp.bfloat16)
    hidden_ref[0, 0] = hidden
    gate_grad = jnp.sum(grad_plain * hidden.astype(jnp.float32), 1, keepdims=True)
    grad_hidden = gate_row * grad_plain
    grad_pre_ref[0, 0, :, :FFE] = (
        grad_hidden * up_pre * sigmoid_gate * (1.0 + gate_pre * (1.0 - sigmoid_gate))
    ).astype(jnp.bfloat16)
    grad_pre_ref[0, 0, :, FFE:] = (grad_hidden * silu_gate).astype(jnp.bfloat16)
    outputs = (gate_row * dot_nt(hidden, w_out_ref[0])).astype(jnp.bfloat16)
    back = dot_nt(grad_pre_ref[0, 0], w_in_ref[0]).astype(jnp.bfloat16)
    for s in range(sources):
        part = slice(s * CAP, (s + 1) * CAP)
        mix_rows[s, here, :] = outputs[part]
        back_rows[s, here, :] = back[part]
        row = jnp.sum(jnp.where(hits[s], gate_grad[part], 0.0), 0, keepdims=True)
        high = row.astype(jnp.bfloat16).astype(jnp.float32)
        gate_back[s, pl.ds(expert, 1), :] = high
        gate_back[s, pl.ds(expert + E, 1), :] = row - high

    @pl.when(step == n_local - 1)
    def _():
        for s in range(sources):
            backs[s][:, :D] = dot_tn(picks[s], back_rows[s]).astype(jnp.bfloat16)
            backs[s][:, D:] = gate_back[s].T.astype(jnp.bfloat16)
            mixes[s][...] = dot_tn(picks[s], mix_rows[s]).astype(jnp.bfloat16)


def experts(chunk, chunks, ids, xs, gs, own_in, own_out, kept):
    sources, n_local, tokens = len(xs), own_in.shape[0], xs[0].shape[0]
    rows = sources * CAP
    bf16, f32 = jnp.bfloat16, jnp.float32
    fixed = lambda i, ids: (0, 0)
    saved = lambda columns: pl.BlockSpec((1, 1, rows, columns), lambda i, ids: (i, chunk, 0, 0))
    widths = (D, D, FFE, 2 * FFE)
    in_specs = (
        [pl.BlockSpec((tokens, D + TAIL), fixed)] * sources
        + [pl.BlockSpec((tokens, D), fixed)] * sources
        + [
            pl.BlockSpec((1, D, 2 * FFE), lambda i, ids: (i, 0, 0)),
            pl.BlockSpec((1, D, FFE), lambda i, ids: (i, 0, 0)),
        ]
        + [pl.BlockSpec(memory_space=pl.ANY)] * len(kept)
    )
    results = pl.pallas_call(
        functools.partial(expert_kernel, sources, n_local, len(kept)),
        grid_spec=pltpu.PrefetchScalarGridSpec(
            num_scalar_prefetch=1,
            grid=(n_local,),
            in_specs=in_specs,
            out_specs=[saved(columns) for columns in widths]
            + [pl.BlockSpec((tokens, D + TAIL), fixed)] * sources
            + [pl.BlockSpec((tokens, D), fixed)] * sources,
            scratch_shapes=[
                pltpu.VMEM((sources, TAIL, tokens), f32),
                pltpu.VMEM((sources, n_local * CAP, tokens), bf16),
                pltpu.VMEM((sources, n_local * CAP, D), bf16),
                pltpu.VMEM((sources, n_local * CAP, D), bf16),
                pltpu.VMEM((sources, TAIL, tokens), f32),
            ],
        ),
        out_shape=[
            jax.ShapeDtypeStruct((n_local, chunks, rows, columns), bf16) for columns in widths
        ]
        + [jax.ShapeDtypeStruct((tokens, D + TAIL), bf16)] * sources
        + [jax.ShapeDtypeStruct((tokens, D), bf16)] * sources,
        input_output_aliases={3 + 2 * sources + i: i for i in range(len(kept))},
        compiler_params=pltpu.CompilerParams(vmem_limit_bytes=VMEM_BYTES),
        cost_estimate=pl.CostEstimate(
            flops=n_local * rows * D * (4 * tokens + 9 * FFE),
            bytes_accessed=n_local * D * FFE * 6 + tokens * sources * D * 8,
            transcendentals=0,
        ),
        name="experts",
    )(ids, *xs, *gs, own_in, own_out, *kept)
    return results[:4], results[4 : 4 + sources], results[4 + sources :]


def cut_rows_kernel(offset, left_ref, right_ref, normed_ref, logits_ref, gain_ref, out_ref):
    parts, rows = out_ref.shape[0], out_ref.shape[2]
    width = right_ref.shape[1]
    product = dot_tn(left_ref[...], right_ref[...])
    out_ref[:, 0, :, :offset] = jnp.zeros((parts, rows, offset), out_ref.dtype)
    out_ref[:, 0, :, offset : offset + width] = product.reshape(parts, rows, width).astype(
        out_ref.dtype
    )
    rest = logits_ref[...]
    tail = jnp.zeros((left_ref.shape[1], TAIL), jnp.float32)
    for _ in range(3):
        term = rest.astype(jnp.bfloat16)
        rest = rest - term.astype(jnp.float32)
        tail = tail + dot_tn(normed_ref[...], term)
    lane = lax.broadcasted_iota(jnp.int32, tail.shape, 1)
    tail = jnp.where(lane == E, gain_ref[...], tail)
    out_ref[:, 0, :, offset + width :] = tail.reshape(parts, rows, TAIL).astype(out_ref.dtype)


def cut_rows(left, right, normed, logits, gain_term, parts, offset):
    n_heads, depth, each = left.shape
    width = right.shape[1]
    columns = offset + width + TAIL
    return pl.pallas_call(
        functools.partial(cut_rows_kernel, offset),
        grid=(n_heads,),
        in_specs=[
            pl.BlockSpec((pl.squeezed, depth, each), lambda h: (h, 0, 0)),
            pl.BlockSpec((depth, width), lambda h: (0, 0)),
            pl.BlockSpec((depth, each), lambda h: (0, h)),
            pl.BlockSpec((depth, TAIL), lambda h: (0, 0)),
            pl.BlockSpec((each, 1), lambda h: (h, 0)),
        ],
        out_specs=pl.BlockSpec((parts, 1, each // parts, columns), lambda h: (0, h, 0, 0)),
        out_shape=jax.ShapeDtypeStruct(
            (parts, n_heads, each // parts, columns),
            jnp.bfloat16 if each // parts % 16 == 0 else jnp.float32,
        ),
        compiler_params=pltpu.CompilerParams(vmem_limit_bytes=VMEM_BYTES),
        cost_estimate=pl.CostEstimate(
            flops=4 * depth * each * n_heads * columns,
            bytes_accessed=depth * (each * n_heads + width) * 2 + each * n_heads * columns * 4,
            transcendentals=0,
        ),
        name="cut_rows",
    )(left, right, normed, logits, gain_term)


def expert_grads_kernel(
    order_ref, left_ref, right_ref, own_ref, first_send, second_send, first_keep, second_keep
):
    product = dot_tn(left_ref[0], right_ref[0])
    step = pl.program_id(0)
    half = product.shape[0] // 2
    low = jnp.bfloat16

    @pl.when(step == 0)
    def _():
        own_ref[...] = product

    @pl.when(step == 1)
    def _():
        first_send[0] = product[:half].astype(low)
        second_keep[...] = product[half:]

    @pl.when(step == 2)
    def _():
        first_keep[...] = product[:half]
        second_send[0] = product[half:].astype(low)

    @pl.when(step == 3)
    def _():
        first_send[1] = product[:half].astype(low)
        second_send[1] = product[half:].astype(low)


def expert_grads(order, left, right):
    count, depth, height = left.shape
    width = right.shape[2]
    half = height // 2
    bf16, f32 = jnp.bfloat16, jnp.float32
    whole, pair, one = (height, width), (2, half, width), (half, width)
    return pl.pallas_call(
        expert_grads_kernel,
        grid_spec=pltpu.PrefetchScalarGridSpec(
            num_scalar_prefetch=1,
            grid=(count,),
            in_specs=[
                pl.BlockSpec((1, depth, height), lambda i, order: (order[i], 0, 0)),
                pl.BlockSpec((1, depth, width), lambda i, order: (order[i], 0, 0)),
            ],
            out_specs=[
                pl.BlockSpec(whole, lambda i, order: (0, 0)),
                pl.BlockSpec(pair, lambda i, order: (0, 0, 0)),
                pl.BlockSpec(pair, lambda i, order: (0, 0, 0)),
                pl.BlockSpec(one, lambda i, order: (0, 0)),
                pl.BlockSpec(one, lambda i, order: (0, 0)),
            ],
        ),
        out_shape=[
            jax.ShapeDtypeStruct(whole, f32),
            jax.ShapeDtypeStruct(pair, bf16),
            jax.ShapeDtypeStruct(pair, bf16),
            jax.ShapeDtypeStruct(one, f32),
            jax.ShapeDtypeStruct(one, f32),
        ],
        compiler_params=pltpu.CompilerParams(vmem_limit_bytes=VMEM_BYTES),
        cost_estimate=SHORT,
        name="expert_grads",
    )(order, left, right)


def plain_grads_kernel(left_ref, right_ref, out_ref):
    out_ref[0] = dot_tn(left_ref[0], right_ref[0]).astype(out_ref.dtype)


def plain_grads(left, right):
    count, depth, height = left.shape
    width = right.shape[2]
    return pl.pallas_call(
        plain_grads_kernel,
        grid=(count,),
        in_specs=[
            pl.BlockSpec((1, depth, height), lambda i: (i, 0, 0)),
            pl.BlockSpec((1, depth, width), lambda i: (i, 0, 0)),
        ],
        out_specs=pl.BlockSpec((1, height, width), lambda i: (i, 0, 0)),
        out_shape=jax.ShapeDtypeStruct((count, height, width), jnp.bfloat16),
        compiler_params=pltpu.CompilerParams(vmem_limit_bytes=VMEM_BYTES),
        cost_estimate=pl.CostEstimate(
            flops=4 * count * depth * height * width,
            bytes_accessed=2 * count * (depth * (height + width) + height * width),
            transcendentals=0,
        ),
        name="plain_grads",
    )(left, right)


def make_local(n_heads, chip, core):
    everyone = ("heads", "chip", "core")
    group_size = n_heads * core
    n_local = E // group_size
    groups_local = KEY_VALUE_HEADS // n_heads
    ring = [(i, (i + 1) % n_heads) for i in range(n_heads)]
    crossed = [(i, core - 1 - i) for i in range(core)]

    def onward(value):
        return lax.ppermute(value, "heads", ring)

    def across(value):
        return lax.ppermute(value, "core", crossed)

    def around(value):
        values = [value]
        for _ in range(n_heads - 1):
            values.append(onward(values[-1]))
        return values

    def both(value):
        return [value] if core == 1 else [value, across(value)]

    def joined(parts):
        total = parts[0].astype(jnp.float32)
        if core > 1:
            total = total + across(parts[1]).astype(jnp.float32)
        return total

    def first_phase(parts):
        return (paired(parts[1], 1), paired(parts[2], 2))

    def second_phase(parts, got):
        own, _, _, first_keep, second_keep = parts
        first_next = (first_keep + got[0][1].astype(jnp.float32)).astype(jnp.bfloat16)
        second_next = (second_keep + got[1][1].astype(jnp.float32)).astype(jnp.bfloat16)
        return (paired(first_next, 2), paired(second_next, 1))

    def finished(parts, got, last):
        own = parts[0]
        half = own.shape[0] // 2
        first = own[:half] + got[0][0].astype(jnp.float32) + last[0].astype(jnp.float32)
        second = own[half:] + got[1][0].astype(jnp.float32) + last[1].astype(jnp.float32)
        return jnp.concatenate([first, second], 0)

    def after(value, *others):
        return lax.optimization_barrier((value, others))[0]

    def paired(value, other):
        return lax.ppermute(value, "chip", [(i, i ^ other) for i in range(chip)])

    def spread_rows(cut):
        part = lax.psum_scatter(
            cut.reshape(-1, cut.shape[3]), ("chip", "core"), scatter_dimension=0, tiled=True
        )
        return part.reshape(cut.shape[1:])

    def local(
        tokens,
        cotangent,
        lengths,
        routes,
        attention_input_weight,
        attn_out,
        router,
        gain_attn,
        gain_ffn,
        expert_in,
        expert_out,
    ):
        slots, span, width = tokens.shape
        token_rows = slots * span
        length = span * n_heads
        rank = lax.axis_index("heads")
        qkv_width = attention_input_weight.shape[1]
        own_columns = groups_local * GROUP
        rings = around(tokens)
        small = jnp.concatenate(
            [
                attention_input_weight,
                attn_out,
                router,
                gain_attn[:, None],
                gain_ffn[:, None],
                jnp.zeros((router.shape[0], TAIL - E - 2), jnp.bfloat16),
            ],
            1,
        )
        column = lax.all_to_all(
            jnp.broadcast_to(after(small, rings[1])[None], (n_heads,) + small.shape),
            "heads",
            split_axis=0,
            concat_axis=0,
            tiled=True,
        )

        own_out = lax.all_gather(expert_out, "chip", axis=0, tiled=True).reshape(n_local, D, FFE)

        def plane(value):
            value = lax.all_gather(value, ("chip", "core"), axis=1, tiled=True)
            return value.reshape(-1, value.shape[2])

        first = plane(
            after(
                jnp.concatenate(
                    [
                        lax.dynamic_slice_in_dim(column, rank * own_columns, own_columns, 2),
                        column[:, :, qkv_width + D :],
                    ],
                    2,
                ),
                own_out,
                rings[2],
            )
        )
        w_own = first
        gain_one = first[:, own_columns + E].astype(jnp.float32)
        w_proj = plane(column[:, :, qkv_width:])
        w_router = w_proj[:, D : D + E]
        gain_two = w_proj[:, D + E + 1].astype(jnp.float32)
        w_proj = w_proj[:, :D]
        own_grads = cotangent.reshape(token_rows, width)
        own_in = lax.all_gather(after(expert_in, first, rings[-1]), "chip", axis=0, tiled=True).reshape(
            n_local, D, 2 * FFE
        )

        positions = rank * span + jnp.arange(span, dtype=jnp.int32)
        valid = (positions[None, :] < lengths[:, None]).reshape(token_rows)
        valid_float = valid.astype(jnp.float32)[:, None]
        route_rows = routes.reshape(token_rows, TOPK)
        routed = jnp.any(
            route_rows[:, :, None] == jnp.arange(E, dtype=jnp.int32)[None, None, :], 1
        )
        live = (routed & valid[:, None]).astype(jnp.bfloat16)
        earlier = (
            jnp.arange(token_rows)[:, None] > jnp.arange(token_rows)[None, :]
        ).astype(jnp.bfloat16)
        count = jnp.dot(earlier, live, preferred_element_type=jnp.float32)
        kept = (live > 0) & (count < CAP)
        code = jnp.where(kept, count, -1.0).astype(jnp.bfloat16)
        ids = (rank * n_local + jnp.arange(n_local, dtype=jnp.int32)) * core + lax.axis_index("core")

        tables = rotary_tables(length)
        places = (rank + n_heads - jnp.arange(n_heads, dtype=jnp.int32)) % n_heads
        packed, context_heads, lse, normed_whole = attention_forward(
            rings, places, gain_one[None, :], w_own, tables, groups_local
        )
        grad_ring = [own_grads, onward(after(own_grads, rings[-1]))]
        context_heads = after(context_heads, grad_ring[1])
        context = lax.all_to_all(context_heads, "heads", split_axis=0, concat_axis=0, tiled=True)
        grad_ring.append(onward(after(grad_ring[1], context)))
        heads_width = groups_local * PAIR
        context = context.reshape(n_heads, token_rows, heads_width)

        state = tokens.astype(jnp.float32).reshape(token_rows, width)
        mid_state = state
        for h in range(n_heads):
            mid_state = mid_state + dot_nn(
                context[h], w_proj[h * heads_width : (h + 1) * heads_width]
            )
        factor_two = norm_factor(mid_state)
        normed_ffn = (mid_state * factor_two * gain_two).astype(jnp.bfloat16)
        logits = jnp.dot(normed_ffn, w_router, preferred_element_type=jnp.float32)
        highest = jnp.max(jnp.where(routed, logits, NEGATIVE), -1, keepdims=True)
        weights = jnp.where(routed, jnp.exp(jnp.where(routed, logits - highest, 0.0)), 0.0)
        gates = weights / jnp.sum(weights, -1, keepdims=True)
        gates_high = lax.reduce_precision(gates, 8, 7)
        payload = jnp.concatenate(
            [
                normed_ffn,
                code,
                gates_high.astype(jnp.bfloat16),
                (gates - gates_high).astype(jnp.bfloat16),
                jnp.zeros((token_rows, TAIL - 3 * E), jnp.bfloat16),
            ],
            1,
        )
        while len(grad_ring) < n_heads:
            grad_ring.append(onward(grad_ring[-1]))
        payloads = around(after(payload, grad_ring[-1]))
        sequence = list(range(1, n_heads - 1)) + [0, n_heads - 1]
        saved, moving = (), None
        backs, mixes = {}, {}
        for step in sequence:
            xs, gs = both(payloads[step]), both(grad_ring[step])
            if moving is not None and step:
                xs[0] = after(xs[0], moving)
            saved, back, mix = experts(
                step, n_heads, ids, xs, gs, own_in, own_out, tuple(saved)
            )
            backs[step], mixes[step] = back, mix
            if step:
                total = joined(back)
                if moving is not None:
                    total = total + onward(moving).astype(jnp.float32)
                moving = total.astype(jnp.bfloat16)
        buffer, grad_outputs, hidden, grad_pre = [
            value.reshape(n_local, group_size * CAP, value.shape[3]) for value in saved
        ]
        grad_pre = after(grad_pre, moving)
        last_back = onward(moving)
        hidden, last_back = lax.optimization_barrier((hidden, last_back))
        if expert_in.shape[0] == D:
            order = lax.axis_index("chip") ^ jnp.arange(chip, dtype=jnp.int32)
            parts_in = expert_grads(order, buffer, grad_pre)
        else:
            parts_in = [plain_grads(buffer, grad_pre)]
        w_qkv = plane(after(column[:, :, :qkv_width], context))
        mix_moving = joined(mixes[1]).astype(jnp.bfloat16)
        mix_received = onward(after(mix_moving, last_back))
        back_sum = joined(backs[0]) + after(last_back, w_qkv, *parts_in).astype(jnp.float32)

        grad_gates = back_sum[:, width : width + E] + back_sum[:, width + E : width + 2 * E]
        grad_logits = gates * (grad_gates - jnp.sum(gates * grad_gates, -1, keepdims=True))
        grad_logits = grad_logits * valid_float
        grad_out = cotangent.astype(jnp.float32).reshape(token_rows, width) * valid_float
        grad_normed_ffn = back_sum[:, :width] + jnp.dot(
            grad_logits, w_router.astype(jnp.float32).T, precision=TOP_PRECISION
        )
        grad_mid_norm, gain_two_term = norm_back(grad_normed_ffn, mid_state, factor_two, gain_two)
        grad_mid = grad_out + grad_mid_norm
        grad_mid_low = grad_mid.astype(jnp.bfloat16)
        context_gradient = jnp.stack(
            [
                dot_nt(grad_mid_low, w_proj[h * heads_width : (h + 1) * heads_width])
                for h in range(n_heads)
            ]
        ).astype(jnp.bfloat16)
        context_gradient = after(context_gradient, mix_received)
        near, near_out = (), ()
        if len(parts_in) > 1:
            near = first_phase(parts_in)
            parts_out = expert_grads(order, grad_outputs, hidden)
        else:
            parts_out = [plain_grads(grad_outputs, hidden)]
        context_gradient, parts_out = lax.optimization_barrier((context_gradient, parts_out))
        if near:
            near_out = first_phase(parts_out)
        grad_context_heads = lax.all_to_all(
            context_gradient.reshape(n_heads, slots, span, heads_width),
            "heads",
            split_axis=0,
            concat_axis=0,
            tiled=True,
        )
        logits_padded = jnp.concatenate(
            [grad_logits, jnp.zeros((token_rows, TAIL - E), jnp.float32)], 1
        )
        second = cut_rows(
            context,
            after(grad_mid_low, context_gradient),
            normed_ffn,
            logits_padded,
            gain_two_term[:, None],
            chip * core,
            own_columns,
        )

        mix_received, near, second = lax.optimization_barrier((mix_received, near, second))
        for chunk in range(2, n_heads):
            mix_moving = (joined(mixes[chunk]) + mix_received.astype(jnp.float32)).astype(
                jnp.bfloat16
            )
            if chunk == 2:
                grad_before, cut = attention_backward(
                    packed,
                    lse,
                    after(grad_context_heads, mix_moving),
                    normed_whole,
                    tables,
                    groups_local,
                    second,
                )
            if chunk < n_heads - 1:
                mix_received = onward(after(mix_moving, grad_context_heads))
        grad_before, near_out = lax.optimization_barrier((grad_before, near_out))
        grad_mine = lax.all_to_all(
            after(grad_before, mix_received), "heads", split_axis=0, concat_axis=0, tiled=True
        ).reshape(n_heads, token_rows, own_columns)
        part = spread_rows(cut)
        if near:
            far_in, far_out = second_phase(parts_in, near), second_phase(parts_out, near_out)
        mix_moving, grad_mine = lax.optimization_barrier((mix_moving, grad_mine))
        mix_last = onward(mix_moving)
        grad_normed_attn = dot_nt(grad_mine[0], w_qkv[:, :own_columns])
        for h in range(1, n_heads):
            grad_normed_attn = grad_normed_attn + dot_nt(
                grad_mine[h], w_qkv[:, h * own_columns : (h + 1) * own_columns]
            )
        grad_state_norm, _ = norm_back(grad_normed_attn, state, norm_factor(state), gain_one)
        grad_tokens = (grad_mid + grad_state_norm).astype(jnp.bfloat16).reshape(tokens.shape)
        if near:
            grad_expert_in = finished(parts_in, near, after(far_in, grad_tokens))
            grad_expert_out = finished(parts_out, near_out, after(far_out, mix_last))
        else:
            grad_expert_in, grad_expert_out = [
                lax.psum_scatter(
                    value[0].reshape(-1, value[0].shape[2]),
                    "chip",
                    scatter_dimension=0,
                    tiled=True,
                ).astype(jnp.float32)
                for value in (parts_in, parts_out)
            ]
        mixture = joined(mixes[0]) + mix_last.astype(jnp.float32)
        mixed = (valid_float * (mid_state + mixture)).astype(jnp.bfloat16)

        last = lax.all_to_all(
            part, "heads", split_axis=0, concat_axis=0, tiled=True
        ).astype(jnp.float32)
        second = jnp.sum(last[:, :, own_columns:], 0)
        grad_attn_out = second[:, :D]
        grad_router = second[:, D : D + E]
        grad_gain_ffn = second[:, D + E]
        grad_attn_in = jnp.concatenate([last[h, :, :own_columns] for h in range(n_heads)], 1)
        grad_gain_attn = jnp.sum(
            grad_attn_in * attention_input_weight.astype(jnp.float32), -1
        ) / gain_attn.astype(jnp.float32)
        return (
            mixed.reshape(tokens.shape),
            grad_tokens,
            grad_attn_in,
            grad_attn_out,
            grad_router,
            grad_gain_attn,
            grad_gain_ffn,
            grad_expert_in,
            grad_expert_out,
        )

    return local


def solution(mesh):
    n_heads, n_shard = mesh.shape["heads"], mesh.shape["shard"]
    core = 2 if n_heads * n_shard == E else 1
    chip = n_shard // core
    split = jax.sharding.Mesh(
        mesh.devices.reshape(n_heads, chip, core), ("heads", "chip", "core")
    )
    shard = ("chip", "core")
    everyone = ("heads", "chip", "core")
    token_spec = P(shard, "heads", None)
    rows = P(everyone, None)
    in_specs = (
        token_spec,
        token_spec,
        P(shard),
        token_spec,
        rows,
        rows,
        rows,
        P(everyone),
        P(everyone),
        rows,
        rows,
    )
    out_specs = (token_spec, token_spec, rows, rows, rows, P(everyone), P(everyone), rows, rows)
    return jax.shard_map(
        make_local(n_heads, chip, core),
        mesh=split,
        in_specs=in_specs,
        out_specs=out_specs,
        check_vma=False,
    )
```

```python
import functools
import math

import jax
import jax.numpy as jnp
import numpy as np
from jax import lax
from jax.experimental import pallas as pl
from jax.experimental.pallas import tpu as pltpu
from jax.sharding import PartitionSpec as P

D = 1024
QUERY_HEADS = 16
KEY_VALUE_HEADS = 8
HEAD_SIZE = 64
E = 32
FFE = 512
TOPK = 8
QUERIES_PER_KV = 2
CAP = 160
GROUP = (QUERIES_PER_KV + 2) * HEAD_SIZE
PAIR = QUERIES_PER_KV * HEAD_SIZE
TAIL = 128
BLOCK = 256
VMEM_BYTES = 56 * 2**20


EPSILON = 1e-06
THETA_BASE = 10000.0
NEGATIVE = -1e30
TOP_PRECISION = lax.Precision.HIGHEST
SCALE = 1.0 / math.sqrt(HEAD_SIZE)
SHORT = pl.CostEstimate(flops=1024, bytes_accessed=1024, transcendentals=0)


def dot_nn(left, right):
    return jnp.dot(left, right, preferred_element_type=jnp.float32)


def dot_nt(left, right):
    return lax.dot_general(
        left, right, (((1,), (1,)), ((), ())), preferred_element_type=jnp.float32
    )


def dot_tn(left, right):
    return lax.dot_general(
        left, right, (((0,), (0,)), ((), ())), preferred_element_type=jnp.float32
    )


def norm_factor(value):
    return lax.rsqrt(jnp.mean(value * value, -1, keepdims=True) + EPSILON)


def norm_back(grad_in, value, factor, gain):
    normalized_rows = value * factor
    scaled = grad_in * gain
    gain_term = jnp.sum(grad_in * normalized_rows, 0)
    grad_value = factor * (
        scaled - normalized_rows * jnp.mean(scaled * normalized_rows, -1, keepdims=True)
    )
    return (grad_value, gain_term)


def rotary_tables(length):
    half_size = HEAD_SIZE // 2
    freqs = THETA_BASE ** (-2.0 * np.arange(half_size) / HEAD_SIZE)
    angles = np.arange(length)[:, None] * freqs[None, :]
    cosine, sine = np.cos(angles), np.sin(angles)
    one = np.ones((length, HEAD_SIZE))
    own = np.concatenate([cosine, cosine] * (QUERIES_PER_KV + 1) + [one], 1)
    other = np.concatenate([-sine, sine] * (QUERIES_PER_KV + 1) + [0.0 * one], 1)
    return (jnp.asarray(own, jnp.float32), jnp.asarray(other, jnp.float32))


def partner(values):
    width = values.shape[1]
    lane = lax.broadcasted_iota(jnp.int32, values.shape, 1)
    half_size = HEAD_SIZE // 2
    return jnp.where(
        lax.rem(lane, HEAD_SIZE) < half_size,
        pltpu.roll(values, width - half_size, 1),
        pltpu.roll(values, half_size, 1),
    )


def stack_queries(block):
    values = block.astype(jnp.float32) * SCALE
    low = lax.broadcasted_iota(jnp.int32, values.shape, 1) < HEAD_SIZE
    first = jnp.where(low, values, 0.0)
    second = jnp.where(low, pltpu.roll(values, HEAD_SIZE, 1), 0.0)
    return jnp.concatenate([first, second], 0).astype(jnp.bfloat16)


def stack_grads(block):
    values = block.astype(jnp.float32)
    low = lax.broadcasted_iota(jnp.int32, values.shape, 1) < HEAD_SIZE
    first = jnp.where(low, 0.0, pltpu.roll(values, HEAD_SIZE, 1))
    second = jnp.where(low, 0.0, values)
    return jnp.concatenate([first, second], 0).astype(jnp.bfloat16)


def attention_forward_kernel(pieces, place_ref, *refs):
    xs, refs = refs[:pieces], refs[pieces:]
    gain_ref, w_ref, own_ref, other_ref = refs[:4]
    packed_ref, context_ref, lse_ref, normed_ref = refs[4:]
    span = xs[0].shape[1]
    length = pieces * span

    @pl.when(pl.program_id(1) == 0)
    def _():
        for step in range(pieces):
            at = place_ref[step]
            for start in range(0, span, BLOCK):
                value = xs[step][0, start : start + BLOCK, :].astype(jnp.float32)
                normed_ref[at, 0, start : start + BLOCK, :] = (
                    value * norm_factor(value) * gain_ref[...]
                ).astype(jnp.bfloat16)

    for start in range(0, length, BLOCK):
        rows = slice(start, start + BLOCK)
        before = dot_nn(
            normed_ref[start // span, 0, start % span : start % span + BLOCK, :], w_ref[...]
        )
        packed_ref[0, rows, :] = (
            before * own_ref[rows, :] + partner(before) * other_ref[rows, :]
        ).astype(jnp.bfloat16)

    low = lax.broadcasted_iota(jnp.int32, (BLOCK, PAIR), 1) < HEAD_SIZE
    lane_zero = lax.broadcasted_iota(jnp.int32, (BLOCK, PAIR), 1) == 0
    query_row = lax.rem(lax.broadcasted_iota(jnp.int32, (2 * BLOCK, BLOCK), 0), BLOCK)
    allowed = lax.broadcasted_iota(jnp.int32, (2 * BLOCK, BLOCK), 1) <= query_row
    for start in range(0, length, BLOCK):
        rows = slice(start, start + BLOCK)
        queries = stack_queries(packed_ref[0, rows, :PAIR])
        inside = packed_ref[0, rows, PAIR:]
        scores_inside = jnp.where(allowed, dot_nt(queries, inside), NEGATIVE)
        highest = jnp.max(scores_inside, 1, keepdims=True)
        if start:
            before_keys = packed_ref[0, :start, PAIR:]
            scores_before = dot_nt(queries, before_keys)
            highest = jnp.maximum(highest, jnp.max(scores_before, 1, keepdims=True))
        weights = jnp.exp(scores_inside - highest)
        total = jnp.sum(weights, 1, keepdims=True)
        result = dot_nn(weights.astype(jnp.bfloat16), inside)
        if start:
            weights = jnp.exp(scores_before - highest)
            total = total + jnp.sum(weights, 1, keepdims=True)
            result = result + dot_nn(weights.astype(jnp.bfloat16), before_keys)
        result = result / total
        context_ref[start // span, 0, start % span : start % span + BLOCK, :] = jnp.where(
            low, pltpu.roll(result[:BLOCK], HEAD_SIZE, 1), result[BLOCK:]
        ).astype(jnp.bfloat16)
        log_total = highest + jnp.log(total)
        columns = jnp.where(lane_zero, log_total[:BLOCK], log_total[BLOCK:])
        lse_ref[0, 0, :, rows] = columns.T[:8, :]


def attention_forward(xs, places, gain, weights, tables, groups_local):
    pieces = len(xs)
    slots, span, width = xs[0].shape
    length = pieces * span
    bf16, f32 = jnp.bfloat16, jnp.float32
    return pl.pallas_call(
        functools.partial(attention_forward_kernel, pieces),
        grid_spec=pltpu.PrefetchScalarGridSpec(
            num_scalar_prefetch=1,
            grid=(slots, groups_local),
            in_specs=[pl.BlockSpec((1, span, width), lambda s, g, place: (s, 0, 0))] * pieces
            + [
                pl.BlockSpec((1, width), lambda s, g, place: (0, 0)),
                pl.BlockSpec((width, GROUP), lambda s, g, place: (0, g)),
                pl.BlockSpec((length, GROUP), lambda s, g, place: (0, 0)),
                pl.BlockSpec((length, GROUP), lambda s, g, place: (0, 0)),
            ],
            out_specs=[
                pl.BlockSpec((1, length, GROUP), lambda s, g, place: (s, 0, g)),
                pl.BlockSpec((pieces, 1, span, PAIR), lambda s, g, place: (0, s, 0, g)),
                pl.BlockSpec((1, 1, 8, length), lambda s, g, place: (s, g, 0, 0)),
                pl.BlockSpec((pieces, 1, span, width), lambda s, g, place: (0, s, 0, 0)),
            ],
        ),
        out_shape=[
            jax.ShapeDtypeStruct((slots, length, groups_local * GROUP), bf16),
            jax.ShapeDtypeStruct((pieces, slots, span, groups_local * PAIR), bf16),
            jax.ShapeDtypeStruct((slots, groups_local, 8, length), f32),
            jax.ShapeDtypeStruct((pieces, slots, span, width), bf16),
        ],
        compiler_params=pltpu.CompilerParams(vmem_limit_bytes=VMEM_BYTES),
        cost_estimate=SHORT,
        name="attention_forward",
    )(places, *xs, gain, weights, *tables)


def attention_backward_kernel(
    packed_ref,
    lse_ref,
    grad_ref,
    normed_ref,
    own_ref,
    other_ref,
    filled_ref,
    out_ref,
    cut_ref,
    total_ref,
    product_ref,
):
    length, span = packed_ref.shape[1], grad_ref.shape[2]
    low = lax.broadcasted_iota(jnp.int32, (BLOCK, PAIR), 1) < HEAD_SIZE
    query_lane = lax.rem(lax.broadcasted_iota(jnp.int32, (BLOCK, 2 * BLOCK), 1), BLOCK)
    allowed = lax.broadcasted_iota(jnp.int32, (BLOCK, 2 * BLOCK), 0) <= query_lane
    total_ref[...] = jnp.zeros_like(total_ref)

    def unturn(values, lanes, rows):
        values = values.astype(jnp.bfloat16).astype(jnp.float32)
        return (
            values * own_ref[rows, lanes] - partner(values) * other_ref[rows, lanes]
        ).astype(jnp.bfloat16)

    for start in range(0, length, BLOCK):
        rows = slice(start, start + BLOCK)
        queries = stack_queries(packed_ref[0, rows, :PAIR])
        inner = slice(start % span, start % span + BLOCK)
        grads = stack_grads(grad_ref[start // span, 0, inner, :])
        log_total = jnp.concatenate([lse_ref[0, 0, 0:1, rows], lse_ref[0, 0, 1:2, rows]], 1)

        def piece(keys):
            scores = dot_nt(keys, queries)
            probs = jnp.exp(scores - log_total)
            return (probs, dot_nt(keys, grads))

        inside = packed_ref[0, rows, PAIR:]
        probs_inside, grad_inside = piece(inside)
        probs_inside = jnp.where(allowed, probs_inside, 0.0)
        delta = jnp.sum(probs_inside * grad_inside, 0, keepdims=True)
        if start:
            before = packed_ref[0, :start, PAIR:]
            probs_before, grad_before = piece(before)
            delta = delta + jnp.sum(probs_before * grad_before, 0, keepdims=True)
        score_grads = (probs_inside * (grad_inside - delta)).astype(jnp.bfloat16)
        total_ref[rows, :] += dot_nn(probs_inside.astype(jnp.bfloat16), grads) + dot_nn(
            score_grads, queries
        )
        grad_query = dot_tn(score_grads, inside)
        if start:
            score_grads = (probs_before * (grad_before - delta)).astype(jnp.bfloat16)
            total_ref[:start, :] += dot_nn(probs_before.astype(jnp.bfloat16), grads) + dot_nn(
                score_grads, queries
            )
            grad_query = grad_query + dot_tn(score_grads, before)
        grad_query = (
            jnp.where(low, grad_query[:BLOCK], pltpu.roll(grad_query[BLOCK:], HEAD_SIZE, 1)) * SCALE
        )
        out_ref[start // span, 0, inner, :PAIR] = unturn(grad_query, slice(0, PAIR), rows)
    for start in range(0, length, BLOCK):
        rows = slice(start, start + BLOCK)
        inner = slice(start % span, start % span + BLOCK)
        out_ref[start // span, 0, inner, PAIR:] = unturn(
            total_ref[rows, :], slice(PAIR, GROUP), rows
        )

    @pl.when(pl.program_id(1) == 0)
    def _():
        product_ref[...] = jnp.zeros_like(product_ref)

    for at in range(length // span):
        product_ref[...] += dot_tn(normed_ref[at, 0], out_ref[at, 0])

    @pl.when(pl.program_id(1) == pl.num_programs(1) - 1)
    def _():
        parts, heads, each = cut_ref.shape[:3]
        for h in range(heads):
            block = product_ref[h * parts * each : (h + 1) * parts * each, :]
            cut_ref[:, h] = block.reshape(parts, each, GROUP).astype(cut_ref.dtype)


def attention_backward(packed, lse, grads, normed, tables, groups_local, cut):
    slots, length = packed.shape[:2]
    pieces, span, width = grads.shape[0], grads.shape[2], normed.shape[3]
    parts, _, each, _ = cut.shape
    return pl.pallas_call(
        attention_backward_kernel,
        grid=(groups_local, slots),
        in_specs=[
            pl.BlockSpec((1, length, GROUP), lambda g, s: (s, 0, g)),
            pl.BlockSpec((1, 1, 8, length), lambda g, s: (s, g, 0, 0)),
            pl.BlockSpec((pieces, 1, span, PAIR), lambda g, s: (0, s, 0, g)),
            pl.BlockSpec((pieces, 1, span, width), lambda g, s: (0, s, 0, 0)),
            pl.BlockSpec((length, GROUP), lambda g, s: (0, 0)),
            pl.BlockSpec((length, GROUP), lambda g, s: (0, 0)),
            pl.BlockSpec(memory_space=pl.ANY),
        ],
        out_specs=[
            pl.BlockSpec((pieces, 1, span, GROUP), lambda g, s: (0, s, 0, g)),
            pl.BlockSpec((parts, pieces, each, GROUP), lambda g, s: (0, 0, 0, g)),
        ],
        out_shape=[
            jax.ShapeDtypeStruct((pieces, slots, span, packed.shape[2]), jnp.bfloat16),
            jax.ShapeDtypeStruct(cut.shape, cut.dtype),
        ],
        input_output_aliases={6: 1},
        scratch_shapes=[
            pltpu.VMEM((length, PAIR), jnp.float32),
            pltpu.VMEM((width, GROUP), jnp.float32),
        ],
        compiler_params=pltpu.CompilerParams(vmem_limit_bytes=VMEM_BYTES),
        cost_estimate=SHORT,
        name="attention_backward",
    )(packed, lse, grads, normed, *tables, cut)


def expert_kernel(sources, n_local, kept, ids_ref, *refs):
    xs, refs = refs[:sources], refs[sources:]
    gs, refs = refs[:sources], refs[sources:]
    w_in_ref, w_out_ref = refs[:2]
    refs = refs[2 + kept :]
    buffer_ref, grad_out_ref, hidden_ref, grad_pre_ref = refs[:4]
    backs, mixes = refs[4 : 4 + sources], refs[4 + sources : 4 + 2 * sources]
    table, picks, mix_rows, back_rows, gate_back = refs[4 + 2 * sources :]
    step = pl.program_id(0)
    expert = ids_ref[step]
    tokens = xs[0].shape[0]
    here = pl.ds(pl.multiple_of(step * CAP, 16), CAP)

    @pl.when(step == 0)
    def _():
        for s in range(sources):
            table[s] = xs[s][:, D:].astype(jnp.float32).T
            gate_back[s] = jnp.zeros((TAIL, tokens), jnp.float32)

    place = lax.broadcasted_iota(jnp.int32, (CAP, tokens), 0).astype(jnp.float32)
    hits, gate_rows, grad_rows = [], [], []
    for s in range(sources):
        code = table[s, pl.ds(expert, 1), :]
        gate = table[s, pl.ds(expert + E, 1), :] + table[s, pl.ds(expert + 2 * E, 1), :]
        hit = code == place
        pick = jnp.where(hit, 1.0, 0.0).astype(jnp.bfloat16)
        picks[s, here, :] = pick
        hits.append(hit)
        gate_rows.append(jnp.sum(jnp.where(hit, gate, 0.0), 1, keepdims=True))
        buffer_ref[0, 0, s * CAP : (s + 1) * CAP, :] = dot_nn(pick, xs[s][:, :D]).astype(
            jnp.bfloat16
        )
        grad_rows.append(dot_nn(pick, gs[s][...]))
    gate_row = jnp.concatenate(gate_rows, 0)
    grad_row = jnp.concatenate(grad_rows, 0)
    grad_out_ref[0, 0] = (gate_row * grad_row).astype(jnp.bfloat16)
    pre = dot_nn(buffer_ref[0, 0], w_in_ref[0])
    grad_plain = dot_nn(grad_row.astype(jnp.bfloat16), w_out_ref[0])
    gate_pre, up_pre = pre[:, :FFE], pre[:, FFE:]
    sigmoid_gate = 1.0 / (1.0 + jnp.exp(-gate_pre))
    silu_gate = gate_pre * sigmoid_gate
    hidden = (silu_gate * up_pre).astype(jnp.bfloat16)
    hidden_ref[0, 0] = hidden
    gate_grad = jnp.sum(grad_plain * hidden.astype(jnp.float32), 1, keepdims=True)
    grad_hidden = gate_row * grad_plain
    grad_pre_ref[0, 0, :, :FFE] = (
        grad_hidden * up_pre * sigmoid_gate * (1.0 + gate_pre * (1.0 - sigmoid_gate))
    ).astype(jnp.bfloat16)
    grad_pre_ref[0, 0, :, FFE:] = (grad_hidden * silu_gate).astype(jnp.bfloat16)
    outputs = (gate_row * dot_nt(hidden, w_out_ref[0])).astype(jnp.bfloat16)
    back = dot_nt(grad_pre_ref[0, 0], w_in_ref[0]).astype(jnp.bfloat16)
    for s in range(sources):
        part = slice(s * CAP, (s + 1) * CAP)
        mix_rows[s, here, :] = outputs[part]
        back_rows[s, here, :] = back[part]
        row = jnp.sum(jnp.where(hits[s], gate_grad[part], 0.0), 0, keepdims=True)
        high = row.astype(jnp.bfloat16).astype(jnp.float32)
        gate_back[s, pl.ds(expert, 1), :] = high
        gate_back[s, pl.ds(expert + E, 1), :] = row - high

    @pl.when(step == n_local - 1)
    def _():
        for s in range(sources):
            backs[s][:, :D] = dot_tn(picks[s], back_rows[s]).astype(jnp.bfloat16)
            backs[s][:, D:] = gate_back[s].T.astype(jnp.bfloat16)
            mixes[s][...] = dot_tn(picks[s], mix_rows[s]).astype(jnp.bfloat16)


def experts(chunk, chunks, ids, xs, gs, own_in, own_out, kept):
    sources, n_local, tokens = len(xs), own_in.shape[0], xs[0].shape[0]
    rows = sources * CAP
    bf16, f32 = jnp.bfloat16, jnp.float32
    fixed = lambda i, ids: (0, 0)
    saved = lambda columns: pl.BlockSpec((1, 1, rows, columns), lambda i, ids: (i, chunk, 0, 0))
    widths = (D, D, FFE, 2 * FFE)
    in_specs = (
        [pl.BlockSpec((tokens, D + TAIL), fixed)] * sources
        + [pl.BlockSpec((tokens, D), fixed)] * sources
        + [
            pl.BlockSpec((1, D, 2 * FFE), lambda i, ids: (i, 0, 0)),
            pl.BlockSpec((1, D, FFE), lambda i, ids: (i, 0, 0)),
        ]
        + [pl.BlockSpec(memory_space=pl.ANY)] * len(kept)
    )
    results = pl.pallas_call(
        functools.partial(expert_kernel, sources, n_local, len(kept)),
        grid_spec=pltpu.PrefetchScalarGridSpec(
            num_scalar_prefetch=1,
            grid=(n_local,),
            in_specs=in_specs,
            out_specs=[saved(columns) for columns in widths]
            + [pl.BlockSpec((tokens, D + TAIL), fixed)] * sources
            + [pl.BlockSpec((tokens, D), fixed)] * sources,
            scratch_shapes=[
                pltpu.VMEM((sources, TAIL, tokens), f32),
                pltpu.VMEM((sources, n_local * CAP, tokens), bf16),
                pltpu.VMEM((sources, n_local * CAP, D), bf16),
                pltpu.VMEM((sources, n_local * CAP, D), bf16),
                pltpu.VMEM((sources, TAIL, tokens), f32),
            ],
        ),
        out_shape=[
            jax.ShapeDtypeStruct((n_local, chunks, rows, columns), bf16) for columns in widths
        ]
        + [jax.ShapeDtypeStruct((tokens, D + TAIL), bf16)] * sources
        + [jax.ShapeDtypeStruct((tokens, D), bf16)] * sources,
        input_output_aliases={3 + 2 * sources + i: i for i in range(len(kept))},
        compiler_params=pltpu.CompilerParams(vmem_limit_bytes=VMEM_BYTES),
        cost_estimate=pl.CostEstimate(
            flops=n_local * rows * D * (4 * tokens + 9 * FFE),
            bytes_accessed=n_local * D * FFE * 6 + tokens * sources * D * 8,
            transcendentals=0,
        ),
        name="experts",
    )(ids, *xs, *gs, own_in, own_out, *kept)
    return results[:4], results[4 : 4 + sources], results[4 + sources :]


def cut_rows_kernel(offset, left_ref, right_ref, normed_ref, logits_ref, gain_ref, out_ref):
    parts, rows = out_ref.shape[0], out_ref.shape[2]
    width = right_ref.shape[1]
    product = dot_tn(left_ref[...], right_ref[...])
    out_ref[:, 0, :, :offset] = jnp.zeros((parts, rows, offset), out_ref.dtype)
    out_ref[:, 0, :, offset : offset + width] = product.reshape(parts, rows, width).astype(
        out_ref.dtype
    )
    rest = logits_ref[...]
    tail = jnp.zeros((left_ref.shape[1], TAIL), jnp.float32)
    for _ in range(3):
        term = rest.astype(jnp.bfloat16)
        rest = rest - term.astype(jnp.float32)
        tail = tail + dot_tn(normed_ref[...], term)
    lane = lax.broadcasted_iota(jnp.int32, tail.shape, 1)
    tail = jnp.where(lane == E, gain_ref[...], tail)
    out_ref[:, 0, :, offset + width :] = tail.reshape(parts, rows, TAIL).astype(out_ref.dtype)


def cut_rows(left, right, normed, logits, gain_term, parts, offset):
    n_heads, depth, each = left.shape
    width = right.shape[1]
    columns = offset + width + TAIL
    return pl.pallas_call(
        functools.partial(cut_rows_kernel, offset),
        grid=(n_heads,),
        in_specs=[
            pl.BlockSpec((pl.squeezed, depth, each), lambda h: (h, 0, 0)),
            pl.BlockSpec((depth, width), lambda h: (0, 0)),
            pl.BlockSpec((depth, each), lambda h: (0, h)),
            pl.BlockSpec((depth, TAIL), lambda h: (0, 0)),
            pl.BlockSpec((each, 1), lambda h: (h, 0)),
        ],
        out_specs=pl.BlockSpec((parts, 1, each // parts, columns), lambda h: (0, h, 0, 0)),
        out_shape=jax.ShapeDtypeStruct(
            (parts, n_heads, each // parts, columns),
            jnp.bfloat16 if each // parts % 16 == 0 else jnp.float32,
        ),
        compiler_params=pltpu.CompilerParams(vmem_limit_bytes=VMEM_BYTES),
        cost_estimate=pl.CostEstimate(
            flops=4 * depth * each * n_heads * columns,
            bytes_accessed=depth * (each * n_heads + width) * 2 + each * n_heads * columns * 4,
            transcendentals=0,
        ),
        name="cut_rows",
    )(left, right, normed, logits, gain_term)


def expert_grads_kernel(
    order_ref, left_ref, right_ref, own_ref, first_send, second_send, first_keep, second_keep
):
    product = dot_tn(left_ref[0], right_ref[0])
    step = pl.program_id(0)
    half = product.shape[0] // 2
    low = jnp.bfloat16

    @pl.when(step == 0)
    def _():
        own_ref[...] = product

    @pl.when(step == 1)
    def _():
        first_send[0] = product[:half].astype(low)
        second_keep[...] = product[half:]

    @pl.when(step == 2)
    def _():
        first_keep[...] = product[:half]
        second_send[0] = product[half:].astype(low)

    @pl.when(step == 3)
    def _():
        first_send[1] = product[:half].astype(low)
        second_send[1] = product[half:].astype(low)


def expert_grads(order, left, right):
    count, depth, height = left.shape
    width = right.shape[2]
    half = height // 2
    bf16, f32 = jnp.bfloat16, jnp.float32
    whole, pair, one = (height, width), (2, half, width), (half, width)
    return pl.pallas_call(
        expert_grads_kernel,
        grid_spec=pltpu.PrefetchScalarGridSpec(
            num_scalar_prefetch=1,
            grid=(count,),
            in_specs=[
                pl.BlockSpec((1, depth, height), lambda i, order: (order[i], 0, 0)),
                pl.BlockSpec((1, depth, width), lambda i, order: (order[i], 0, 0)),
            ],
            out_specs=[
                pl.BlockSpec(whole, lambda i, order: (0, 0)),
                pl.BlockSpec(pair, lambda i, order: (0, 0, 0)),
                pl.BlockSpec(pair, lambda i, order: (0, 0, 0)),
                pl.BlockSpec(one, lambda i, order: (0, 0)),
                pl.BlockSpec(one, lambda i, order: (0, 0)),
            ],
        ),
        out_shape=[
            jax.ShapeDtypeStruct(whole, f32),
            jax.ShapeDtypeStruct(pair, bf16),
            jax.ShapeDtypeStruct(pair, bf16),
            jax.ShapeDtypeStruct(one, f32),
            jax.ShapeDtypeStruct(one, f32),
        ],
        compiler_params=pltpu.CompilerParams(vmem_limit_bytes=VMEM_BYTES),
        cost_estimate=SHORT,
        name="expert_grads",
    )(order, left, right)


def plain_grads_kernel(left_ref, right_ref, out_ref):
    out_ref[0] = dot_tn(left_ref[0], right_ref[0]).astype(out_ref.dtype)


def plain_grads(left, right):
    count, depth, height = left.shape
    width = right.shape[2]
    return pl.pallas_call(
        plain_grads_kernel,
        grid=(count,),
        in_specs=[
            pl.BlockSpec((1, depth, height), lambda i: (i, 0, 0)),
            pl.BlockSpec((1, depth, width), lambda i: (i, 0, 0)),
        ],
        out_specs=pl.BlockSpec((1, height, width), lambda i: (i, 0, 0)),
        out_shape=jax.ShapeDtypeStruct((count, height, width), jnp.bfloat16),
        compiler_params=pltpu.CompilerParams(vmem_limit_bytes=VMEM_BYTES),
        cost_estimate=pl.CostEstimate(
            flops=4 * count * depth * height * width,
            bytes_accessed=2 * count * (depth * (height + width) + height * width),
            transcendentals=0,
        ),
        name="plain_grads",
    )(left, right)


def make_local(n_heads, chip, core):
    everyone = ("heads", "chip", "core")
    group_size = n_heads * core
    n_local = E // group_size
    groups_local = KEY_VALUE_HEADS // n_heads
    ring = [(i, (i + 1) % n_heads) for i in range(n_heads)]
    crossed = [(i, core - 1 - i) for i in range(core)]

    def onward(value):
        return lax.ppermute(value, "heads", ring)

    def across(value):
        return lax.ppermute(value, "core", crossed)

    def around(value):
        values = [value]
        for _ in range(n_heads - 1):
            values.append(onward(values[-1]))
        return values

    def both(value):
        return [value] if core == 1 else [value, across(value)]

    def joined(parts):
        total = parts[0].astype(jnp.float32)
        if core > 1:
            total = total + across(parts[1]).astype(jnp.float32)
        return total

    def first_phase(parts):
        return (paired(parts[1], 1), paired(parts[2], 2))

    def second_phase(parts, got):
        own, _, _, first_keep, second_keep = parts
        first_next = (first_keep + got[0][1].astype(jnp.float32)).astype(jnp.bfloat16)
        second_next = (second_keep + got[1][1].astype(jnp.float32)).astype(jnp.bfloat16)
        return (paired(first_next, 2), paired(second_next, 1))

    def finished(parts, got, last):
        own = parts[0]
        half = own.shape[0] // 2
        first = own[:half] + got[0][0].astype(jnp.float32) + last[0].astype(jnp.float32)
        second = own[half:] + got[1][0].astype(jnp.float32) + last[1].astype(jnp.float32)
        return jnp.concatenate([first, second], 0)

    def after(value, *others):
        return lax.optimization_barrier((value, others))[0]

    def paired(value, other):
        return lax.ppermute(value, "chip", [(i, i ^ other) for i in range(chip)])

    def spread_rows(cut):
        part = lax.psum_scatter(
            cut.reshape(-1, cut.shape[3]), ("chip", "core"), scatter_dimension=0, tiled=True
        )
        return part.reshape(cut.shape[1:])

    def local(
        tokens,
        cotangent,
        lengths,
        routes,
        attention_input_weight,
        attn_out,
        router,
        gain_attn,
        gain_ffn,
        expert_in,
        expert_out,
    ):
        slots, span, width = tokens.shape
        token_rows = slots * span
        length = span * n_heads
        rank = lax.axis_index("heads")
        qkv_width = attention_input_weight.shape[1]
        own_columns = groups_local * GROUP
        rings = around(tokens)
        small = jnp.concatenate(
            [
                attention_input_weight,
                attn_out,
                router,
                gain_attn[:, None],
                gain_ffn[:, None],
                jnp.zeros((router.shape[0], TAIL - E - 2), jnp.bfloat16),
            ],
            1,
        )
        column = lax.all_to_all(
            jnp.broadcast_to(after(small, rings[1])[None], (n_heads,) + small.shape),
            "heads",
            split_axis=0,
            concat_axis=0,
            tiled=True,
        )

        own_out = lax.all_gather(expert_out, "chip", axis=0, tiled=True).reshape(n_local, D, FFE)

        def plane(value):
            value = lax.all_gather(value, ("chip", "core"), axis=1, tiled=True)
            return value.reshape(-1, value.shape[2])

        first = plane(
            after(
                jnp.concatenate(
                    [
                        lax.dynamic_slice_in_dim(column, rank * own_columns, own_columns, 2),
                        column[:, :, qkv_width + D :],
                    ],
                    2,
                ),
                own_out,
                rings[2],
            )
        )
        w_own = first
        gain_one = first[:, own_columns + E].astype(jnp.float32)
        w_proj = plane(column[:, :, qkv_width:])
        w_router = w_proj[:, D : D + E]
        gain_two = w_proj[:, D + E + 1].astype(jnp.float32)
        w_proj = w_proj[:, :D]
        own_grads = cotangent.reshape(token_rows, width)
        own_in = lax.all_gather(after(expert_in, first, rings[-1]), "chip", axis=0, tiled=True).reshape(
            n_local, D, 2 * FFE
        )

        positions = rank * span + jnp.arange(span, dtype=jnp.int32)
        valid = (positions[None, :] < lengths[:, None]).reshape(token_rows)
        valid_float = valid.astype(jnp.float32)[:, None]
        route_rows = routes.reshape(token_rows, TOPK)
        routed = jnp.any(
            route_rows[:, :, None] == jnp.arange(E, dtype=jnp.int32)[None, None, :], 1
        )
        live = (routed & valid[:, None]).astype(jnp.bfloat16)
        earlier = (
            jnp.arange(token_rows)[:, None] > jnp.arange(token_rows)[None, :]
        ).astype(jnp.bfloat16)
        count = jnp.dot(earlier, live, preferred_element_type=jnp.float32)
        kept = (live > 0) & (count < CAP)
        code = jnp.where(kept, count, -1.0).astype(jnp.bfloat16)
        ids = (rank * n_local + jnp.arange(n_local, dtype=jnp.int32)) * core + lax.axis_index("core")

        tables = rotary_tables(length)
        places = (rank + n_heads - jnp.arange(n_heads, dtype=jnp.int32)) % n_heads
        packed, context_heads, lse, normed_whole = attention_forward(
            rings, places, gain_one[None, :], w_own, tables, groups_local
        )
        grad_ring = [own_grads, onward(after(own_grads, rings[-1]))]
        context_heads = after(context_heads, grad_ring[1])
        context = lax.all_to_all(context_heads, "heads", split_axis=0, concat_axis=0, tiled=True)
        grad_ring.append(onward(after(grad_ring[1], context)))
        heads_width = groups_local * PAIR
        context = context.reshape(n_heads, token_rows, heads_width)

        state = tokens.astype(jnp.float32).reshape(token_rows, width)
        mid_state = state
        for h in range(n_heads):
            mid_state = mid_state + dot_nn(
                context[h], w_proj[h * heads_width : (h + 1) * heads_width]
            )
        factor_two = norm_factor(mid_state)
        normed_ffn = (mid_state * factor_two * gain_two).astype(jnp.bfloat16)
        logits = jnp.dot(normed_ffn, w_router, preferred_element_type=jnp.float32)
        highest = jnp.max(jnp.where(routed, logits, NEGATIVE), -1, keepdims=True)
        weights = jnp.where(routed, jnp.exp(jnp.where(routed, logits - highest, 0.0)), 0.0)
        gates = weights / jnp.sum(weights, -1, keepdims=True)
        gates_high = lax.reduce_precision(gates, 8, 7)
        payload = jnp.concatenate(
            [
                normed_ffn,
                code,
                gates_high.astype(jnp.bfloat16),
                (gates - gates_high).astype(jnp.bfloat16),
                jnp.zeros((token_rows, TAIL - 3 * E), jnp.bfloat16),
            ],
            1,
        )
        while len(grad_ring) < n_heads:
            grad_ring.append(onward(grad_ring[-1]))
        payloads = around(after(payload, grad_ring[-1]))
        sequence = list(range(1, n_heads - 1)) + [0, n_heads - 1]
        saved, moving = (), None
        backs, mixes = {}, {}
        for step in sequence:
            xs, gs = both(payloads[step]), both(grad_ring[step])
            if moving is not None and step:
                xs[0] = after(xs[0], moving)
            saved, back, mix = experts(
                step, n_heads, ids, xs, gs, own_in, own_out, tuple(saved)
            )
            backs[step], mixes[step] = back, mix
            if step:
                total = joined(back)
                if moving is not None:
                    total = total + onward(moving).astype(jnp.float32)
                moving = total.astype(jnp.bfloat16)
        buffer, grad_outputs, hidden, grad_pre = [
            value.reshape(n_local, group_size * CAP, value.shape[3]) for value in saved
        ]
        grad_pre = after(grad_pre, moving)
        last_back = onward(moving)
        hidden, last_back = lax.optimization_barrier((hidden, last_back))
        if expert_in.shape[0] == D:
            order = lax.axis_index("chip") ^ jnp.arange(chip, dtype=jnp.int32)
            parts_in = expert_grads(order, buffer, grad_pre)
        else:
            parts_in = [plain_grads(buffer, grad_pre)]
        w_qkv = plane(after(column[:, :, :qkv_width], context))
        mix_moving = joined(mixes[1]).astype(jnp.bfloat16)
        mix_received = onward(after(mix_moving, last_back))
        back_sum = joined(backs[0]) + after(last_back, w_qkv, *parts_in).astype(jnp.float32)

        grad_gates = back_sum[:, width : width + E] + back_sum[:, width + E : width + 2 * E]
        grad_logits = gates * (grad_gates - jnp.sum(gates * grad_gates, -1, keepdims=True))
        grad_logits = grad_logits * valid_float
        grad_out = cotangent.astype(jnp.float32).reshape(token_rows, width) * valid_float
        grad_normed_ffn = back_sum[:, :width] + jnp.dot(
            grad_logits, w_router.astype(jnp.float32).T, precision=TOP_PRECISION
        )
        grad_mid_norm, gain_two_term = norm_back(grad_normed_ffn, mid_state, factor_two, gain_two)
        grad_mid = grad_out + grad_mid_norm
        grad_mid_low = grad_mid.astype(jnp.bfloat16)
        context_gradient = jnp.stack(
            [
                dot_nt(grad_mid_low, w_proj[h * heads_width : (h + 1) * heads_width])
                for h in range(n_heads)
            ]
        ).astype(jnp.bfloat16)
        context_gradient = after(context_gradient, mix_received)
        near, near_out = (), ()
        if len(parts_in) > 1:
            near = first_phase(parts_in)
            parts_out = expert_grads(order, grad_outputs, hidden)
        else:
            parts_out = [plain_grads(grad_outputs, hidden)]
        context_gradient, parts_out = lax.optimization_barrier((context_gradient, parts_out))
        if near:
            near_out = first_phase(parts_out)
        grad_context_heads = lax.all_to_all(
            context_gradient.reshape(n_heads, slots, span, heads_width),
            "heads",
            split_axis=0,
            concat_axis=0,
            tiled=True,
        )
        logits_padded = jnp.concatenate(
            [grad_logits, jnp.zeros((token_rows, TAIL - E), jnp.float32)], 1
        )
        second = cut_rows(
            context,
            after(grad_mid_low, context_gradient),
            normed_ffn,
            logits_padded,
            gain_two_term[:, None],
            chip * core,
            own_columns,
        )

        mix_received, near, second = lax.optimization_barrier((mix_received, near, second))
        for chunk in range(2, n_heads):
            mix_moving = (joined(mixes[chunk]) + mix_received.astype(jnp.float32)).astype(
                jnp.bfloat16
            )
            if chunk == 2:
                grad_before, cut = attention_backward(
                    packed,
                    lse,
                    after(grad_context_heads, mix_moving),
                    normed_whole,
                    tables,
                    groups_local,
                    second,
                )
            if chunk < n_heads - 1:
                mix_received = onward(after(mix_moving, grad_context_heads))
        grad_before, near_out = lax.optimization_barrier((grad_before, near_out))
        grad_mine = lax.all_to_all(
            after(grad_before, mix_received), "heads", split_axis=0, concat_axis=0, tiled=True
        ).reshape(n_heads, token_rows, own_columns)
        part = spread_rows(cut)
        if near:
            far_in, far_out = second_phase(parts_in, near), second_phase(parts_out, near_out)
        mix_moving, grad_mine = lax.optimization_barrier((mix_moving, grad_mine))
        mix_last = onward(mix_moving)
        grad_normed_attn = dot_nt(grad_mine[0], w_qkv[:, :own_columns])
        for h in range(1, n_heads):
            grad_normed_attn = grad_normed_attn + dot_nt(
                grad_mine[h], w_qkv[:, h * own_columns : (h + 1) * own_columns]
            )
        grad_state_norm, _ = norm_back(grad_normed_attn, state, norm_factor(state), gain_one)
        grad_tokens = (grad_mid + grad_state_norm).astype(jnp.bfloat16).reshape(tokens.shape)
        if near:
            grad_expert_in = finished(parts_in, near, after(far_in, grad_tokens))
            grad_expert_out = finished(parts_out, near_out, after(far_out, grad_tokens))
        else:
            grad_expert_in, grad_expert_out = [
                lax.psum_scatter(
                    value[0].reshape(-1, value[0].shape[2]),
                    "chip",
                    scatter_dimension=0,
                    tiled=True,
                ).astype(jnp.float32)
                for value in (parts_in, parts_out)
            ]
        mixture = joined(mixes[0]) + mix_last.astype(jnp.float32)
        mixed = (valid_float * (mid_state + mixture)).astype(jnp.bfloat16)

        last = lax.all_to_all(
            part, "heads", split_axis=0, concat_axis=0, tiled=True
        ).astype(jnp.float32)
        second = jnp.sum(last[:, :, own_columns:], 0)
        grad_attn_out = second[:, :D]
        grad_router = second[:, D : D + E]
        grad_gain_ffn = second[:, D + E]
        grad_attn_in = jnp.concatenate([last[h, :, :own_columns] for h in range(n_heads)], 1)
        grad_gain_attn = jnp.sum(
            grad_attn_in * attention_input_weight.astype(jnp.float32), -1
        ) / gain_attn.astype(jnp.float32)
        return (
            mixed.reshape(tokens.shape),
            grad_tokens,
            grad_attn_in,
            grad_attn_out,
            grad_router,
            grad_gain_attn,
            grad_gain_ffn,
            grad_expert_in,
            grad_expert_out,
        )

    return local


def solution(mesh):
    n_heads, n_shard = mesh.shape["heads"], mesh.shape["shard"]
    core = 2 if n_heads * n_shard == E else 1
    chip = n_shard // core
    split = jax.sharding.Mesh(
        mesh.devices.reshape(n_heads, chip, core), ("heads", "chip", "core")
    )
    shard = ("chip", "core")
    everyone = ("heads", "chip", "core")
    token_spec = P(shard, "heads", None)
    rows = P(everyone, None)
    in_specs = (
        token_spec,
        token_spec,
        P(shard),
        token_spec,
        rows,
        rows,
        rows,
        P(everyone),
        P(everyone),
        rows,
        rows,
    )
    out_specs = (token_spec, token_spec, rows, rows, rows, P(everyone), P(everyone), rows, rows)
    return jax.shard_map(
        make_local(n_heads, chip, core),
        mesh=split,
        in_specs=in_specs,
        out_specs=out_specs,
        check_vma=False,
    )
```
